512 devices in a mesh: grp: 4 (over x_lo, core), gx: 8 (over y, x_hi), gy: 16 (over z).
Axes of the slice: x: 4 (x_hi: 2, x_lo: 2; x = x_hi * 2 + x_lo), y: 4, z: 16, core: 2. Of those that a mesh axis runs over, the one named last changes fastest.
Arguments:
- pressure: float32 [24, 512, 4096], P(None, ('grp', 'gy'), 'gx'), may hold values from -2 to 0.2
- soil_class: int32 [24, 512, 4096], P(None, ('grp', 'gy'), 'gx'), may hold values from 0 to 11
- capacity_range: float32 [12], replicated, may hold values from 0.25 to 0.45
- inverse_entry: float32 [12], replicated, may hold values from 0.3 to 3
- shape_index: float32 [12], replicated, may hold values from 1.3 to 2.5
- conductivity: float32 [12], replicated, may hold values from 0.05 to 1
- depth: float32 [512, 4096], P('grp', ('gx', 'gy')), may hold values from 0 to 2
- elevation: float32 [512, 4096], P('grp', ('gx', 'gy')), may hold values from -4 to 4
- roughness: float32 [512, 4096], P('grp', ('gx', 'gy')), may hold values from 2 to 8
- rain: float32 [512, 4096], P('grp', ('gx', 'gy')), may hold values from 0.1 to 1
- land_mask: int32 [512, 4096], P('grp', ('gx', 'gy')), may hold values 0 or 1
- channel_mask: int32 [512, 4096], P('grp', ('gx', 'gy')), may hold values 0 or 1
Outputs:
- head: float32 [24, 512, 4096], P(None, ('grp', 'gy'), 'gx')
- water: float32 [512, 4096], P('grp', ('gx', 'gy'))
The draws below stay inside these ranges and needn't reach their ends.
All inputs are finite; a program needn't handle non-finite values. No bound on the sum of `land_mask` or of `channel_mask` on one device may be relied on, other than what follows from the above.
Results may differ from the reference program's by a relative error of at most 0.0003.
Values sent between devices are 32-bit elements; how exact they have to be, the bound alone decides.
A program may use at most 64 MiB of HBM per device.

```python
import math
import jax
import jax.numpy as jnp

NZ = 24
NCLASS = 12
SWEEPS = 2
PASSES = 3
NX = 512
NY = 4096


def touch_ends(entries, key, low, top_value):
    longest = entries.shape.index(max(entries.shape))
    spots = []
    for shift in (0, 1):
        where = [jax.random.randint(jax.random.fold_in(key, axis), (), 0, length) for axis, length in enumerate(entries.shape)]
        where[longest] = (where[longest] + shift) % entries.shape[longest]
        spots.append(tuple(where))
    return entries.at[spots[0]].set(low).at[spots[1]].set(top_value)


def shard_levels(rng, shape, pieces, smallest, largest):
    level, own = 1.0, jax.random.fold_in(rng, 6)
    for dim, shards_of in pieces:
        heights = jnp.exp(jax.random.uniform(jax.random.fold_in(own, dim), (shards_of,), jnp.float32, smallest / len(pieces), largest / len(pieces)))
        level = level * jnp.repeat(heights, shape[dim] // shards_of).reshape([-1 if axis == dim else 1 for axis in range(len(shape))])
    return level


def scatter_about(own_key, extent, scale, reach, cuts=(), kind=jnp.bfloat16):
    level = shard_levels(own_key, extent, cuts, -0.22, 0.18) if cuts else 1.0
    drawn = jax.random.normal(own_key, extent, jnp.float32) * scale * level
    return jnp.minimum(jnp.maximum(drawn, -reach), reach).astype(kind)


def setup_inputs(seed: int = 0) -> dict:
    key_list = jax.random.split(jax.random.key(seed), 13)
    pressure = jnp.clip(-2.0 + 2.2 * jax.random.uniform(key_list[0], (NZ, NX, NY), jnp.float32) ** shard_levels(key_list[0], (NZ, NX, NY), ((1, 64), (2, 8)), -0.2, 0.2), -2.0, 0.2)
    soil_class = touch_ends(jax.random.randint(key_list[1], (NZ, NX, NY), 0, NCLASS), jax.random.fold_in(key_list[1], 1), 0, NCLASS - 1).astype(jnp.int32)
    capacity_range = jnp.clip(jax.random.uniform(key_list[2], (NCLASS,), jnp.float32, 0.25, 0.45), 0.25, 0.45)
    inverse_entry = jnp.clip(jnp.exp(jax.random.uniform(key_list[3], (NCLASS,), jnp.float32, math.log(0.3), math.log(3.0))), 0.3, 3.0)
    shape_index = jnp.clip(jax.random.uniform(key_list[4], (NCLASS,), jnp.float32, 1.3, 2.5), 1.3, 2.5)
    conductivity = jnp.clip(jnp.exp(jax.random.uniform(key_list[5], (NCLASS,), jnp.float32, math.log(0.05), math.log(1.0))), 0.05, 1.0)
    depth = jnp.clip(2.0 * jax.random.uniform(key_list[6], (NX, NY), jnp.float32) ** shard_levels(key_list[6], (NX, NY), ((0, 4), (1, 128)), -0.2, 0.2), 0.0, 2.0)
    elevation = scatter_about(key_list[7], (NX, NY), 1.0, 4.0, ((0, 4), (1, 128)), jnp.float32)
    roughness = jnp.clip(jnp.exp(math.log(8.0) - 1.3862944 * jax.random.uniform(key_list[8], (NX, NY), jnp.float32) ** shard_levels(key_list[8], (NX, NY), ((0, 4), (1, 128)), -0.2, 0.2)), 2.0, 8.0)
    rain = jnp.clip(jnp.exp(math.log(1.0) - 2.3025851 * jax.random.uniform(key_list[9], (NX, NY), jnp.float32) ** shard_levels(key_list[9], (NX, NY), ((0, 4), (1, 128)), -0.2, 0.2)), 0.1, 1.0)
    land_mask = touch_ends((jax.random.randint(key_list[10], (NX, NY), 0, 5) < 4).astype(jnp.int32), jax.random.fold_in(key_list[10], 1), 0, 1)
    channel_mask = touch_ends((jax.random.randint(key_list[11], (NX, NY), 0, 8) < 1).astype(jnp.int32), jax.random.fold_in(key_list[11], 1), 0, 1)
    return {"pressure": pressure, "soil_class": soil_class, "capacity_range": capacity_range, "inverse_entry": inverse_entry, "shape_index": shape_index, "conductivity": conductivity, "depth": depth, "elevation": elevation, "roughness": roughness, "rain": rain, "land_mask": land_mask, "channel_mask": channel_mask}


STORAGE = 0.01
LATERAL = 4.0
VERTICAL = 4.0
GRAVITY_STEP = 0.5
SUCTION_FLOOR = 0.01
SLOPE_FLOOR = 0.1
SURFACE_STEP = 0.3
LEAKANCE = 0.5
SOURCE_GAIN = 1.0

def lookup(soil_class, tables):
    results = []
    for table in tables:
        filled = jnp.zeros(soil_class.shape, table.dtype)
        for kind_number in range(table.shape[0]):
            filled = jnp.where(soil_class == kind_number, table[kind_number], filled)
        results.append(filled)
    return results

def closures(pressure, capacity_range, inverse_entry, pore_index, conductivity):
    exponent = 1.0 / (1.0 - pore_index)
    scaled = jnp.maximum(-inverse_entry * pressure, SUCTION_FLOOR)
    log_scaled = jnp.log(scaled)
    log_sum = jnp.log1p(jnp.exp(exponent * log_scaled))
    saturation = jnp.exp(-pore_index * log_sum)
    content = capacity_range * saturation
    capacity = STORAGE + capacity_range * pore_index * exponent * inverse_entry * jnp.exp((exponent - 1.0) * log_scaled - (pore_index + 1.0) * log_sum)
    conduct = conductivity * jnp.sqrt(saturation) * jnp.square(1.0 - jnp.exp(pore_index * (exponent * log_scaled - log_sum)))
    return (content, capacity, conduct)

def update_cells(padded, conduct_pad, capacity, content_gap, source):
    layers = padded.shape[0] - 2
    rows = padded.shape[1] - 2
    cols = padded.shape[2] - 2
    center = padded[1:-1, 1:-1, 1:-1]
    own_conduct = conduct_pad[1:-1, 1:-1, 1:-1]
    numerator = capacity * center - content_gap
    denominator = capacity
    neighbours = ((1, 0, 1, LATERAL, 0.0), (1, 2, 1, LATERAL, 0.0), (1, 1, 0, LATERAL, 0.0), (1, 1, 2, LATERAL, 0.0), (0, 1, 1, VERTICAL, GRAVITY_STEP), (2, 1, 1, VERTICAL, -GRAVITY_STEP))
    for first, second, third, weight, offset in neighbours:
        beside = padded[first:first + layers, second:second + rows, third:third + cols]
        beside_conduct = conduct_pad[first:first + layers, second:second + rows, third:third + cols]
        face_weight = weight * jnp.sqrt(own_conduct * beside_conduct)
        numerator = numerator + face_weight * (beside + offset)
        denominator = denominator + face_weight
    gained = jnp.concatenate([(SOURCE_GAIN * source)[None], jnp.zeros((layers - 1, rows, cols), source.dtype)], axis=0)
    numerator = numerator + gained
    return numerator / denominator

def face_flux(upper_level, lower_level, upper_depth, lower_depth, upper_convey, lower_convey):
    slope = upper_level - lower_level
    upwind = jnp.where(slope >= 0, upper_depth, lower_depth)
    carried = upwind * jnp.cbrt(upwind * upwind)
    return jnp.sqrt(upper_convey * lower_convey) * carried * slope / jnp.sqrt(jnp.maximum(jnp.abs(slope), SLOPE_FLOOR))

def overland(depth_pad, level_pad, convey_pad, leak, top, rain):
    current = depth_pad[1:-1, 1:-1]
    surface = level_pad + depth_pad
    across = face_flux(surface[:-1, 1:-1], surface[1:, 1:-1], depth_pad[:-1, 1:-1], depth_pad[1:, 1:-1], convey_pad[:-1, 1:-1], convey_pad[1:, 1:-1])
    along = face_flux(surface[1:-1, :-1], surface[1:-1, 1:], depth_pad[1:-1, :-1], depth_pad[1:-1, 1:], convey_pad[1:-1, :-1], convey_pad[1:-1, 1:])
    outflow = across[1:] - across[:-1] + (along[:, 1:] - along[:, :-1])
    rate = leak * (current - top)
    return (jnp.maximum(current + SURFACE_STEP * (rain - rate - outflow), 0.0), rate)

def reference(pressure, soil_class, capacity_range, inverse_entry, shape_index, conductivity, depth, elevation, roughness, rain, land_mask, channel_mask):
    pore_table = 1.0 - 1.0 / shape_index
    range_cells, entry_cells, pore_cells, conduct_cells = lookup(soil_class, (capacity_range, inverse_entry, pore_table, conductivity))
    content0, capacity, conduct = closures(pressure, range_cells, entry_cells, pore_cells, conduct_cells)
    top = pressure[0]
    leak = LEAKANCE * land_mask.astype(jnp.float32) * conduct[0]
    convey = (1.0 + channel_mask.astype(jnp.float32)) / roughness
    level_pad = jnp.pad(elevation, 1)
    convey_pad = jnp.pad(convey, 1)
    water = depth
    exchange = jnp.zeros_like(depth)
    for pass_number in range(PASSES):
        water, rate = overland(jnp.pad(water, 1), level_pad, convey_pad, leak, top, rain)
        exchange = exchange + SURFACE_STEP * rate
    head = pressure
    content = content0
    for sweep_number in range(SWEEPS):
        head = update_cells(jnp.pad(head, 1), jnp.pad(conduct, 1), capacity, content - content0, exchange)
        if sweep_number + 1 < SWEEPS:
            content, capacity, conduct = closures(head, range_cells, entry_cells, pore_cells, conduct_cells)
    return (head, water)
```

```python
import functools

import jax
import jax.numpy as jnp
from jax import lax
from jax.experimental import pallas as pl
from jax.experimental.pallas import tpu as pltpu
from jax.sharding import PartitionSpec as P

MESH = pl.DeviceIdType.MESH
F32 = jnp.float32

STORAGE = 0.01
GRAVITY_STEP = 0.5
SUCTION_FLOOR = 0.01
SLOPE_FLOOR = 0.1
SURFACE_STEP = 0.3
LEAKANCE = 0.5

TILE = 128
ROWS = 8
FIELDS = 5
PARAMS = 6


def lanes():
    return lax.broadcasted_iota(jnp.int32, (ROWS, TILE), 1)


def sublanes():
    return lax.broadcasted_iota(jnp.int32, (ROWS, TILE), 0)


def gather(table, index):
    return jnp.take_along_axis(table, index, axis=1, mode="promise_in_bounds")


def build_tables(tab, kinds):
    lane = lanes()
    rows = []
    for i in range(4):
        row = jnp.zeros((ROWS, TILE), F32)
        for kind in range(kinds):
            row = jnp.where(lane == kind, tab[i, kind], row)
        rows.append(row)
    span, entry, shape, conduct = rows
    shape = jnp.where(lane < kinds, shape, 2.0)
    pore = 1.0 - 1.0 / shape
    expo = 1.0 / (1.0 - pore)
    return (
        -entry,
        expo,
        pore,
        span * pore * expo * entry,
        span,
        2.0 * jnp.sqrt(conduct),
    )


def closures(p, params):
    entry, expo, pore, lead, _, scale = params
    log_scaled = jnp.log(jnp.maximum(entry * p, SUCTION_FLOOR))
    up = expo * log_scaled
    log_sum = jnp.log(1.0 + jnp.exp(up))
    drop = pore * log_sum
    wet = pore * up - drop
    held = jnp.exp(wet)
    capacity = STORAGE + lead * jnp.exp(wet - log_sum)
    fourth = jnp.exp(-0.25 * drop)
    half = fourth * fourth
    root = scale * fourth * (1.0 - held)
    return capacity, half * half, root


def kernel(
    nz, wide, kinds, sizes,
    p_in, k_in, t0_in, t1_in, t2_in, t3_in,
    s0_in, s1_in, s2_in, s3_in, s4_in, s5_in,
    head_out, water_out,
    tab, p, kind, par, cap, sat, root, flow, num,
    row_s, row_r, top_s, top_r, col_s, col_r, tcol_s, tcol_r,
    surf_in, field, below, above,
    down_s, down_r, edge_r, back_s, back_r, source, water,
    sem,
):
    ng, nx, nk = sizes
    tiles = wide // TILE
    per = TILE // 32
    g, x, k = (lax.axis_index(a) for a in ("grp", "gx", "gy"))
    lane, sub = lanes(), sublanes()
    first, last = k == 0, k == nk - 1
    has_n, has_s = g > 0, g < ng - 1
    has_w, has_e = x > 0, x < nx - 1

    names = {}

    def s(name):
        return sem.at[names.setdefault(name, len(names))]

    def at(dg, dx, kk):
        return {"grp": g + dg, "gx": x + dx, "gy": kk}

    def tile(t):
        return slice(t * TILE, (t + 1) * TILE)

    def load(src, dst, name):
        copy = pltpu.make_async_copy(src, dst, s(name))
        copy.start()
        return copy

    table_loads = [
        load(ref, tab.at[i], f"tab{i}")
        for i, ref in enumerate((t0_in, t1_in, t2_in, t3_in))
    ]
    top_loads = [
        load(p_in.at[0:1], p.at[0:1], "p0"),
        load(k_in.at[0:1], kind.at[0:1], "k0"),
    ]
    surf_loads = [
        load(s0_in, surf_in.at[0], "s0"),
        load(s1_in, surf_in.at[1], "s1"),
        load(s2_in, surf_in.at[2], "s2"),
        load(s3_in, surf_in.at[3], "s3"),
    ]
    mask_loads = [
        load(s4_in, water.at[0], "s4"),
        load(s5_in, water.at[1], "s5"),
    ]
    rest_loads = [
        load(p_in.at[1:nz], p.at[1:nz], "p1"),
        load(k_in.at[1:nz], kind.at[1:nz], "k1"),
    ]

    barrier = pltpu.get_barrier_semaphore()

    def greet(device):
        pl.semaphore_signal(barrier, 1, device_id=device, device_id_type=MESH)

    def ring(body):
        def step(i, _):
            body(lax.rem(k + 1 + lax.rem(i + nk // 2 - 1, nk - 1), nk))
            return 0

        lax.fori_loop(0, nk - 1, step, 0)

    def every(body):
        def step(i, _):
            body(i)
            return 0

        lax.fori_loop(0, nk, step, 0)

    col = x * nk + k
    has_l, has_r = col > 0, col < nx * nk - 1
    left = {"gx": jnp.maximum(col - 1, 0) // nk, "gy": lax.rem(jnp.maximum(col - 1, 0), nk)}
    right = {"gx": (col + 1) // nk, "gy": lax.rem(col + 1, nk)}
    row = g * nk + k
    has_u, has_d = row > 0, row < ng * nk - 1
    up = {"grp": jnp.maximum(row - 1, 0) // nk, "gx": x, "gy": lax.rem(jnp.maximum(row - 1, 0), nk)}
    down = {"grp": (row + 1) // nk, "gx": x, "gy": lax.rem(row + 1, nk)}

    ring(lambda kk: greet(at(0, 0, kk)))
    for dg, has in ((-1, has_n), (1, has_s)):
        far = nk - 1 if dg < 0 else 0

        @pl.when(has)
        def _():
            greet(at(dg, 0, far))
            greet(at(dg, 0, k))

            @pl.when(has_l)
            def _():
                greet({"grp": g + dg, **left})

            @pl.when(has_r)
            def _():
                greet({"grp": g + dg, **right})

            @pl.when(first & has_w)
            def _():
                greet(at(dg, -1, far))

            @pl.when(last & has_e)
            def _():
                greet(at(dg, 1, far))

    @pl.when(has_w)
    def _():
        greet(at(0, -1, k))

        @pl.when(first)
        def _():
            every(lambda kk: greet(at(0, -1, kk)))

    @pl.when(has_e)
    def _():
        greet(at(0, 1, k))

        @pl.when(last)
        def _():
            every(lambda kk: greet(at(0, 1, kk)))

    def one(flag):
        return flag.astype(jnp.int32)

    rows_to = one(has_n) + one(has_s)
    cols_to = one(has_w) + one(has_e)
    corner = one(first & has_n) + one(last & has_s)
    expected = (
        (nk - 1)
        + corner * nk
        + rows_to * (1 + one(has_l) + one(has_r))
        + 2 * cols_to
        + corner * cols_to
    )

    zero = jnp.zeros((ROWS, TILE), F32)

    def clear(ref, rows):
        for r in range(0, rows, ROWS):
            for c in range(0, ref.shape[-1], TILE):
                ref[r : r + ROWS, c : c + TILE] = zero

    for t in range(tiles):
        for ph in range(2):
            for z in (0, nz + 1):
                root[ph, z, :, tile(t)] = zero
                flow[ph, z, :, tile(t)] = zero

    for d, has, has_g, ref in ((0, has_u, has_n, above), (1, has_d, has_s, below)):

        @pl.when(jnp.logical_not(has))
        def _():
            for ph in range(2):
                for i in range(2):
                    for t in range(tiles):
                        clear(row_r.at[ph, d, i, t], nz)
            clear(top_r.at[d], ROWS)

        @pl.when(jnp.logical_not(has_g))
        def _():
            for f in range(FIELDS):
                clear(ref.at[f], 48)
            off = 248 if d == 0 else 128
            clear(down_r.at[off : off + ROWS], ROWS)

        @pl.when(has_g & jnp.logical_not(has_r))
        def _():
            for f in range(FIELDS):
                ref[f, 32:40, :] = zero

        @pl.when(has_g & jnp.logical_not(has_l))
        def _():
            for f in range(FIELDS):
                ref[f, 40:48, :] = zero

    for d, has in ((0, has_w), (1, has_e)):

        @pl.when(jnp.logical_not(has))
        def _():
            for ph in range(2):
                col_r[ph, d] = zero
            tcol_r[d] = zero

    for d, has in ((0, has_r), (1, has_l)):

        @pl.when(jnp.logical_not(has))
        def _():
            for f in range(FIELDS):
                field[f, 32 + 8 * d : 40 + 8 * d, 0:TILE] = zero

    gets_edge = (first & has_w) | (last & has_e)

    @pl.when(jnp.logical_not(gets_edge))
    def _():
        clear(edge_r.at[0:TILE], TILE)

    for off, has in ((128, has_s), (248, has_n)):

        @pl.when(jnp.logical_not(gets_edge & has))
        def _():
            clear(edge_r.at[off : off + ROWS], ROWS)

    for c in table_loads:
        c.wait()
    tables = build_tables(tab, kinds)

    def layer_params(z, t):
        index = kind[z, :, tile(t)]
        return [gather(table, index) for table in tables]

    def put_row(dst_first, dst_last, i, z, t, value):
        dst_first[i, t, pl.ds(z, 1), :] = value[0:1, :]
        dst_last[i, t, pl.ds(z, 1), :] = value[7:8, :]

    def shift_to(value, frm, to):
        return pltpu.roll(value, lax.rem(to - frm + TILE, TILE), 1)

    def put_cols(packs, z, q0, r0, q1, r1):
        west, east = packs
        west = jnp.where(lane == z, shift_to(q0, 0, z), west)
        west = jnp.where(lane == z + 64, shift_to(r0, 0, z + 64), west)
        east = jnp.where(lane == z, shift_to(q1, TILE - 1, z), east)
        east = jnp.where(lane == z + 64, shift_to(r1, TILE - 1, z + 64), east)
        return west, east

    def first_closures(z, packs):
        ends = []
        for t in range(tiles):
            params = layer_params(z, t)
            for i in range(PARAMS):
                par[i, z, :, tile(t)] = params[i]
            pz = p[z, :, tile(t)]
            c, se, q = closures(pz, params)
            r = q * pz
            cap[z, :, tile(t)] = c
            sat[z, :, tile(t)] = se
            root[0, z + 1, :, tile(t)] = q
            flow[0, z + 1, :, tile(t)] = r
            put_row(row_s.at[0, 0], row_s.at[0, 1], 0, z, t, q)
            put_row(row_s.at[0, 0], row_s.at[0, 1], 1, z, t, r)
            ends.append((q, r))
        return put_cols(packs, z, *ends[0], *ends[-1])

    for c in top_loads:
        c.wait()
    packs = first_closures(0, (zero, zero))

    tops = [p[0, :, tile(t)] for t in range(tiles)]
    halves = [jnp.square(root[0, 1, :, tile(t)]) * 0.125 for t in range(tiles)]

    def turn(v, by):
        by %= TILE
        return pltpu.roll(v, by, 1) if by else v

    def cut(parts, kk, base):
        t, o = divmod(kk * 32, TILE)
        out = turn(parts[t], base - o)
        before = parts[t] if o else parts[max(t - 1, 0)]
        out = jnp.where(
            (lane >= base + 38) & (lane < base + 40), turn(before, base + 40 - o), out
        )
        if o + 32 == TILE and t + 1 < tiles:
            after = turn(parts[t + 1], base + 32)
            out = jnp.where((lane >= base + 32) & (lane < base + 34), after, out)
        return out

    for kk in range(nk):
        down_s[kk] = jnp.where(lane < 64, cut(tops, kk, 0), cut(halves, kk, 64))
    down_s[nk] = jnp.where(lane < 64, turn(tops[-1], 40), turn(halves[-1], 104))
    down_s[nk + 1] = jnp.where(lane < 64, turn(tops[0], 32), turn(halves[0], 96))
    mine = pl.multiple_of(k * ROWS, ROWS)
    down_r[pl.ds(mine, ROWS), :] = down_s[k]

    pl.semaphore_wait(barrier, expected)

    pending = []

    def send(src, dst, name, device, when=None, keep=True):
        copy = pltpu.make_async_remote_copy(
            src_ref=src,
            dst_ref=dst,
            send_sem=s(name + "_s"),
            recv_sem=s(name + "_r"),
            device_id=device,
            device_id_type=MESH,
        )
        if when is None:
            copy.start()
        else:
            pl.when(when)(copy.start)
        if keep:
            pending.append((copy, when))
        return copy

    def drain(ref, name, when=None):
        wait = pltpu.make_async_copy(ref, ref, s(name)).wait
        if when is None:
            wait()
        else:
            pl.when(when)(wait)

    ring(
        lambda kk: send(
            down_s.at[kk], down_r.at[pl.ds(mine, ROWS)], "down", at(0, 0, kk), keep=False
        )
    )
    for dg, far, has, slot in ((1, last, has_s, 248), (-1, first, has_n, 128)):

        @pl.when(far & has)
        def _():
            every(
                lambda kk: send(
                    down_s.at[kk], down_r.at[slot : slot + ROWS], f"down{slot}", at(dg, 0, kk),
                    keep=False,
                )
            )

        for dx, kk, has_x, i in ((1, 0, has_e, nk), (-1, nk - 1, has_w, nk + 1)):
            send(
                down_s.at[i], edge_r.at[slot : slot + ROWS], f"edge{slot}{dx}",
                at(dg, dx, kk), far & has & has_x,
            )
    for dx, kk, has_x, i in ((1, 0, has_e, nk), (-1, nk - 1, has_w, nk + 1)):
        send(
            down_s.at[i], edge_r.at[pl.ds(mine, ROWS)], f"edge{dx}", at(0, dx, kk), has_x
        )

    for c in surf_loads + mask_loads:
        c.wait()
    field[0, 0:32, 0:TILE] = surf_in[0]
    field[1, 0:32, 0:TILE] = surf_in[1]
    field[2, 0:32, 0:TILE] = jnp.sqrt((1.0 + water[1].astype(F32)) / surf_in[2])
    field[3, 0:32, 0:TILE] = surf_in[3]
    field[4, 0:32, 0:TILE] = water[0].astype(F32)

    def own(a, b):
        return field.at[:, a:b, 0:TILE]

    send(own(24, 32), own(40, 48), "right", {"grp": g, **right}, has_r)
    send(own(0, 8), own(32, 40), "left", {"grp": g, **left}, has_l)
    for dg, has, ref, n in ((1, has_s, above, "s"), (-1, has_n, below, "n")):
        send(own(0, 32), ref.at[:, 0:32], "line" + n, at(dg, 0, k), has)
        send(own(24, 32), ref.at[:, 40:48], "right" + n, {"grp": g + dg, **right}, has & has_r)
        send(own(0, 8), ref.at[:, 32:40], "left" + n, {"grp": g + dg, **left}, has & has_l)

    for c in rest_loads:
        c.wait()
    packs = lax.fori_loop(1, nz, first_closures, packs)
    col_s[0, 0], col_s[0, 1] = packs

    def send_soil(ph):
        send(row_s.at[ph, 1], row_r.at[ph, 0], f"row{ph}d", down, has_d)
        send(row_s.at[ph, 0], row_r.at[ph, 1], f"row{ph}u", up, has_u)
        send(col_s.at[ph, 1], col_r.at[ph, 0], f"col{ph}e", at(0, 1, k), has_e)
        send(col_s.at[ph, 0], col_r.at[ph, 1], f"col{ph}w", at(0, -1, k), has_w)

    def wait_soil(ph):
        drain(row_r.at[ph, 0], f"row{ph}d_r", has_u)
        drain(row_r.at[ph, 1], f"row{ph}u_r", has_d)
        drain(col_r.at[ph, 0], f"col{ph}e_r", has_w)
        drain(col_r.at[ph, 1], f"col{ph}w_r", has_e)

    send_soil(0)

    drain(own(40, 48), "right_r", has_l)
    drain(own(32, 40), "left_r", has_r)
    for has, ref, n in ((has_n, above, "s"), (has_s, below, "n")):
        drain(ref.at[:, 0:32], "line" + n + "_r", has)
        drain(ref.at[:, 40:48], "right" + n + "_r", has & has_l)
        drain(ref.at[:, 32:40], "left" + n + "_r", has & has_r)
    side = lax.broadcasted_iota(jnp.int32, (48, TILE), 1) < 64
    full = []
    for f in range(FIELDS):
        full.append(
            jnp.concatenate(
                [field[f, :, 0:TILE], jnp.where(side, below[f], above[f])], axis=1
            )
        )
    w0, level, bed, rain, land = full

    def next_of(v, axis):
        return pltpu.roll(v, v.shape[axis] - 1, axis)

    def prev_of(v, axis):
        return pltpu.roll(v, 1, axis)

    faces = [bed * next_of(bed, axis) for axis in (0, 1)]

    def outflow(w):
        carried = jnp.exp((5.0 / 3.0) * jnp.log(jnp.maximum(w, 1e-30)))
        surface = level + w
        total = None
        for axis in (0, 1):
            slope = surface - next_of(surface, axis)
            upwind = jnp.where(slope >= 0, carried, next_of(carried, axis))
            flux = faces[axis] * upwind * slope * lax.rsqrt(
                jnp.maximum(jnp.abs(slope), SLOPE_FLOOR)
            )
            net = flux - prev_of(flux, axis)
            total = net if total is None else total + net
        return total

    out0 = outflow(w0)

    drain(down_s.at[0 : nk - 1], "down_r")
    drain(down_s.at[0], "down128_r", has_s)
    drain(down_s.at[0], "down248_r", has_n)
    for dx, gets in ((1, first & has_w), (-1, last & has_e)):
        drain(edge_r.at[0:TILE], f"edge{dx}_r", gets)
        drain(down_s.at[0], f"edge128{dx}_r", gets & has_s)
        drain(down_s.at[0], f"edge248{dx}_r", gets & has_n)

    tall = lax.broadcasted_iota(jnp.int32, (TILE, TILE), 0)
    wide_lane = lax.broadcasted_iota(jnp.int32, (TILE, TILE), 1) & 63
    low = jnp.where(first, 38, 32)
    use_edge = (wide_lane >= low) & (wide_lane < low + 2) & (first | last)

    def received(a):
        rows = jnp.where(use_edge, edge_r[a : a + TILE, :], down_r[a : a + TILE, :])
        if a:
            rows = jnp.where((tall < ROWS) | (tall >= TILE - ROWS), rows, 0.0)
        return rows.T

    main, rim = received(0), received(TILE)

    def pick(a):
        body = [main[a : a + 32], rim[a : a + 32]]
        halo = [main[a + 32 : a + 40], rim[a + 32 : a + 40]]
        body, halo = (jnp.concatenate(v, axis=1) for v in (body, halo))
        return jnp.concatenate([body, halo, halo], axis=0)

    top = pick(0)
    leak = land * pick(64)

    def advance(w, out):
        rate = leak * (w - top)
        return jnp.maximum(w + SURFACE_STEP * (rain - rate - out), 0.0), rate

    w1, rate0 = advance(w0, out0)
    w2, rate1 = advance(w1, outflow(w1))
    rate2 = leak * (w2 - top)
    exchange = SURFACE_STEP * (rate0 + rate1 + rate2)
    square = jnp.concatenate([exchange[0:32, 0:TILE], jnp.zeros((96, TILE), F32)], axis=0)
    back_s[...] = square.T.reshape(nk, ROWS, TILE)
    back_r[k] = back_s[k]
    ring(
        lambda kk: send(back_s.at[kk], back_r.at[k], "back", at(0, 0, kk), keep=False)
    )
    w3, _ = advance(w2, outflow(w2))
    surf_in[0] = w3[0:32, 0:TILE]
    stores = [load(surf_in.at[0], water_out, "water")]

    def sums(ph, z, t, halo_rows, halo_cols):
        both = []
        for i, ref in enumerate((root, flow)):
            mid = ref[ph, z + 1, :, tile(t)]
            total = ref[ph, z, :, tile(t)] + ref[ph, z + 2, :, tile(t)]
            above_row, below_row = halo_rows[0][i], halo_rows[1][i]
            total += jnp.where(sub == 0, above_row, pltpu.roll(mid, 1, 0))
            total += jnp.where(sub == ROWS - 1, below_row, pltpu.roll(mid, ROWS - 1, 0))
            if t > 0:
                west = pltpu.roll(ref[ph, z + 1, :, tile(t - 1)], 1, 1)
            else:
                west = halo_cols[0][i]
            if t + 1 < tiles:
                east = pltpu.roll(ref[ph, z + 1, :, tile(t + 1)], TILE - 1, 1)
            else:
                east = halo_cols[1][i]
            total += jnp.where(lane == 0, west, pltpu.roll(mid, 1, 1))
            total += jnp.where(lane == TILE - 1, east, pltpu.roll(mid, TILE - 1, 1))
            both.append(total)
        q, r = both
        r += GRAVITY_STEP * (root[ph, z, :, tile(t)] - root[ph, z + 2, :, tile(t)])
        return q, r

    def plain_halo(ph, z):
        def rows(t):
            return [
                [row_r[ph, d, i, t, pl.ds(z, 1), :] for i in range(2)] for d in range(2)
            ]

        cols = [
            [shift_to(col_r[ph, d], z + 64 * i, (TILE - 1) * d) for i in range(2)]
            for d in range(2)
        ]
        return rows, cols

    def top_halo():
        def rows(t):
            return [[top_r[d, i : i + 1, tile(t)] for i in range(2)] for d in range(2)]

        cols = [
            [shift_to(tcol_r[d], 64 * i, (TILE - 1) * d) for i in range(2)]
            for d in range(2)
        ]
        return rows, cols

    def sweep(ph, z, t, halo, base, weight, extra):
        rows, cols = halo
        q, r = sums(ph, z, t, rows(t), cols)
        own_root = root[ph, z + 1, :, tile(t)]
        above_line = base + own_root * r
        if extra is not None:
            above_line += extra
        return above_line / (weight + own_root * q)

    def second_closures(z, packs, extras=None):
        halo = plain_halo(0, z)
        ends = []
        for t in range(tiles):
            c0 = cap[z, :, tile(t)]
            extra = None if extras is None else extras[t]
            head = sweep(0, z, t, halo, c0 * p[z, :, tile(t)], c0, extra)
            params = [par[i, z, :, tile(t)] for i in range(PARAMS)]
            c, se, q = closures(head, params)
            r = q * head
            ends.append((c, se, q, r, head, params[4]))
        for t in range(tiles):
            c, se, q, r, head, span = ends[t]
            gap = span * (se - sat[z, :, tile(t)])
            cap[z, :, tile(t)] = c
            num[z, :, tile(t)] = c * head - gap
            root[1, z + 1, :, tile(t)] = q
            flow[1, z + 1, :, tile(t)] = r
            if extras is None:
                put_row(row_s.at[1, 0], row_s.at[1, 1], 0, z, t, q)
                put_row(row_s.at[1, 0], row_s.at[1, 1], 1, z, t, r)
            else:
                for i, v in ((0, q), (1, r)):
                    top_s[0, i : i + 1, tile(t)] = v[0:1, :]
                    top_s[1, i : i + 1, tile(t)] = v[7:8, :]
        return put_cols(packs, z, *ends[0][2:4], *ends[-1][2:4])

    for t in range(tiles):
        for d in range(2):
            top_s[d, :, tile(t)] = zero
            for i in range(2):
                row_s[1, d, i, t, 0:ROWS, :] = zero
    wait_soil(0)
    packs = lax.fori_loop(1, nz, second_closures, (zero, zero))
    col_s[1, 0], col_s[1, 1] = packs
    send_soil(1)

    drain(down_s.at[0 : nk - 1], "back_r")
    extras = []
    for t in range(tiles):
        v = back_r[per * t]
        for i in range(1, per):
            v = jnp.where(lane >= 32 * i, turn(back_r[per * t + i], 32 * i), v)
        source[:, tile(t)] = v
        extras.append(v)
    tcol_s[0], tcol_s[1] = second_closures(0, (zero, zero), extras)
    send(top_s.at[1], top_r.at[0], "topd", down, has_d)
    send(top_s.at[0], top_r.at[1], "topu", up, has_u)
    send(tcol_s.at[1], tcol_r.at[0], "tope", at(0, 1, k), has_e)
    send(tcol_s.at[0], tcol_r.at[1], "topw", at(0, -1, k), has_w)

    wait_soil(1)

    def last_sweep(z, halo, extra=False):
        for t in range(tiles):
            more = source[:, tile(t)] if extra else None
            p[z, :, tile(t)] = sweep(
                1, z, t, halo, num[z, :, tile(t)], cap[z, :, tile(t)], more
            )

    def last_step(z, carry):
        last_sweep(z, plain_halo(1, z))
        return carry

    lax.fori_loop(1, nz, last_step, 0)
    stores.append(load(p.at[1:nz], head_out.at[1:nz], "head1"))
    drain(top_r.at[0], "topd_r", has_u)
    drain(top_r.at[1], "topu_r", has_d)
    drain(tcol_r.at[0], "tope_r", has_w)
    drain(tcol_r.at[1], "topw_r", has_e)
    last_sweep(0, top_halo(), True)
    stores.append(load(p.at[0:1], head_out.at[0:1], "head0"))

    drain(down_s.at[0 : nk - 1], "down_s")
    drain(down_s.at[0 : nk - 1], "back_s")
    drain(down_s.at[0:nk], "down248_s", last & has_s)
    drain(down_s.at[0:nk], "down128_s", first & has_n)
    for copy, when in pending:
        if when is None:
            copy.wait_send()
        else:
            pl.when(when)(copy.wait_send)
    for c in stores:
        c.wait()


def solution(mesh):
    sizes = tuple(mesh.shape[a] for a in ("grp", "gx", "gy"))
    nk = sizes[2]

    def local(
        pressure, soil_class, capacity_range, inverse_entry, shape_index, conductivity,
        depth, elevation, roughness, rain, land_mask, channel_mask,
    ):
        nz, _, wide = pressure.shape
        kinds = capacity_range.shape[0]
        hbm = pl.BlockSpec(memory_space=pl.ANY)
        soil = (nz, ROWS, wide)
        vmem = pltpu.VMEM
        head, water = pl.pallas_call(
            functools.partial(kernel, nz, wide, kinds, sizes),
            out_shape=(
                jax.ShapeDtypeStruct(pressure.shape, F32),
                jax.ShapeDtypeStruct(depth.shape[::-1], F32),
            ),
            in_specs=[hbm] * 12,
            out_specs=(hbm, hbm),
            scratch_shapes=[
                pltpu.SMEM((4, kinds), F32),
                vmem(soil, F32),
                vmem(soil, jnp.int32),
                vmem((PARAMS, *soil), F32),
                vmem(soil, F32),
                vmem(soil, F32),
                vmem((2, nz + 2, ROWS, wide), F32),
                vmem((2, nz + 2, ROWS, wide), F32),
                vmem(soil, F32),
                vmem((2, 2, 2, wide // TILE, nz, TILE), F32),
                vmem((2, 2, 2, wide // TILE, nz, TILE), F32),
                vmem((2, ROWS, wide), F32),
                vmem((2, ROWS, wide), F32),
                vmem((2, 2, ROWS, TILE), F32),
                vmem((2, 2, ROWS, TILE), F32),
                vmem((2, ROWS, TILE), F32),
                vmem((2, ROWS, TILE), F32),
                vmem((4, 32, TILE), F32),
                vmem((FIELDS, 48, 2 * TILE), F32),
                vmem((FIELDS, 48, TILE), F32),
                vmem((FIELDS, 48, TILE), F32),
                vmem((nk + 2, ROWS, TILE), F32),
                vmem((2 * TILE, TILE), F32),
                vmem((2 * TILE, TILE), F32),
                vmem((nk, ROWS, TILE), F32),
                vmem((nk, ROWS, TILE), F32),
                vmem((ROWS, wide), F32),
                vmem((2, 32, TILE), jnp.int32),
                pltpu.SemaphoreType.DMA((100,)),
            ],
            compiler_params=pltpu.CompilerParams(
                collective_id=0, has_side_effects=True, vmem_limit_bytes=48 * 1024 * 1024
            ),
        )(
            pressure, soil_class, capacity_range, inverse_entry, shape_index, conductivity,
            depth.T, elevation.T, roughness.T, rain.T, land_mask.T, channel_mask.T,
        )
        return head, water.T

    tile = P(None, ("grp", "gy"), "gx")
    flat = P("grp", ("gx", "gy"))
    return jax.shard_map(
        local,
        mesh=mesh,
        in_specs=(tile, tile, P(), P(), P(), P()) + (flat,) * 6,
        out_specs=(tile, flat),
        check_vma=False,
    )
```

```python
import functools

import jax
import jax.numpy as jnp
from jax import lax
from jax.experimental import pallas as pl
from jax.experimental.pallas import tpu as pltpu
from jax.sharding import PartitionSpec as P

MESH = pl.DeviceIdType.MESH
F32 = jnp.float32

STORAGE = 0.01
GRAVITY_STEP = 0.5
SUCTION_FLOOR = 0.01
SLOPE_FLOOR = 0.1
SURFACE_STEP = 0.3
LEAKANCE = 0.5

TILE = 128
ROWS = 8
FIELDS = 5
PARAMS = 6


def lanes():
    return lax.broadcasted_iota(jnp.int32, (ROWS, TILE), 1)


def sublanes():
    return lax.broadcasted_iota(jnp.int32, (ROWS, TILE), 0)


def gather(table, index):
    return jnp.take_along_axis(table, index, axis=1, mode="promise_in_bounds")


def build_tables(tab, kinds):
    lane = lanes()
    rows = []
    for i in range(4):
        row = jnp.zeros((ROWS, TILE), F32)
        for kind in range(kinds):
            row = jnp.where(lane == kind, tab[i, kind], row)
        rows.append(row)
    span, entry, shape, conduct = rows
    shape = jnp.where(lane < kinds, shape, 2.0)
    pore = 1.0 - 1.0 / shape
    expo = 1.0 / (1.0 - pore)
    return (
        -entry,
        expo,
        pore,
        span * pore * expo * entry,
        span,
        2.0 * jnp.sqrt(conduct),
    )


def closures(p, params):
    entry, expo, pore, lead, _, scale = params
    log_scaled = jnp.log(jnp.maximum(entry * p, SUCTION_FLOOR))
    up = expo * log_scaled
    log_sum = jnp.log(1.0 + jnp.exp(up))
    drop = pore * log_sum
    wet = pore * up - drop
    held = jnp.exp(wet)
    capacity = STORAGE + lead * jnp.exp(wet - log_sum)
    fourth = jnp.exp(-0.25 * drop)
    half = fourth * fourth
    root = scale * fourth * (1.0 - held)
    return capacity, half * half, root


def kernel(
    nz, wide, kinds, sizes,
    p_in, k_in, t0_in, t1_in, t2_in, t3_in,
    s0_in, s1_in, s2_in, s3_in, s4_in, s5_in,
    head_out, water_out,
    tab, p, kind, par, cap, sat, root, flow, num,
    row_s, row_r, top_s, top_r, col_s, col_r, tcol_s, tcol_r,
    surf_in, field, below, above,
    down_s, down_r, edge_r, back_s, back_r, source, water,
    sem,
):
    ng, nx, nk = sizes
    tiles = wide // TILE
    per = TILE // 32
    g, x, k = (lax.axis_index(a) for a in ("grp", "gx", "gy"))
    lane, sub = lanes(), sublanes()
    first, last = k == 0, k == nk - 1
    has_n, has_s = g > 0, g < ng - 1
    has_w, has_e = x > 0, x < nx - 1

    names = {}

    def s(name):
        return sem.at[names.setdefault(name, len(names))]

    def at(dg, dx, kk):
        return {"grp": g + dg, "gx": x + dx, "gy": kk}

    def tile(t):
        return slice(t * TILE, (t + 1) * TILE)

    def load(src, dst, name):
        copy = pltpu.make_async_copy(src, dst, s(name))
        copy.start()
        return copy

    table_loads = [
        load(ref, tab.at[i], f"tab{i}")
        for i, ref in enumerate((t0_in, t1_in, t2_in, t3_in))
    ]
    top_loads = [
        load(p_in.at[0:1], p.at[0:1], "p0"),
        load(k_in.at[0:1], kind.at[0:1], "k0"),
    ]
    surf_loads = [
        load(s0_in, surf_in.at[0], "s0"),
        load(s1_in, surf_in.at[1], "s1"),
        load(s2_in, surf_in.at[2], "s2"),
        load(s3_in, surf_in.at[3], "s3"),
    ]
    mask_loads = [
        load(s4_in, water.at[0], "s4"),
        load(s5_in, water.at[1], "s5"),
    ]
    rest_loads = [
        load(p_in.at[1:nz], p.at[1:nz], "p1"),
        load(k_in.at[1:nz], kind.at[1:nz], "k1"),
    ]

    barrier = pltpu.get_barrier_semaphore()

    def greet(device):
        pl.semaphore_signal(barrier, 1, device_id=device, device_id_type=MESH)

    def ring(body):
        def step(i, _):
            body(lax.rem(k + 1 + lax.rem(i + nk // 2 - 1, nk - 1), nk))
            return 0

        lax.fori_loop(0, nk - 1, step, 0)

    def every(body):
        def step(i, _):
            body(i)
            return 0

        lax.fori_loop(0, nk, step, 0)

    col = x * nk + k
    has_l, has_r = col > 0, col < nx * nk - 1
    left = {"gx": jnp.maximum(col - 1, 0) // nk, "gy": lax.rem(jnp.maximum(col - 1, 0), nk)}
    right = {"gx": (col + 1) // nk, "gy": lax.rem(col + 1, nk)}
    row = g * nk + k
    has_u, has_d = row > 0, row < ng * nk - 1
    up = {"grp": jnp.maximum(row - 1, 0) // nk, "gx": x, "gy": lax.rem(jnp.maximum(row - 1, 0), nk)}
    down = {"grp": (row + 1) // nk, "gx": x, "gy": lax.rem(row + 1, nk)}

    ring(lambda kk: greet(at(0, 0, kk)))
    for dg, has in ((-1, has_n), (1, has_s)):
        far = nk - 1 if dg < 0 else 0

        @pl.when(has)
        def _():
            greet(at(dg, 0, far))
            greet(at(dg, 0, k))

            @pl.when(has_l)
            def _():
                greet({"grp": g + dg, **left})

            @pl.when(has_r)
            def _():
                greet({"grp": g + dg, **right})

            @pl.when(first & has_w)
            def _():
                greet(at(dg, -1, far))

            @pl.when(last & has_e)
            def _():
                greet(at(dg, 1, far))

    @pl.when(has_w)
    def _():
        greet(at(0, -1, k))

        @pl.when(first)
        def _():
            every(lambda kk: greet(at(0, -1, kk)))

    @pl.when(has_e)
    def _():
        greet(at(0, 1, k))

        @pl.when(last)
        def _():
            every(lambda kk: greet(at(0, 1, kk)))

    def one(flag):
        return flag.astype(jnp.int32)

    rows_to = one(has_n) + one(has_s)
    cols_to = one(has_w) + one(has_e)
    corner = one(first & has_n) + one(last & has_s)
    expected = (
        (nk - 1)
        + corner * nk
        + rows_to * (1 + one(has_l) + one(has_r))
        + 2 * cols_to
        + corner * cols_to
    )

    zero = jnp.zeros((ROWS, TILE), F32)

    def clear(ref, rows):
        for r in range(0, rows, ROWS):
            for c in range(0, ref.shape[-1], TILE):
                ref[r : r + ROWS, c : c + TILE] = zero

    for t in range(tiles):
        for ph in range(2):
            for z in (0, nz + 1):
                root[ph, z, :, tile(t)] = zero
                flow[ph, z, :, tile(t)] = zero

    for d, has, has_g, ref in ((0, has_u, has_n, above), (1, has_d, has_s, below)):

        @pl.when(jnp.logical_not(has))
        def _():
            for ph in range(2):
                for i in range(2):
                    for t in range(tiles):
                        clear(row_r.at[ph, d, i, t], nz)
            clear(top_r.at[d], ROWS)

        @pl.when(jnp.logical_not(has_g))
        def _():
            for f in range(FIELDS):
                clear(ref.at[f], 48)
            off = 248 if d == 0 else 128
            clear(down_r.at[off : off + ROWS], ROWS)

        @pl.when(has_g & jnp.logical_not(has_r))
        def _():
            for f in range(FIELDS):
                ref[f, 32:40, :] = zero

        @pl.when(has_g & jnp.logical_not(has_l))
        def _():
            for f in range(FIELDS):
                ref[f, 40:48, :] = zero

    for d, has in ((0, has_w), (1, has_e)):

        @pl.when(jnp.logical_not(has))
        def _():
            for ph in range(2):
                col_r[ph, d] = zero
            tcol_r[d] = zero

    for d, has in ((0, has_r), (1, has_l)):

        @pl.when(jnp.logical_not(has))
        def _():
            for f in range(FIELDS):
                field[f, 32 + 8 * d : 40 + 8 * d, 0:TILE] = zero

    gets_edge = (first & has_w) | (last & has_e)

    @pl.when(jnp.logical_not(gets_edge))
    def _():
        clear(edge_r.at[0:TILE], TILE)

    for off, has in ((128, has_s), (248, has_n)):

        @pl.when(jnp.logical_not(gets_edge & has))
        def _():
            clear(edge_r.at[off : off + ROWS], ROWS)

    for c in table_loads:
        c.wait()
    tables = build_tables(tab, kinds)

    def layer_params(z, t):
        index = kind[z, :, tile(t)]
        return [gather(table, index) for table in tables]

    def put_row(dst_first, dst_last, i, z, t, value):
        dst_first[i, t, pl.ds(z, 1), :] = value[0:1, :]
        dst_last[i, t, pl.ds(z, 1), :] = value[7:8, :]

    def shift_to(value, frm, to):
        return pltpu.roll(value, lax.rem(to - frm + TILE, TILE), 1)

    def put_cols(packs, z, q0, r0, q1, r1):
        west, east = packs
        west = jnp.where(lane == z, shift_to(q0, 0, z), west)
        west = jnp.where(lane == z + 64, shift_to(r0, 0, z + 64), west)
        east = jnp.where(lane == z, shift_to(q1, TILE - 1, z), east)
        east = jnp.where(lane == z + 64, shift_to(r1, TILE - 1, z + 64), east)
        return west, east

    def first_closures(z, packs):
        ends = []
        for t in range(tiles):
            params = layer_params(z, t)
            for i in range(PARAMS):
                par[i, z, :, tile(t)] = params[i]
            pz = p[z, :, tile(t)]
            c, se, q = closures(pz, params)
            r = q * pz
            cap[z, :, tile(t)] = c
            sat[z, :, tile(t)] = se
            root[0, z + 1, :, tile(t)] = q
            flow[0, z + 1, :, tile(t)] = r
            put_row(row_s.at[0, 0], row_s.at[0, 1], 0, z, t, q)
            put_row(row_s.at[0, 0], row_s.at[0, 1], 1, z, t, r)
            ends.append((q, r))
        return put_cols(packs, z, *ends[0], *ends[-1])

    for c in top_loads:
        c.wait()
    packs = first_closures(0, (zero, zero))

    tops = [p[0, :, tile(t)] for t in range(tiles)]
    halves = [jnp.square(root[0, 1, :, tile(t)]) * 0.125 for t in range(tiles)]

    def turn(v, by):
        by %= TILE
        return pltpu.roll(v, by, 1) if by else v

    def cut(parts, kk, base):
        t, o = divmod(kk * 32, TILE)
        out = turn(parts[t], base - o)
        before = parts[t] if o else parts[max(t - 1, 0)]
        out = jnp.where(
            (lane >= base + 38) & (lane < base + 40), turn(before, base + 40 - o), out
        )
        if o + 32 == TILE and t + 1 < tiles:
            after = turn(parts[t + 1], base + 32)
            out = jnp.where((lane >= base + 32) & (lane < base + 34), after, out)
        return out

    for kk in range(nk):
        down_s[kk] = jnp.where(lane < 64, cut(tops, kk, 0), cut(halves, kk, 64))
    down_s[nk] = jnp.where(lane < 64, turn(tops[-1], 40), turn(halves[-1], 104))
    down_s[nk + 1] = jnp.where(lane < 64, turn(tops[0], 32), turn(halves[0], 96))
    mine = pl.multiple_of(k * ROWS, ROWS)
    down_r[pl.ds(mine, ROWS), :] = down_s[k]

    pl.semaphore_wait(barrier, expected)

    pending = []

    def send(src, dst, name, device, when=None, keep=True):
        copy = pltpu.make_async_remote_copy(
            src_ref=src,
            dst_ref=dst,
            send_sem=s(name + "_s"),
            recv_sem=s(name + "_r"),
            device_id=device,
            device_id_type=MESH,
        )
        if when is None:
            copy.start()
        else:
            pl.when(when)(copy.start)
        if keep:
            pending.append((copy, when))
        return copy

    def drain(ref, name, when=None):
        wait = pltpu.make_async_copy(ref, ref, s(name)).wait
        if when is None:
            wait()
        else:
            pl.when(when)(wait)

    ring(
        lambda kk: send(
            down_s.at[kk], down_r.at[pl.ds(mine, ROWS)], "down", at(0, 0, kk), keep=False
        )
    )
    for dg, far, has, slot in ((1, last, has_s, 248), (-1, first, has_n, 128)):

        @pl.when(far & has)
        def _():
            every(
                lambda kk: send(
                    down_s.at[kk], down_r.at[slot : slot + ROWS], f"down{slot}", at(dg, 0, kk),
                    keep=False,
                )
            )

        for dx, kk, has_x, i in ((1, 0, has_e, nk), (-1, nk - 1, has_w, nk + 1)):
            send(
                down_s.at[i], edge_r.at[slot : slot + ROWS], f"edge{slot}{dx}",
                at(dg, dx, kk), far & has & has_x,
            )
    for dx, kk, has_x, i in ((1, 0, has_e, nk), (-1, nk - 1, has_w, nk + 1)):
        send(
            down_s.at[i], edge_r.at[pl.ds(mine, ROWS)], f"edge{dx}", at(0, dx, kk), has_x
        )

    for c in surf_loads + mask_loads:
        c.wait()
    field[0, 0:32, 0:TILE] = surf_in[0]
    field[1, 0:32, 0:TILE] = surf_in[1]
    field[2, 0:32, 0:TILE] = jnp.sqrt((1.0 + water[1].astype(F32)) / surf_in[2])
    field[3, 0:32, 0:TILE] = surf_in[3]
    field[4, 0:32, 0:TILE] = water[0].astype(F32)

    def own(a, b):
        return field.at[:, a:b, 0:TILE]

    send(own(24, 32), own(40, 48), "right", {"grp": g, **right}, has_r)
    send(own(0, 8), own(32, 40), "left", {"grp": g, **left}, has_l)
    for dg, has, ref, n in ((1, has_s, above, "s"), (-1, has_n, below, "n")):
        send(own(0, 32), ref.at[:, 0:32], "line" + n, at(dg, 0, k), has)
        send(own(24, 32), ref.at[:, 40:48], "right" + n, {"grp": g + dg, **right}, has & has_r)
        send(own(0, 8), ref.at[:, 32:40], "left" + n, {"grp": g + dg, **left}, has & has_l)

    for c in rest_loads:
        c.wait()
    packs = lax.fori_loop(1, nz, first_closures, packs)
    col_s[0, 0], col_s[0, 1] = packs

    def send_soil(ph):
        send(row_s.at[ph, 1], row_r.at[ph, 0], f"row{ph}d", down, has_d)
        send(row_s.at[ph, 0], row_r.at[ph, 1], f"row{ph}u", up, has_u)
        send(col_s.at[ph, 1], col_r.at[ph, 0], f"col{ph}e", at(0, 1, k), has_e)
        send(col_s.at[ph, 0], col_r.at[ph, 1], f"col{ph}w", at(0, -1, k), has_w)

    def wait_soil(ph):
        drain(row_r.at[ph, 0], f"row{ph}d_r", has_u)
        drain(row_r.at[ph, 1], f"row{ph}u_r", has_d)
        drain(col_r.at[ph, 0], f"col{ph}e_r", has_w)
        drain(col_r.at[ph, 1], f"col{ph}w_r", has_e)

    send_soil(0)

    drain(own(40, 48), "right_r", has_l)
    drain(own(32, 40), "left_r", has_r)
    for has, ref, n in ((has_n, above, "s"), (has_s, below, "n")):
        drain(ref.at[:, 0:32], "line" + n + "_r", has)
        drain(ref.at[:, 40:48], "right" + n + "_r", has & has_l)
        drain(ref.at[:, 32:40], "left" + n + "_r", has & has_r)
    side = lax.broadcasted_iota(jnp.int32, (48, TILE), 1) < 64
    full = []
    for f in range(FIELDS):
        full.append(
            jnp.concatenate(
                [field[f, :, 0:TILE], jnp.where(side, below[f], above[f])], axis=1
            )
        )
    w0, level, bed, rain, land = full

    def next_of(v, axis):
        return pltpu.roll(v, v.shape[axis] - 1, axis)

    def prev_of(v, axis):
        return pltpu.roll(v, 1, axis)

    faces = [bed * next_of(bed, axis) for axis in (0, 1)]

    def outflow(w):
        carried = jnp.exp((5.0 / 3.0) * jnp.log(jnp.maximum(w, 1e-30)))
        surface = level + w
        total = None
        for axis in (0, 1):
            slope = surface - next_of(surface, axis)
            upwind = jnp.where(slope >= 0, carried, next_of(carried, axis))
            flux = faces[axis] * upwind * slope * lax.rsqrt(
                jnp.maximum(jnp.abs(slope), SLOPE_FLOOR)
            )
            net = flux - prev_of(flux, axis)
            total = net if total is None else total + net
        return total

    out0 = outflow(w0)

    drain(down_s.at[0 : nk - 1], "down_r")
    drain(down_s.at[0], "down128_r", has_s)
    drain(down_s.at[0], "down248_r", has_n)
    for dx, gets in ((1, first & has_w), (-1, last & has_e)):
        drain(edge_r.at[0:TILE], f"edge{dx}_r", gets)
        drain(down_s.at[0], f"edge128{dx}_r", gets & has_s)
        drain(down_s.at[0], f"edge248{dx}_r", gets & has_n)

    tall = lax.broadcasted_iota(jnp.int32, (TILE, TILE), 0)
    wide_lane = lax.broadcasted_iota(jnp.int32, (TILE, TILE), 1) & 63
    low = jnp.where(first, 38, 32)
    use_edge = (wide_lane >= low) & (wide_lane < low + 2) & (first | last)

    def received(a):
        rows = jnp.where(use_edge, edge_r[a : a + TILE, :], down_r[a : a + TILE, :])
        if a:
            rows = jnp.where((tall < ROWS) | (tall >= TILE - ROWS), rows, 0.0)
        return rows.T

    main, rim = received(0), received(TILE)

    def pick(a):
        body = [main[a : a + 32], rim[a : a + 32]]
        halo = [main[a + 32 : a + 40], rim[a + 32 : a + 40]]
        body, halo = (jnp.concatenate(v, axis=1) for v in (body, halo))
        return jnp.concatenate([body, halo, halo], axis=0)

    top = pick(0)
    leak = land * pick(64)

    def advance(w, out):
        rate = leak * (w - top)
        return jnp.maximum(w + SURFACE_STEP * (rain - rate - out), 0.0), rate

    w1, rate0 = advance(w0, out0)
    w2, rate1 = advance(w1, outflow(w1))
    rate2 = leak * (w2 - top)
    exchange = SURFACE_STEP * (rate0 + rate1 + rate2)
    square = jnp.concatenate([exchange[0:32, 0:TILE], jnp.zeros((96, TILE), F32)], axis=0)
    back_s[...] = square.T.reshape(nk, ROWS, TILE)
    back_r[k] = back_s[k]
    ring(
        lambda kk: send(back_s.at[kk], back_r.at[k], "back", at(0, 0, kk), keep=False)
    )
    w3, _ = advance(w2, outflow(w2))
    surf_in[0] = w3[0:32, 0:TILE]
    stores = [load(surf_in.at[0], water_out, "water")]

    def sums(ph, z, t, halo_rows, halo_cols):
        both = []
        for i, ref in enumerate((root, flow)):
            mid = ref[ph, z + 1, :, tile(t)]
            total = ref[ph, z, :, tile(t)] + ref[ph, z + 2, :, tile(t)]
            above_row, below_row = halo_rows[0][i], halo_rows[1][i]
            total += jnp.where(sub == 0, above_row, pltpu.roll(mid, 1, 0))
            total += jnp.where(sub == ROWS - 1, below_row, pltpu.roll(mid, ROWS - 1, 0))
            if t > 0:
                west = pltpu.roll(ref[ph, z + 1, :, tile(t - 1)], 1, 1)
            else:
                west = halo_cols[0][i]
            if t + 1 < tiles:
                east = pltpu.roll(ref[ph, z + 1, :, tile(t + 1)], TILE - 1, 1)
            else:
                east = halo_cols[1][i]
            total += jnp.where(lane == 0, west, pltpu.roll(mid, 1, 1))
            total += jnp.where(lane == TILE - 1, east, pltpu.roll(mid, TILE - 1, 1))
            both.append(total)
        q, r = both
        r += GRAVITY_STEP * (root[ph, z, :, tile(t)] - root[ph, z + 2, :, tile(t)])
        return q, r

    def plain_halo(ph, z):
        def rows(t):
            return [
                [row_r[ph, d, i, t, pl.ds(z, 1), :] for i in range(2)] for d in range(2)
            ]

        cols = [
            [shift_to(col_r[ph, d], z + 64 * i, (TILE - 1) * d) for i in range(2)]
            for d in range(2)
        ]
        return rows, cols

    def top_halo():
        def rows(t):
            return [[top_r[d, i : i + 1, tile(t)] for i in range(2)] for d in range(2)]

        cols = [
            [shift_to(tcol_r[d], 64 * i, (TILE - 1) * d) for i in range(2)]
            for d in range(2)
        ]
        return rows, cols

    def sweep(ph, z, t, halo, base, weight, extra):
        rows, cols = halo
        q, r = sums(ph, z, t, rows(t), cols)
        own_root = root[ph, z + 1, :, tile(t)]
        above_line = base + own_root * r
        if extra is not None:
            above_line += extra
        return above_line / (weight + own_root * q)

    def second_closures(z, packs, extras=None):
        halo = plain_halo(0, z)
        ends = []
        for t in range(tiles):
            c0 = cap[z, :, tile(t)]
            extra = None if extras is None else extras[t]
            head = sweep(0, z, t, halo, c0 * p[z, :, tile(t)], c0, extra)
            params = [par[i, z, :, tile(t)] for i in range(PARAMS)]
            c, se, q = closures(head, params)
            r = q * head
            ends.append((c, se, q, r, head, params[4]))
        for t in range(tiles):
            c, se, q, r, head, span = ends[t]
            gap = span * (se - sat[z, :, tile(t)])
            cap[z, :, tile(t)] = c
            num[z, :, tile(t)] = c * head - gap
            root[1, z + 1, :, tile(t)] = q
            flow[1, z + 1, :, tile(t)] = r
            if extras is None:
                put_row(row_s.at[1, 0], row_s.at[1, 1], 0, z, t, q)
                put_row(row_s.at[1, 0], row_s.at[1, 1], 1, z, t, r)
            else:
                for i, v in ((0, q), (1, r)):
                    top_s[0, i : i + 1, tile(t)] = v[0:1, :]
                    top_s[1, i : i + 1, tile(t)] = v[7:8, :]
        return put_cols(packs, z, *ends[0][2:4], *ends[-1][2:4])

    for t in range(tiles):
        for d in range(2):
            top_s[d, :, tile(t)] = zero
            for i in range(2):
                row_s[1, d, i, t, 0:ROWS, :] = zero
    wait_soil(0)
    packs = lax.fori_loop(1, nz, second_closures, (zero, zero))
    col_s[1, 0], col_s[1, 1] = packs
    send_soil(1)

    drain(down_s.at[0 : nk - 1], "back_r")
    extras = []
    for t in range(tiles):
        v = back_r[per * t]
        for i in range(1, per):
            v = jnp.where(lane >= 32 * i, turn(back_r[per * t + i], 32 * i), v)
        source[:, tile(t)] = v
        extras.append(v)
    tcol_s[0], tcol_s[1] = second_closures(0, (zero, zero), extras)
    send(top_s.at[1], top_r.at[0], "topd", down, has_d)
    send(top_s.at[0], top_r.at[1], "topu", up, has_u)
    send(tcol_s.at[1], tcol_r.at[0], "tope", at(0, 1, k), has_e)
    send(tcol_s.at[0], tcol_r.at[1], "topw", at(0, -1, k), has_w)

    wait_soil(1)

    def last_sweep(z, halo, extra=False):
        for t in range(tiles):
            more = source[:, tile(t)] if extra else None
            p[z, :, tile(t)] = sweep(
                1, z, t, halo, num[z, :, tile(t)], cap[z, :, tile(t)], more
            )

    def last_step(z, carry):
        last_sweep(z, plain_halo(1, z))
        return carry

    lax.fori_loop(1, nz, last_step, 0)
    stores.append(load(p.at[1:nz], head_out.at[1:nz], "head1"))
    drain(top_r.at[0], "topd_r", has_u)
    drain(top_r.at[1], "topu_r", has_d)
    drain(tcol_r.at[0], "tope_r", has_w)
    drain(tcol_r.at[1], "topw_r", has_e)
    last_sweep(0, top_halo(), True)
    stores.append(load(p.at[0:1], head_out.at[0:1], "head0"))

    drain(down_s.at[0 : nk - 1], "down_s")
    drain(down_s.at[0 : nk - 1], "back_s")
    drain(down_s.at[0:nk], "down248_s", last & has_s)
    drain(down_s.at[0:nk], "down128_s", first & has_n)
    for copy, when in pending:
        if when is None:
            copy.wait_send()
        else:
            pl.when(when)(copy.wait_send)
    for c in stores:
        c.wait()


def solution(mesh):
    sizes = tuple(mesh.shape[a] for a in ("grp", "gx", "gy"))
    nk = sizes[2]

    def local(
        pressure, soil_class, capacity_range, inverse_entry, shape_index, conductivity,
        depth, elevation, roughness, rain, land_mask, channel_mask,
    ):
        nz, _, wide = pressure.shape
        kinds = capacity_range.shape[0]
        hbm = pl.BlockSpec(memory_space=pl.ANY)
        soil = (nz, ROWS, wide)
        vmem = pltpu.VMEM
        head, water = pl.pallas_call(
            functools.partial(kernel, nz, wide, kinds, sizes),
            out_shape=(
                jax.ShapeDtypeStruct(pressure.shape, F32),
                jax.ShapeDtypeStruct(depth.shape[::-1], F32),
            ),
            in_specs=[hbm] * 12,
            out_specs=(hbm, hbm),
            scratch_shapes=[
                pltpu.SMEM((4, kinds), F32),
                vmem(soil, F32),
                vmem(soil, jnp.int32),
                vmem((PARAMS, *soil), F32),
                vmem(soil, F32),
                vmem(soil, F32),
                vmem((2, nz + 2, ROWS, wide), F32),
                vmem((2, nz + 2, ROWS, wide), F32),
                vmem(soil, F32),
                vmem((2, 2, 2, wide // TILE, nz, TILE), F32),
                vmem((2, 2, 2, wide // TILE, nz, TILE), F32),
                vmem((2, ROWS, wide), F32),
                vmem((2, ROWS, wide), F32),
                vmem((2, 2, ROWS, TILE), F32),
                vmem((2, 2, ROWS, TILE), F32),
                vmem((2, ROWS, TILE), F32),
                vmem((2, ROWS, TILE), F32),
                vmem((4, 32, TILE), F32),
                vmem((FIELDS, 48, 2 * TILE), F32),
                vmem((FIELDS, 48, TILE), F32),
                vmem((FIELDS, 48, TILE), F32),
                vmem((nk + 2, ROWS, TILE), F32),
                vmem((2 * TILE, TILE), F32),
                vmem((2 * TILE, TILE), F32),
                vmem((nk, ROWS, TILE), F32),
                vmem((nk, ROWS, TILE), F32),
                vmem((ROWS, wide), F32),
                vmem((2, 32, TILE), jnp.int32),
                pltpu.SemaphoreType.DMA((100,)),
            ],
            compiler_params=pltpu.CompilerParams(
                collective_id=0, has_side_effects=True, vmem_limit_bytes=60 * 1024 * 1024
            ),
        )(
            pressure, soil_class, capacity_range, inverse_entry, shape_index, conductivity,
            depth.T, elevation.T, roughness.T, rain.T, land_mask.T, channel_mask.T,
        )
        return head, water.T

    tile = P(None, ("grp", "gy"), "gx")
    flat = P("grp", ("gx", "gy"))
    return jax.shard_map(
        local,
        mesh=mesh,
        in_specs=(tile, tile, P(), P(), P(), P()) + (flat,) * 6,
        out_specs=(tile, flat),
        check_vma=False,
    )
```

```python
import functools

import jax
import jax.numpy as jnp
from jax import lax
from jax.experimental import pallas as pl
from jax.experimental.pallas import tpu as pltpu
from jax.sharding import PartitionSpec as P

MESH = pl.DeviceIdType.MESH
F32 = jnp.float32

STORAGE = 0.01
GRAVITY_STEP = 0.5
SUCTION_FLOOR = 0.01
SLOPE_FLOOR = 0.1
SURFACE_STEP = 0.3
LEAKANCE = 0.5

TILE = 128
ROWS = 8
FIELDS = 5
PARAMS = 6


def lanes():
    return lax.broadcasted_iota(jnp.int32, (ROWS, TILE), 1)


def sublanes():
    return lax.broadcasted_iota(jnp.int32, (ROWS, TILE), 0)


def gather(table, index):
    return jnp.take_along_axis(table, index, axis=1, mode="promise_in_bounds")


def build_tables(tab, kinds):
    lane = lanes()
    rows = []
    for i in range(4):
        row = jnp.zeros((ROWS, TILE), F32)
        for kind in range(kinds):
            row = jnp.where(lane == kind, tab[i, kind], row)
        rows.append(row)
    span, entry, shape, conduct = rows
    shape = jnp.where(lane < kinds, shape, 2.0)
    pore = 1.0 - 1.0 / shape
    expo = 1.0 / (1.0 - pore)
    return (
        -entry,
        expo,
        pore,
        span * pore * expo * entry,
        span,
        2.0 * jnp.sqrt(conduct),
    )


def closures(p, params):
    entry, expo, pore, lead, _, scale = params
    log_scaled = jnp.log(jnp.maximum(entry * p, SUCTION_FLOOR))
    up = expo * log_scaled
    log_sum = jnp.log(1.0 + jnp.exp(up))
    drop = pore * log_sum
    wet = pore * up - drop
    held = jnp.exp(wet)
    capacity = STORAGE + lead * jnp.exp(wet - log_sum)
    fourth = jnp.exp(-0.25 * drop)
    half = fourth * fourth
    root = scale * fourth * (1.0 - held)
    return capacity, half * half, root


def kernel(
    nz, wide, kinds, sizes,
    p_in, k_in, t0_in, t1_in, t2_in, t3_in,
    s0_in, s1_in, s2_in, s3_in, s4_in, s5_in,
    head_out, water_out,
    tab, p, kind, par, cap, sat, root, flow, num,
    row_s, row_r, top_s, top_r, col_s, col_r, tcol_s, tcol_r,
    surf_in, field, below, above,
    down_s, down_r, edge_r, under_s, under_r, rim_s, rim_r, source, water,
    sem,
):
    ng, nx, nk = sizes
    tiles = wide // TILE
    per = TILE // 32
    g, x, k = (lax.axis_index(a) for a in ("grp", "gx", "gy"))
    lane, sub = lanes(), sublanes()
    first, last = k == 0, k == nk - 1
    has_n, has_s = g > 0, g < ng - 1
    has_w, has_e = x > 0, x < nx - 1

    names = {}

    def s(name):
        return sem.at[names.setdefault(name, len(names))]

    def at(dg, dx, kk):
        return {"grp": g + dg, "gx": x + dx, "gy": kk}

    def tile(t):
        return slice(t * TILE, (t + 1) * TILE)

    def load(src, dst, name):
        copy = pltpu.make_async_copy(src, dst, s(name))
        copy.start()
        return copy

    table_loads = [
        load(ref, tab.at[i], f"tab{i}")
        for i, ref in enumerate((t0_in, t1_in, t2_in, t3_in))
    ]
    top_loads = [
        load(p_in.at[0:1], p.at[0:1], "p0"),
        load(k_in.at[0:1], kind.at[0:1], "k0"),
    ]
    surf_loads = [
        load(s0_in, surf_in.at[0], "s0"),
        load(s1_in, surf_in.at[1], "s1"),
        load(s2_in, surf_in.at[2], "s2"),
        load(s3_in, surf_in.at[3], "s3"),
    ]
    mask_loads = [
        load(s4_in, water.at[0], "s4"),
        load(s5_in, water.at[1], "s5"),
    ]
    rest_loads = [
        load(p_in.at[1:nz], p.at[1:nz], "p1"),
        load(k_in.at[1:nz], kind.at[1:nz], "k1"),
    ]

    barrier = pltpu.get_barrier_semaphore()

    def greet(device):
        pl.semaphore_signal(barrier, 1, device_id=device, device_id_type=MESH)

    def ring(body):
        def step(i, _):
            body(lax.rem(k + 1 + lax.rem(i + nk // 2 - 1, nk - 1), nk))
            return 0

        lax.fori_loop(0, nk - 1, step, 0)

    def every(body):
        def step(i, _):
            body(i)
            return 0

        lax.fori_loop(0, nk, step, 0)

    col = x * nk + k
    has_l, has_r = col > 0, col < nx * nk - 1
    left = {"gx": jnp.maximum(col - 1, 0) // nk, "gy": lax.rem(jnp.maximum(col - 1, 0), nk)}
    right = {"gx": (col + 1) // nk, "gy": lax.rem(col + 1, nk)}
    row = g * nk + k
    has_u, has_d = row > 0, row < ng * nk - 1
    up = {"grp": jnp.maximum(row - 1, 0) // nk, "gx": x, "gy": lax.rem(jnp.maximum(row - 1, 0), nk)}
    down = {"grp": (row + 1) // nk, "gx": x, "gy": lax.rem(row + 1, nk)}

    ring(lambda kk: greet(at(0, 0, kk)))
    for dg, has in ((-1, has_n), (1, has_s)):
        far = nk - 1 if dg < 0 else 0

        @pl.when(has)
        def _():
            greet(at(dg, 0, far))
            greet(at(dg, 0, k))
            ends = first if dg < 0 else last

            @pl.when(ends)
            def _():
                every(lambda kk: greet(at(dg, 0, kk)))

            @pl.when(has_l)
            def _():
                greet({"grp": g + dg, **left})

            @pl.when(has_r)
            def _():
                greet({"grp": g + dg, **right})

            @pl.when(first & has_w)
            def _():
                greet(at(dg, -1, far))

            @pl.when(last & has_e)
            def _():
                greet(at(dg, 1, far))

            @pl.when(ends & has_w)
            def _():
                greet(at(dg, -1, nk - 1))

            @pl.when(ends & has_e)
            def _():
                greet(at(dg, 1, 0))

    @pl.when(has_w)
    def _():
        greet(at(0, -1, k))
        greet(at(0, -1, nk - 1))

        @pl.when(first)
        def _():
            every(lambda kk: greet(at(0, -1, kk)))

    @pl.when(has_e)
    def _():
        greet(at(0, 1, k))
        greet(at(0, 1, 0))

        @pl.when(last)
        def _():
            every(lambda kk: greet(at(0, 1, kk)))

    def one(flag):
        return flag.astype(jnp.int32)

    rows_to = one(has_n) + one(has_s)
    cols_to = one(has_w) + one(has_e)
    corner = one(first & has_n) + one(last & has_s)
    side = one(first & has_w) + one(last & has_e)
    expected = (
        (nk - 1)
        + corner * nk
        + rows_to * (2 + one(has_l) + one(has_r))
        + 2 * cols_to
        + corner * cols_to
        + side * (nk + rows_to)
    )

    zero = jnp.zeros((ROWS, TILE), F32)

    def clear(ref, rows):
        for r in range(0, rows, ROWS):
            for c in range(0, ref.shape[-1], TILE):
                ref[r : r + ROWS, c : c + TILE] = zero

    for t in range(tiles):
        for ph in range(2):
            for z in (0, nz + 1):
                root[ph, z, :, tile(t)] = zero
                flow[ph, z, :, tile(t)] = zero

    for d, has, has_g, ref in ((0, has_u, has_n, above), (1, has_d, has_s, below)):

        @pl.when(jnp.logical_not(has))
        def _():
            for ph in range(2):
                for i in range(2):
                    for t in range(tiles):
                        clear(row_r.at[ph, d, i, t], nz)
            clear(top_r.at[d], ROWS)

        @pl.when(jnp.logical_not(has_g))
        def _():
            for f in range(FIELDS):
                clear(ref.at[f], 48)
            off = 248 if d == 0 else 128
            clear(down_r.at[off : off + ROWS], ROWS)

        @pl.when(has_g & jnp.logical_not(has_r))
        def _():
            for f in range(FIELDS):
                ref[f, 32:40, :] = zero

        @pl.when(has_g & jnp.logical_not(has_l))
        def _():
            for f in range(FIELDS):
                ref[f, 40:48, :] = zero

    for d, has in ((0, has_w), (1, has_e)):

        @pl.when(jnp.logical_not(has))
        def _():
            for ph in range(2):
                col_r[ph, d] = zero
            tcol_r[d] = zero

    for d, has in ((0, has_r), (1, has_l)):

        @pl.when(jnp.logical_not(has))
        def _():
            for f in range(FIELDS):
                field[f, 32 + 8 * d : 40 + 8 * d, 0:TILE] = zero

    gets_edge = (first & has_w) | (last & has_e)

    @pl.when(jnp.logical_not(gets_edge))
    def _():
        clear(edge_r.at[0:TILE], TILE)

    for off, has in ((128, has_s), (248, has_n)):

        @pl.when(jnp.logical_not(gets_edge & has))
        def _():
            clear(edge_r.at[off : off + ROWS], ROWS)

    for slot, has in ((nk, has_e), (nk + 1, has_w)):

        @pl.when(jnp.logical_not(has))
        def _():
            clear(under_r.at[slot], 2 * ROWS)

    gets_rim = (first & has_n) | (last & has_s)

    @pl.when(jnp.logical_not(gets_rim))
    def _():
        for j in range(nk):
            rim_r[j] = zero

    for slot, has in ((nk, has_e), (nk + 1, has_w)):

        @pl.when(jnp.logical_not(gets_rim & has))
        def _():
            rim_r[slot] = zero

    for c in table_loads:
        c.wait()
    tables = build_tables(tab, kinds)

    def layer_params(z, t):
        index = kind[z, :, tile(t)]
        return [gather(table, index) for table in tables]

    def put_row(dst_first, dst_last, i, z, t, value):
        dst_first[i, t, pl.ds(z, 1), :] = value[0:1, :]
        dst_last[i, t, pl.ds(z, 1), :] = value[7:8, :]

    def shift_to(value, frm, to):
        return pltpu.roll(value, lax.rem(to - frm + TILE, TILE), 1)

    def put_cols(packs, z, q0, r0, q1, r1):
        west, east = packs
        west = jnp.where(lane == z, shift_to(q0, 0, z), west)
        west = jnp.where(lane == z + 64, shift_to(r0, 0, z + 64), west)
        east = jnp.where(lane == z, shift_to(q1, TILE - 1, z), east)
        east = jnp.where(lane == z + 64, shift_to(r1, TILE - 1, z + 64), east)
        return west, east

    def first_closures(z, packs):
        ends = []
        for t in range(tiles):
            params = layer_params(z, t)
            for i in range(PARAMS):
                par[i, z, :, tile(t)] = params[i]
            pz = p[z, :, tile(t)]
            c, se, q = closures(pz, params)
            r = q * pz
            cap[z, :, tile(t)] = c
            sat[z, :, tile(t)] = se
            root[0, z + 1, :, tile(t)] = q
            flow[0, z + 1, :, tile(t)] = r
            put_row(row_s.at[0, 0], row_s.at[0, 1], 0, z, t, q)
            put_row(row_s.at[0, 0], row_s.at[0, 1], 1, z, t, r)
            ends.append((q, r))
        return put_cols(packs, z, *ends[0], *ends[-1])

    for c in top_loads:
        c.wait()
    packs = first_closures(0, (zero, zero))

    tops = [p[0, :, tile(t)] for t in range(tiles)]
    halves = [jnp.square(root[0, 1, :, tile(t)]) * 0.125 for t in range(tiles)]

    def turn(v, by):
        by %= TILE
        return pltpu.roll(v, by, 1) if by else v

    def cut(parts, kk, base):
        t, o = divmod(kk * 32, TILE)
        out = turn(parts[t], base - o)
        before = parts[t] if o else parts[max(t - 1, 0)]
        out = jnp.where(
            (lane >= base + 38) & (lane < base + 40), turn(before, base + 40 - o), out
        )
        if o + 32 == TILE and t + 1 < tiles:
            after = turn(parts[t + 1], base + 32)
            out = jnp.where((lane >= base + 32) & (lane < base + 34), after, out)
        return out

    for kk in range(nk):
        down_s[kk] = jnp.where(lane < 64, cut(tops, kk, 0), cut(halves, kk, 64))
    down_s[nk] = jnp.where(lane < 64, turn(tops[-1], 40), turn(halves[-1], 104))
    down_s[nk + 1] = jnp.where(lane < 64, turn(tops[0], 32), turn(halves[0], 96))
    mine = pl.multiple_of(k * ROWS, ROWS)
    down_r[pl.ds(mine, ROWS), :] = down_s[k]

    pending = []

    def send(src, dst, name, device, when=None, keep=True):
        copy = pltpu.make_async_remote_copy(
            src_ref=src,
            dst_ref=dst,
            send_sem=s(name + "_s"),
            recv_sem=s(name + "_r"),
            device_id=device,
            device_id_type=MESH,
        )
        if when is None:
            copy.start()
        else:
            pl.when(when)(copy.start)
        if keep:
            pending.append((copy, when))
        return copy

    def drain(ref, name, when=None):
        wait = pltpu.make_async_copy(ref, ref, s(name)).wait
        if when is None:
            wait()
        else:
            pl.when(when)(wait)

    for c in surf_loads + mask_loads:
        c.wait()
    field[0, 0:32, 0:TILE] = surf_in[0]
    field[1, 0:32, 0:TILE] = surf_in[1]
    field[2, 0:32, 0:TILE] = jnp.sqrt((1.0 + water[1].astype(F32)) / surf_in[2])
    field[3, 0:32, 0:TILE] = water[0].astype(F32)
    field[4, 0:32, 0:TILE] = surf_in[3]

    tall = jnp.concatenate([field[f, 0:32, 0:TILE] for f in range(4)], axis=0).T
    wet = [field[4, 0:32, 0:TILE]] * 3
    wet = jnp.concatenate(wet + [jnp.zeros((32, TILE), F32)], axis=0).T
    tall = [tall[ROWS * j : ROWS * (j + 1)] for j in range(nk)]
    wet = [wet[ROWS * j : ROWS * (j + 1)] for j in range(nk)]
    wet_down = [pltpu.roll(v, 2, 0) for v in wet]
    wet_up = [pltpu.roll(v, ROWS - 2, 0) for v in wet]
    inner = (sub >= 2) & (sub < 6)
    for j in range(nk):
        n, m = min(j + 1, nk - 1), max(j - 1, 0)
        ends = jnp.where(sub < 4, wet_down[n], wet_up[m])
        mid = jnp.where(lane < 32, wet_down[j], jnp.where(lane < 64, wet_up[j], ends))
        under_s[j, 0:ROWS, :] = tall[j]
        under_s[j, ROWS:, :] = jnp.where(inner, mid, jnp.where(sub < 2, tall[n], tall[m]))
    rim_s[0] = jnp.where(inner, wet_up[nk - 1], tall[nk - 1])
    rim_s[1] = jnp.where(inner, wet_down[0], tall[0])
    under_r[k] = under_s[k]

    for c in rest_loads:
        c.wait()
    packs = lax.fori_loop(1, nz, first_closures, packs)
    col_s[0, 0], col_s[0, 1] = packs

    def send_soil(ph):
        send(row_s.at[ph, 1], row_r.at[ph, 0], f"row{ph}d", down, has_d)
        send(row_s.at[ph, 0], row_r.at[ph, 1], f"row{ph}u", up, has_u)
        send(col_s.at[ph, 1], col_r.at[ph, 0], f"col{ph}e", at(0, 1, k), has_e)
        send(col_s.at[ph, 0], col_r.at[ph, 1], f"col{ph}w", at(0, -1, k), has_w)

    def wait_soil(ph):
        drain(row_r.at[ph, 0], f"row{ph}d_r", has_u)
        drain(row_r.at[ph, 1], f"row{ph}u_r", has_d)
        drain(col_r.at[ph, 0], f"col{ph}e_r", has_w)
        drain(col_r.at[ph, 1], f"col{ph}w_r", has_e)

    pl.semaphore_wait(barrier, expected)
    send_soil(0)

    ring(lambda kk: send(under_s.at[kk], under_r.at[k], "under", at(0, 0, kk), keep=False))
    for dx, ends, has_x, slot in ((1, last, has_e, nk + 1), (-1, first, has_w, nk)):

        @pl.when(ends & has_x)
        def _():
            every(
                lambda kk: send(
                    under_s.at[kk], under_r.at[slot], f"under{slot}", at(0, dx, kk), keep=False
                )
            )

    for i, (dg, has, far) in enumerate(((1, has_s, 0), (-1, has_n, nk - 1))):
        send(rim_s.at[i], rim_r.at[k], f"rim{i}", at(dg, 0, far), has)
        for dx, ends, has_x, slot in ((1, last, has_e, nk + 1), (-1, first, has_w, nk)):
            send(
                rim_s.at[i], rim_r.at[slot], f"rim{i}{slot}", at(dg, dx, far),
                has & ends & has_x,
            )

    def own(a, b):
        return field.at[:, a:b, 0:TILE]

    send(own(24, 32), own(40, 48), "right", {"grp": g, **right}, has_r)
    send(own(0, 8), own(32, 40), "left", {"grp": g, **left}, has_l)
    for dg, has, ref, n in ((1, has_s, above, "s"), (-1, has_n, below, "n")):
        send(own(0, 32), ref.at[:, 0:32], "line" + n, at(dg, 0, k), has)
        send(own(24, 32), ref.at[:, 40:48], "right" + n, {"grp": g + dg, **right}, has & has_r)
        send(own(0, 8), ref.at[:, 32:40], "left" + n, {"grp": g + dg, **left}, has & has_l)

    ring(
        lambda kk: send(
            down_s.at[kk], down_r.at[pl.ds(mine, ROWS)], "down", at(0, 0, kk), keep=False
        )
    )
    for dg, far, has, slot in ((1, last, has_s, 248), (-1, first, has_n, 128)):

        @pl.when(far & has)
        def _():
            every(
                lambda kk: send(
                    down_s.at[kk], down_r.at[slot : slot + ROWS], f"down{slot}", at(dg, 0, kk),
                    keep=False,
                )
            )

        for dx, kk, has_x, i in ((1, 0, has_e, nk), (-1, nk - 1, has_w, nk + 1)):
            send(
                down_s.at[i], edge_r.at[slot : slot + ROWS], f"edge{slot}{dx}",
                at(dg, dx, kk), far & has & has_x,
            )
    for dx, kk, has_x, i in ((1, 0, has_e, nk), (-1, nk - 1, has_w, nk + 1)):
        send(
            down_s.at[i], edge_r.at[pl.ds(mine, ROWS)], f"edge{dx}", at(0, dx, kk), has_x
        )

    def sums(ph, z, t, halo_rows, halo_cols):
        both = []
        for i, ref in enumerate((root, flow)):
            mid = ref[ph, z + 1, :, tile(t)]
            total = ref[ph, z, :, tile(t)] + ref[ph, z + 2, :, tile(t)]
            above_row, below_row = halo_rows[0][i], halo_rows[1][i]
            total += jnp.where(sub == 0, above_row, pltpu.roll(mid, 1, 0))
            total += jnp.where(sub == ROWS - 1, below_row, pltpu.roll(mid, ROWS - 1, 0))
            if t > 0:
                west = pltpu.roll(ref[ph, z + 1, :, tile(t - 1)], 1, 1)
            else:
                west = halo_cols[0][i]
            if t + 1 < tiles:
                east = pltpu.roll(ref[ph, z + 1, :, tile(t + 1)], TILE - 1, 1)
            else:
                east = halo_cols[1][i]
            total += jnp.where(lane == 0, west, pltpu.roll(mid, 1, 1))
            total += jnp.where(lane == TILE - 1, east, pltpu.roll(mid, TILE - 1, 1))
            both.append(total)
        q, r = both
        r += GRAVITY_STEP * (root[ph, z, :, tile(t)] - root[ph, z + 2, :, tile(t)])
        return q, r

    def plain_halo(ph, z):
        def rows(t):
            return [
                [row_r[ph, d, i, t, pl.ds(z, 1), :] for i in range(2)] for d in range(2)
            ]

        cols = [
            [shift_to(col_r[ph, d], z + 64 * i, (TILE - 1) * d) for i in range(2)]
            for d in range(2)
        ]
        return rows, cols

    def top_halo():
        def rows(t):
            return [[top_r[d, i : i + 1, tile(t)] for i in range(2)] for d in range(2)]

        cols = [
            [shift_to(tcol_r[d], 64 * i, (TILE - 1) * d) for i in range(2)]
            for d in range(2)
        ]
        return rows, cols

    def sweep(ph, z, t, halo, base, weight, extra):
        rows, cols = halo
        q, r = sums(ph, z, t, rows(t), cols)
        own_root = root[ph, z + 1, :, tile(t)]
        above_line = base + own_root * r
        if extra is not None:
            above_line += extra
        return above_line / (weight + own_root * q)

    def second_closures(z, packs, extras=None):
        halo = plain_halo(0, z)
        ends = []
        for t in range(tiles):
            c0 = cap[z, :, tile(t)]
            extra = None if extras is None else extras[t]
            head = sweep(0, z, t, halo, c0 * p[z, :, tile(t)], c0, extra)
            params = [par[i, z, :, tile(t)] for i in range(PARAMS)]
            c, se, q = closures(head, params)
            r = q * head
            ends.append((c, se, q, r, head, params[4]))
        for t in range(tiles):
            c, se, q, r, head, span = ends[t]
            gap = span * (se - sat[z, :, tile(t)])
            cap[z, :, tile(t)] = c
            num[z, :, tile(t)] = c * head - gap
            root[1, z + 1, :, tile(t)] = q
            flow[1, z + 1, :, tile(t)] = r
            if extras is None:
                put_row(row_s.at[1, 0], row_s.at[1, 1], 0, z, t, q)
                put_row(row_s.at[1, 0], row_s.at[1, 1], 1, z, t, r)
            else:
                for i, v in ((0, q), (1, r)):
                    top_s[0, i : i + 1, tile(t)] = v[0:1, :]
                    top_s[1, i : i + 1, tile(t)] = v[7:8, :]
        return put_cols(packs, z, *ends[0][2:4], *ends[-1][2:4])

    for t in range(tiles):
        for d in range(2):
            top_s[d, :, tile(t)] = zero
            for i in range(2):
                row_s[1, d, i, t, 0:ROWS, :] = zero
    wait_soil(0)
    packs = lax.fori_loop(1, nz, second_closures, (zero, zero))
    col_s[1, 0], col_s[1, 1] = packs
    send_soil(1)

    def next_of(v, axis):
        return pltpu.roll(v, v.shape[axis] - 1, axis)

    def prev_of(v, axis):
        return pltpu.roll(v, 1, axis)

    def outflow_of(level, bed):
        faces = [bed * next_of(bed, axis) for axis in (0, 1)]

        def outflow(w):
            carried = jnp.exp((5.0 / 3.0) * jnp.log(jnp.maximum(w, 1e-30)))
            surface = level + w
            total = None
            for axis in (0, 1):
                slope = surface - next_of(surface, axis)
                upwind = jnp.where(slope >= 0, carried, next_of(carried, axis))
                flux = faces[axis] * upwind * slope * lax.rsqrt(
                    jnp.maximum(jnp.abs(slope), SLOPE_FLOOR)
                )
                net = flux - prev_of(flux, axis)
                total = net if total is None else total + net
            return total

        return outflow

    drain(under_s.at[0 : nk - 1], "under_r")
    drain(under_s.at[0], f"under{nk}_r", has_e)
    drain(under_s.at[0], f"under{nk + 1}_r", has_w)
    for i, gets in enumerate((first & has_n, last & has_s)):
        drain(down_s.at[0:nk], f"rim{i}_r", gets)
        drain(down_s.at[0], f"rim{i}{nk}_r", gets & has_e)
        drain(down_s.at[0], f"rim{i}{nk + 1}_r", gets & has_w)
    use_rim = (first & (sub >= 4) & ((sub >= 6) | (lane >= 64))) | (
        last & (sub < 4) & ((sub < 2) | (lane >= 64))
    )
    near = [under_r[j, 0:ROWS, :] for j in range(nk + 2)]
    beyond = [jnp.where(use_rim, rim_r[j], under_r[j, ROWS:, :]) for j in range(nk + 2)]

    def gathered(parts, group):
        out = []
        for t in range(tiles):
            v = turn(parts[per * t], -32 * group)
            for i in range(1, per):
                v = jnp.where(lane >= 32 * i, turn(parts[per * t + i], 32 * (i - group)), v)
            out.append(v)
        ends = turn(parts[nk], -32 * group), turn(parts[nk + 1], 32 * (per - 1 - group))
        return out + [jnp.where(lane < 64, *ends)]

    def stacked(high, low):
        high, low = (jnp.concatenate(v, axis=1) for v in (high, low))
        return jnp.concatenate([high, low], axis=0)

    w, level, bed, land = (stacked(gathered(near, f), gathered(beyond, f)) for f in range(4))
    parts = [gathered(beyond, f) for f in range(3)]

    def spread(a, b):
        pairs = zip(a, b)
        return [
            jnp.where(sub < 4, pltpu.roll(u, ROWS - 2, 0), pltpu.roll(v, 2, 0)) for u, v in pairs
        ]

    rain = stacked(spread(parts[0], parts[1]), spread(parts[2], parts[2]))
    tops = []
    for i, ref in enumerate((root, flow)):
        high = [ref[0, 1, :, tile(t)] for t in range(tiles)]
        low = [
            jnp.where(sub == 0, row_r[0, 1, i, t, 0:1, :], jnp.where(sub == 7, row_r[0, 0, i, t, 0:1, :], 0.0))
            for t in range(tiles)
        ]
        west, east = (turn(col_r[0, d], v - 64 * i) for d, v in ((0, TILE - 1), (1, 0)))
        high.append(jnp.where(lane < 64, east, west))
        tops.append(stacked(high, low + [zero]))
    q_top, r_top = tops
    seep = land * q_top * 0.125
    outflow = outflow_of(level, bed)
    exchange = None
    for step in range(3):
        rate = seep * (q_top * w - r_top)
        exchange = rate if exchange is None else exchange + rate
        if step < 2:
            w = jnp.maximum(w + SURFACE_STEP * (rain - rate - outflow(w)), 0.0)
    extras = [SURFACE_STEP * exchange[0:ROWS, tile(t)] for t in range(tiles)]
    for t in range(tiles):
        source[:, tile(t)] = extras[t]
    tcol_s[0], tcol_s[1] = second_closures(0, (zero, zero), extras)
    send(top_s.at[1], top_r.at[0], "topd", down, has_d)
    send(top_s.at[0], top_r.at[1], "topu", up, has_u)
    send(tcol_s.at[1], tcol_r.at[0], "tope", at(0, 1, k), has_e)
    send(tcol_s.at[0], tcol_r.at[1], "topw", at(0, -1, k), has_w)

    drain(own(40, 48), "right_r", has_l)
    drain(own(32, 40), "left_r", has_r)
    for has, ref, n in ((has_n, above, "s"), (has_s, below, "n")):
        drain(ref.at[:, 0:32], "line" + n + "_r", has)
        drain(ref.at[:, 40:48], "right" + n + "_r", has & has_l)
        drain(ref.at[:, 32:40], "left" + n + "_r", has & has_r)
    side = lax.broadcasted_iota(jnp.int32, (48, TILE), 1) < 64
    full = []
    for f in range(FIELDS):
        full.append(
            jnp.concatenate(
                [field[f, :, 0:TILE], jnp.where(side, below[f], above[f])], axis=1
            )
        )
    w0, level, bed, land, rain = full

    outflow = outflow_of(level, bed)
    out0 = outflow(w0)

    drain(down_s.at[0 : nk - 1], "down_r")
    drain(down_s.at[0], "down128_r", has_s)
    drain(down_s.at[0], "down248_r", has_n)
    for dx, gets in ((1, first & has_w), (-1, last & has_e)):
        drain(edge_r.at[0:TILE], f"edge{dx}_r", gets)
        drain(down_s.at[0], f"edge128{dx}_r", gets & has_s)
        drain(down_s.at[0], f"edge248{dx}_r", gets & has_n)

    tall = lax.broadcasted_iota(jnp.int32, (TILE, TILE), 0)
    wide_lane = lax.broadcasted_iota(jnp.int32, (TILE, TILE), 1) & 63
    low = jnp.where(first, 38, 32)
    use_edge = (wide_lane >= low) & (wide_lane < low + 2) & (first | last)

    def received(a):
        rows = jnp.where(use_edge, edge_r[a : a + TILE, :], down_r[a : a + TILE, :])
        if a:
            rows = jnp.where((tall < ROWS) | (tall >= TILE - ROWS), rows, 0.0)
        return rows.T

    main, rim = received(0), received(TILE)

    def pick(a):
        body = [main[a : a + 32], rim[a : a + 32]]
        halo = [main[a + 32 : a + 40], rim[a + 32 : a + 40]]
        body, halo = (jnp.concatenate(v, axis=1) for v in (body, halo))
        return jnp.concatenate([body, halo, halo], axis=0)

    top = pick(0)
    leak = land * pick(64)

    def advance(w, out):
        return jnp.maximum(w + SURFACE_STEP * (rain - leak * (w - top) - out), 0.0)

    for step in range(3):
        w0 = advance(w0, out0 if step == 0 else outflow(w0))
    water_out[...] = w0[0:32, 0:TILE]

    wait_soil(1)

    def last_sweep(z, halo, extra=False):
        for t in range(tiles):
            more = source[:, tile(t)] if extra else None
            head_out[z, :, tile(t)] = sweep(
                1, z, t, halo, num[z, :, tile(t)], cap[z, :, tile(t)], more
            )

    def last_step(z, carry):
        last_sweep(z, plain_halo(1, z))
        return carry

    lax.fori_loop(1, nz, last_step, 0)
    drain(top_r.at[0], "topd_r", has_u)
    drain(top_r.at[1], "topu_r", has_d)
    drain(tcol_r.at[0], "tope_r", has_w)
    drain(tcol_r.at[1], "topw_r", has_e)
    last_sweep(0, top_halo(), True)

    drain(down_s.at[0 : nk - 1], "down_s")
    drain(under_s.at[0 : nk - 1], "under_s")
    drain(under_s, f"under{nk + 1}_s", last & has_e)
    drain(under_s, f"under{nk}_s", first & has_w)
    drain(down_s.at[0:nk], "down248_s", last & has_s)
    drain(down_s.at[0:nk], "down128_s", first & has_n)
    for copy, when in pending:
        if when is None:
            copy.wait_send()
        else:
            pl.when(when)(copy.wait_send)


def solution(mesh):
    sizes = tuple(mesh.shape[a] for a in ("grp", "gx", "gy"))
    nk = sizes[2]

    def local(
        pressure, soil_class, capacity_range, inverse_entry, shape_index, conductivity,
        depth, elevation, roughness, rain, land_mask, channel_mask,
    ):
        nz, _, wide = pressure.shape
        kinds = capacity_range.shape[0]
        hbm = pl.BlockSpec(memory_space=pl.ANY)
        soil = (nz, ROWS, wide)
        vmem = pltpu.VMEM
        head, water = pl.pallas_call(
            functools.partial(kernel, nz, wide, kinds, sizes),
            out_shape=(
                vmem(pressure.shape, F32),
                vmem(depth.shape[::-1], F32),
            ),
            in_specs=[hbm] * 12,
            out_specs=(pl.BlockSpec(memory_space=vmem),) * 2,
            scratch_shapes=[
                pltpu.SMEM((4, kinds), F32),
                vmem(soil, F32),
                vmem(soil, jnp.int32),
                vmem((PARAMS, *soil), F32),
                vmem(soil, F32),
                vmem(soil, F32),
                vmem((2, nz + 2, ROWS, wide), F32),
                vmem((2, nz + 2, ROWS, wide), F32),
                vmem(soil, F32),
                vmem((2, 2, 2, wide // TILE, nz, TILE), F32),
                vmem((2, 2, 2, wide // TILE, nz, TILE), F32),
                vmem((2, ROWS, wide), F32),
                vmem((2, ROWS, wide), F32),
                vmem((2, 2, ROWS, TILE), F32),
                vmem((2, 2, ROWS, TILE), F32),
                vmem((2, ROWS, TILE), F32),
                vmem((2, ROWS, TILE), F32),
                vmem((4, 32, TILE), F32),
                vmem((FIELDS, 48, 2 * TILE), F32),
                vmem((FIELDS, 48, TILE), F32),
                vmem((FIELDS, 48, TILE), F32),
                vmem((nk + 2, ROWS, TILE), F32),
                vmem((2 * TILE, TILE), F32),
                vmem((2 * TILE, TILE), F32),
                vmem((nk, 2 * ROWS, TILE), F32),
                vmem((nk + 2, 2 * ROWS, TILE), F32),
                vmem((2, ROWS, TILE), F32),
                vmem((nk + 2, ROWS, TILE), F32),
                vmem((ROWS, wide), F32),
                vmem((2, 32, TILE), jnp.int32),
                pltpu.SemaphoreType.DMA((100,)),
            ],
            compiler_params=pltpu.CompilerParams(
                collective_id=0, has_side_effects=True, vmem_limit_bytes=60 * 1024 * 1024
            ),
        )(
            pressure, soil_class, capacity_range, inverse_entry, shape_index, conductivity,
            depth.T, elevation.T, roughness.T, rain.T, land_mask.T, channel_mask.T,
        )
        return head, water.T

    tile = P(None, ("grp", "gy"), "gx")
    flat = P("grp", ("gx", "gy"))
    return jax.shard_map(
        local,
        mesh=mesh,
        in_specs=(tile, tile, P(), P(), P(), P()) + (flat,) * 6,
        out_specs=(tile, flat),
        check_vma=False,
    )
```

```python
import functools

import jax
import jax.numpy as jnp
from jax import lax
from jax.experimental import pallas as pl
from jax.experimental.pallas import tpu as pltpu
from jax.sharding import PartitionSpec as P

MESH = pl.DeviceIdType.MESH
F32 = jnp.float32

STORAGE = 0.01
GRAVITY_STEP = 0.5
SUCTION_FLOOR = 0.01
SLOPE_FLOOR = 0.1
SURFACE_STEP = 0.3
LEAKANCE = 0.5

TILE = 128
ROWS = 8
FIELDS = 5
PARAMS = 6


def lanes():
    return lax.broadcasted_iota(jnp.int32, (ROWS, TILE), 1)


def sublanes():
    return lax.broadcasted_iota(jnp.int32, (ROWS, TILE), 0)


def gather(table, index):
    return jnp.take_along_axis(table, index, axis=1, mode="promise_in_bounds")


def build_tables(tab, kinds):
    lane = lanes()
    rows = []
    for i in range(4):
        row = jnp.zeros((ROWS, TILE), F32)
        for kind in range(kinds):
            row = jnp.where(lane == kind, tab[i, kind], row)
        rows.append(row)
    span, entry, shape, conduct = rows
    shape = jnp.where(lane < kinds, shape, 2.0)
    pore = 1.0 - 1.0 / shape
    expo = 1.0 / (1.0 - pore)
    return (
        -entry,
        expo,
        pore,
        span * pore * expo * entry,
        span,
        2.0 * jnp.sqrt(conduct),
    )


def closures(p, params):
    entry, expo, pore, lead, _, scale = params
    log_scaled = jnp.log(jnp.maximum(entry * p, SUCTION_FLOOR))
    up = expo * log_scaled
    log_sum = jnp.log(1.0 + jnp.exp(up))
    drop = pore * log_sum
    wet = pore * up - drop
    held = jnp.exp(wet)
    capacity = STORAGE + lead * jnp.exp(wet - log_sum)
    fourth = jnp.exp(-0.25 * drop)
    half = fourth * fourth
    root = scale * fourth * (1.0 - held)
    return capacity, half * half, root


def kernel(
    nz, wide, kinds, sizes, cut_z,
    p_in, k_in, t0_in, t1_in, t2_in, t3_in,
    s0_in, s1_in, s2_in, s3_in, s4_in, s5_in,
    head_out, water_out,
    tab, p, kind, par, cap, sat, root, flow, num,
    row_s, row_r, top_s, top_r, col_s, col_r, tcol_s, tcol_r,
    surf_in, field, below, above,
    down_s, down_r, edge_r, back_s, back_r, water,
    sem,
):
    ng, nx, nk = sizes
    tiles = wide // TILE
    per = TILE // 32
    g, x, k = (lax.axis_index(a) for a in ("grp", "gx", "gy"))
    lane, sub = lanes(), sublanes()
    first, last = k == 0, k == nk - 1
    has_n, has_s = g > 0, g < ng - 1
    has_w, has_e = x > 0, x < nx - 1

    names = {}

    def s(name):
        return sem.at[names.setdefault(name, len(names))]

    def at(dg, dx, kk):
        return {"grp": g + dg, "gx": x + dx, "gy": kk}

    def tile(t):
        return slice(t * TILE, (t + 1) * TILE)

    def load(src, dst, name):
        copy = pltpu.make_async_copy(src, dst, s(name))
        copy.start()
        return copy

    table_loads = [
        load(ref, tab.at[i], f"tab{i}")
        for i, ref in enumerate((t0_in, t1_in, t2_in, t3_in))
    ]
    top_loads = [
        load(p_in.at[0:1], p.at[0:1], "p0"),
        load(k_in.at[0:1], kind.at[0:1], "k0"),
    ]
    surf_loads = [
        load(s0_in, surf_in.at[0], "s0"),
        load(s1_in, surf_in.at[1], "s1"),
        load(s2_in, surf_in.at[2], "s2"),
        load(s3_in, surf_in.at[3], "s3"),
    ]
    mask_loads = [
        load(s4_in, water.at[0], "s4"),
        load(s5_in, water.at[1], "s5"),
    ]
    rest_loads = [
        load(p_in.at[1:nz], p.at[1:nz], "p1"),
        load(k_in.at[1:nz], kind.at[1:nz], "k1"),
    ]

    barrier = pltpu.get_barrier_semaphore()

    def greet(device):
        pl.semaphore_signal(barrier, 1, device_id=device, device_id_type=MESH)

    def ring(body):
        for away in sorted(range(1, nk), key=lambda d: -min(d, nk - d)):
            body(jnp.where(k + away >= nk, k + away - nk, k + away))

    def every(body):
        def step(i, _):
            body(i)
            return 0

        lax.fori_loop(0, nk, step, 0)

    col = x * nk + k
    has_l, has_r = col > 0, col < nx * nk - 1
    left = {"gx": jnp.maximum(col - 1, 0) // nk, "gy": lax.rem(jnp.maximum(col - 1, 0), nk)}
    right = {"gx": (col + 1) // nk, "gy": lax.rem(col + 1, nk)}
    row = g * nk + k
    has_u, has_d = row > 0, row < ng * nk - 1
    up = {"grp": jnp.maximum(row - 1, 0) // nk, "gx": x, "gy": lax.rem(jnp.maximum(row - 1, 0), nk)}
    down = {"grp": (row + 1) // nk, "gx": x, "gy": lax.rem(row + 1, nk)}

    ring(lambda kk: greet(at(0, 0, kk)))
    for dg, has in ((-1, has_n), (1, has_s)):
        far = nk - 1 if dg < 0 else 0

        @pl.when(has)
        def _():
            greet(at(dg, 0, far))
            greet(at(dg, 0, k))

            @pl.when(has_l)
            def _():
                greet({"grp": g + dg, **left})

            @pl.when(has_r)
            def _():
                greet({"grp": g + dg, **right})

            @pl.when(first & has_w)
            def _():
                greet(at(dg, -1, far))

            @pl.when(last & has_e)
            def _():
                greet(at(dg, 1, far))

    @pl.when(has_w)
    def _():
        greet(at(0, -1, k))

        @pl.when(first)
        def _():
            every(lambda kk: greet(at(0, -1, kk)))

    @pl.when(has_e)
    def _():
        greet(at(0, 1, k))

        @pl.when(last)
        def _():
            every(lambda kk: greet(at(0, 1, kk)))

    def one(flag):
        return flag.astype(jnp.int32)

    rows_to = one(has_n) + one(has_s)
    cols_to = one(has_w) + one(has_e)
    corner = one(first & has_n) + one(last & has_s)
    expected = (
        (nk - 1)
        + corner * nk
        + rows_to * (1 + one(has_l) + one(has_r))
        + 2 * cols_to
        + corner * cols_to
    )

    zero = jnp.zeros((ROWS, TILE), F32)

    def clear(ref, rows):
        for r in range(0, rows, ROWS):
            for c in range(0, ref.shape[-1], TILE):
                ref[r : r + ROWS, c : c + TILE] = zero

    for t in range(tiles):
        for ph in range(2):
            for z in (0, nz + 1):
                root[ph, z, :, tile(t)] = zero
                flow[ph, z, :, tile(t)] = zero

    for d, has, has_g, ref in ((0, has_u, has_n, above), (1, has_d, has_s, below)):

        @pl.when(jnp.logical_not(has))
        def _():
            for ph in range(2):
                for i in range(2):
                    for t in range(tiles):
                        clear(row_r.at[ph, d, i, t], nz)
            clear(top_r.at[d], ROWS)

        @pl.when(jnp.logical_not(has_g))
        def _():
            for f in range(FIELDS):
                clear(ref.at[f], 48)
            off = 248 if d == 0 else 128
            clear(down_r.at[off : off + ROWS], ROWS)

        @pl.when(has_g & jnp.logical_not(has_r))
        def _():
            for f in range(FIELDS):
                ref[f, 32:40, :] = zero

        @pl.when(has_g & jnp.logical_not(has_l))
        def _():
            for f in range(FIELDS):
                ref[f, 40:48, :] = zero

    for d, has in ((0, has_w), (1, has_e)):

        @pl.when(jnp.logical_not(has))
        def _():
            for c in range(3):
                col_r[c, d] = zero
            tcol_r[d] = zero

    for d, has in ((0, has_r), (1, has_l)):

        @pl.when(jnp.logical_not(has))
        def _():
            for f in range(FIELDS):
                field[f, 32 + 8 * d : 40 + 8 * d, 0:TILE] = zero

    gets_edge = (first & has_w) | (last & has_e)

    @pl.when(jnp.logical_not(gets_edge))
    def _():
        clear(edge_r.at[0:TILE], TILE)

    for off, has in ((128, has_s), (248, has_n)):

        @pl.when(jnp.logical_not(gets_edge & has))
        def _():
            clear(edge_r.at[off : off + ROWS], ROWS)

    for c in table_loads:
        c.wait()
    tables = build_tables(tab, kinds)

    def layer_params(z, t):
        index = kind[z, :, tile(t)]
        return [gather(table, index) for table in tables]

    def put_row(dst_first, dst_last, i, z, t, value):
        dst_first[i, t, pl.ds(z, 1), :] = value[0:1, :]
        dst_last[i, t, pl.ds(z, 1), :] = value[7:8, :]

    def shift_to(value, frm, to):
        return pltpu.roll(value, lax.rem(to - frm + TILE, TILE), 1)

    def put_cols(packs, z, q0, r0, q1, r1):
        west, east = packs
        west = jnp.where(lane == z, shift_to(q0, 0, z), west)
        west = jnp.where(lane == z + 64, shift_to(r0, 0, z + 64), west)
        east = jnp.where(lane == z, shift_to(q1, TILE - 1, z), east)
        east = jnp.where(lane == z + 64, shift_to(r1, TILE - 1, z + 64), east)
        return west, east

    def first_closures(z, packs):
        ends = []
        for t in range(tiles):
            params = layer_params(z, t)
            for i in range(PARAMS):
                par[i, z, :, tile(t)] = params[i]
            pz = p[z, :, tile(t)]
            c, se, q = closures(pz, params)
            r = q * pz
            cap[z, :, tile(t)] = c
            sat[z, :, tile(t)] = se
            root[0, z + 1, :, tile(t)] = q
            flow[0, z + 1, :, tile(t)] = r
            put_row(row_s.at[0, 0], row_s.at[0, 1], 0, z, t, q)
            put_row(row_s.at[0, 0], row_s.at[0, 1], 1, z, t, r)
            ends.append((q, r))
        return put_cols(packs, z, *ends[0], *ends[-1])

    for c in top_loads:
        c.wait()
    packs = first_closures(0, (zero, zero))

    tops = [p[0, :, tile(t)] for t in range(tiles)]
    halves = [jnp.square(root[0, 1, :, tile(t)]) * 0.125 for t in range(tiles)]

    def turn(v, by):
        by %= TILE
        return pltpu.roll(v, by, 1) if by else v

    def cut(parts, kk, base):
        t, o = divmod(kk * 32, TILE)
        out = turn(parts[t], base - o)
        before = parts[t] if o else parts[max(t - 1, 0)]
        out = jnp.where(
            (lane >= base + 38) & (lane < base + 40), turn(before, base + 40 - o), out
        )
        if o + 32 == TILE and t + 1 < tiles:
            after = turn(parts[t + 1], base + 32)
            out = jnp.where((lane >= base + 32) & (lane < base + 34), after, out)
        return out

    for kk in range(nk):
        down_s[kk] = jnp.where(lane < 64, cut(tops, kk, 0), cut(halves, kk, 64))
    down_s[nk] = jnp.where(lane < 64, turn(tops[-1], 40), turn(halves[-1], 104))
    down_s[nk + 1] = jnp.where(lane < 64, turn(tops[0], 32), turn(halves[0], 96))
    mine = pl.multiple_of(k * ROWS, ROWS)
    down_r[pl.ds(mine, ROWS), :] = down_s[k]

    pending = []

    def send(src, dst, name, device, when=None, keep=True):
        copy = pltpu.make_async_remote_copy(
            src_ref=src,
            dst_ref=dst,
            send_sem=s(name + "_s"),
            recv_sem=s(name + "_r"),
            device_id=device,
            device_id_type=MESH,
        )
        if when is None:
            copy.start()
        else:
            pl.when(when)(copy.start)
        if keep:
            pending.append((copy, when))
        return copy

    def drain(ref, name, when=None):
        wait = pltpu.make_async_copy(ref, ref, s(name)).wait
        if when is None:
            wait()
        else:
            pl.when(when)(wait)

    for c in surf_loads + mask_loads:
        c.wait()
    field[0, 0:32, 0:TILE] = surf_in[0]
    field[1, 0:32, 0:TILE] = surf_in[1]
    field[2, 0:32, 0:TILE] = jnp.sqrt((1.0 + water[1].astype(F32)) / surf_in[2])
    field[3, 0:32, 0:TILE] = surf_in[3]
    field[4, 0:32, 0:TILE] = water[0].astype(F32)

    for c in rest_loads:
        c.wait()
    packs = lax.fori_loop(1, nz, first_closures, packs)
    col_s[0, 0], col_s[0, 1] = packs

    pl.semaphore_wait(barrier, expected)
    ring(
        lambda kk: send(
            down_s.at[kk], down_r.at[pl.ds(mine, ROWS)], "down", at(0, 0, kk), keep=False
        )
    )
    for dg, far, has, slot in ((1, last, has_s, 248), (-1, first, has_n, 128)):

        @pl.when(far & has)
        def _():
            every(
                lambda kk: send(
                    down_s.at[kk], down_r.at[slot : slot + ROWS], f"down{slot}", at(dg, 0, kk),
                    keep=False,
                )
            )

        for dx, kk, has_x, i in ((1, 0, has_e, nk), (-1, nk - 1, has_w, nk + 1)):
            send(
                down_s.at[i], edge_r.at[slot : slot + ROWS], f"edge{slot}{dx}",
                at(dg, dx, kk), far & has & has_x,
            )
    for dx, kk, has_x, i in ((1, 0, has_e, nk), (-1, nk - 1, has_w, nk + 1)):
        send(
            down_s.at[i], edge_r.at[pl.ds(mine, ROWS)], f"edge{dx}", at(0, dx, kk), has_x
        )

    chunks = ((0, 0, nz), (1, 0, cut_z), (1, cut_z, nz))

    def send_soil(c):
        ph, a, b = chunks[c]
        send(row_s.at[ph, 1, :, :, a:b], row_r.at[ph, 0, :, :, a:b], f"row{c}d", down, has_d)
        send(row_s.at[ph, 0, :, :, a:b], row_r.at[ph, 1, :, :, a:b], f"row{c}u", up, has_u)
        send(col_s.at[c, 1], col_r.at[c, 0], f"col{c}e", at(0, 1, k), has_e)
        send(col_s.at[c, 0], col_r.at[c, 1], f"col{c}w", at(0, -1, k), has_w)

    def wait_soil(c):
        ph, a, b = chunks[c]
        drain(row_r.at[ph, 0, :, :, a:b], f"row{c}d_r", has_u)
        drain(row_r.at[ph, 1, :, :, a:b], f"row{c}u_r", has_d)
        drain(col_r.at[c, 0], f"col{c}e_r", has_w)
        drain(col_r.at[c, 1], f"col{c}w_r", has_e)

    send_soil(0)

    def own(a, b):
        return field.at[:, a:b, 0:TILE]

    send(own(24, 32), own(40, 48), "right", {"grp": g, **right}, has_r)
    send(own(0, 8), own(32, 40), "left", {"grp": g, **left}, has_l)
    for dg, has, ref, n in ((1, has_s, above, "s"), (-1, has_n, below, "n")):
        send(own(0, 32), ref.at[:, 0:32], "line" + n, at(dg, 0, k), has)
        send(own(24, 32), ref.at[:, 40:48], "right" + n, {"grp": g + dg, **right}, has & has_r)
        send(own(0, 8), ref.at[:, 32:40], "left" + n, {"grp": g + dg, **left}, has & has_l)

    def sums(ph, z, t, halo_rows, halo_cols):
        both = []
        for i, ref in enumerate((root, flow)):
            mid = ref[ph, z + 1, :, tile(t)]
            total = ref[ph, z, :, tile(t)] + ref[ph, z + 2, :, tile(t)]
            above_row, below_row = halo_rows[0][i], halo_rows[1][i]
            total += jnp.where(sub == 0, above_row, pltpu.roll(mid, 1, 0))
            total += jnp.where(sub == ROWS - 1, below_row, pltpu.roll(mid, ROWS - 1, 0))
            if t > 0:
                west = pltpu.roll(ref[ph, z + 1, :, tile(t - 1)], 1, 1)
            else:
                west = halo_cols[0][i]
            if t + 1 < tiles:
                east = pltpu.roll(ref[ph, z + 1, :, tile(t + 1)], TILE - 1, 1)
            else:
                east = halo_cols[1][i]
            total += jnp.where(lane == 0, west, pltpu.roll(mid, 1, 1))
            total += jnp.where(lane == TILE - 1, east, pltpu.roll(mid, TILE - 1, 1))
            both.append(total)
        q, r = both
        r += GRAVITY_STEP * (root[ph, z, :, tile(t)] - root[ph, z + 2, :, tile(t)])
        return q, r

    def plain_halo(c, z):
        ph = chunks[c][0]

        def rows(t):
            return [
                [row_r[ph, d, i, t, pl.ds(z, 1), :] for i in range(2)] for d in range(2)
            ]

        cols = [
            [shift_to(col_r[c, d], z + 64 * i, (TILE - 1) * d) for i in range(2)]
            for d in range(2)
        ]
        return rows, cols

    def sweep_parts(ph, z, t, halo, base, weight):
        rows, cols = halo
        q, r = sums(ph, z, t, rows(t), cols)
        own_root = root[ph, z + 1, :, tile(t)]
        return base + own_root * r, weight + own_root * q

    def sweep(ph, z, t, halo, base, weight):
        above_line, below_line = sweep_parts(ph, z, t, halo, base, weight)
        return above_line / below_line

    def keep(z, t, head, params):
        c, se, q = closures(head, params)
        gap = params[4] * (se - sat[z, :, tile(t)])
        cap[z, :, tile(t)] = c
        num[z, :, tile(t)] = c * head - gap
        r = q * head
        root[1, z + 1, :, tile(t)] = q
        flow[1, z + 1, :, tile(t)] = r
        return q, r

    def second_closures(z, packs):
        halo = plain_halo(0, z)
        heads = []
        for t in range(tiles):
            c0 = cap[z, :, tile(t)]
            heads.append(sweep(0, z, t, halo, c0 * p[z, :, tile(t)], c0))
        ends = []
        for t in range(tiles):
            q, r = keep(z, t, heads[t], [par[i, z, :, tile(t)] for i in range(PARAMS)])
            put_row(row_s.at[1, 0], row_s.at[1, 1], 0, z, t, q)
            put_row(row_s.at[1, 0], row_s.at[1, 1], 1, z, t, r)
            ends.append((q, r))
        return put_cols(packs, z, *ends[0], *ends[-1])

    for t in range(tiles):
        for d in range(2):
            top_s[d, :, tile(t)] = zero
            for i in range(2):
                row_s[1, d, i, t, 0:ROWS, :] = zero
    wait_soil(0)

    halo = plain_halo(0, 0)
    west, east = zero, zero
    for t in range(tiles):
        c0 = cap[0, :, tile(t)]
        upper, lower = sweep_parts(0, 0, t, halo, c0 * p[0, :, tile(t)], c0)
        num[0, :, tile(t)] = upper
        cap[0, :, tile(t)] = lower
        for i, v in enumerate([upper, lower] + [par[j, 0, :, tile(t)] for j in (0, 1, 2, 5)]):
            top_s[0, i : i + 1, tile(t)] = v[0:1, :]
            top_s[1, i : i + 1, tile(t)] = v[ROWS - 1 : ROWS, :]
            if t == 0:
                west = jnp.where(lane == i, turn(v, i), west)
            if t == tiles - 1:
                east = jnp.where(lane == i, turn(v, i + 1), east)
    tcol_s[0], tcol_s[1] = west, east
    send(top_s.at[1], top_r.at[0], "topd", down, has_d)
    send(top_s.at[0], top_r.at[1], "topu", up, has_u)
    send(tcol_s.at[1], tcol_r.at[0], "tope", at(0, 1, k), has_e)
    send(tcol_s.at[0], tcol_r.at[1], "topw", at(0, -1, k), has_w)

    packs = lax.fori_loop(1, cut_z, second_closures, (zero, zero))
    col_s[1, 0], col_s[1, 1] = packs
    send_soil(1)

    drain(own(40, 48), "right_r", has_l)
    drain(own(32, 40), "left_r", has_r)
    for has, ref, n in ((has_n, above, "s"), (has_s, below, "n")):
        drain(ref.at[:, 0:32], "line" + n + "_r", has)
        drain(ref.at[:, 40:48], "right" + n + "_r", has & has_l)
        drain(ref.at[:, 32:40], "left" + n + "_r", has & has_r)
    side = lax.broadcasted_iota(jnp.int32, (48, TILE), 1) < 64
    full = []
    for f in range(FIELDS):
        full.append(
            jnp.concatenate(
                [field[f, :, 0:TILE], jnp.where(side, below[f], above[f])], axis=1
            )
        )
    w0, level, bed, rain, land = full

    def next_of(v, axis):
        return pltpu.roll(v, v.shape[axis] - 1, axis)

    def prev_of(v, axis):
        return pltpu.roll(v, 1, axis)

    faces = [bed * next_of(bed, axis) for axis in (0, 1)]

    def outflow(w):
        carried = jnp.exp((5.0 / 3.0) * jnp.log(jnp.maximum(w, 1e-30)))
        surface = level + w
        total = None
        for axis in (0, 1):
            slope = surface - next_of(surface, axis)
            upwind = jnp.where(slope >= 0, carried, next_of(carried, axis))
            flux = faces[axis] * upwind * slope * lax.rsqrt(
                jnp.maximum(jnp.abs(slope), SLOPE_FLOOR)
            )
            net = flux - prev_of(flux, axis)
            total = net if total is None else total + net
        return total

    out0 = outflow(w0)

    drain(down_s.at[0 : nk - 1], "down_r")
    drain(down_s.at[0], "down128_r", has_s)
    drain(down_s.at[0], "down248_r", has_n)
    for dx, gets in ((1, first & has_w), (-1, last & has_e)):
        drain(edge_r.at[0:TILE], f"edge{dx}_r", gets)
        drain(down_s.at[0], f"edge128{dx}_r", gets & has_s)
        drain(down_s.at[0], f"edge248{dx}_r", gets & has_n)

    tall = lax.broadcasted_iota(jnp.int32, (TILE, TILE), 0)
    wide_lane = lax.broadcasted_iota(jnp.int32, (TILE, TILE), 1) & 63
    low = jnp.where(first, 38, 32)
    use_edge = (wide_lane >= low) & (wide_lane < low + 2) & (first | last)

    def received(a):
        rows = jnp.where(use_edge, edge_r[a : a + TILE, :], down_r[a : a + TILE, :])
        if a:
            rows = jnp.where((tall < ROWS) | (tall >= TILE - ROWS), rows, 0.0)
        return rows.T

    main, rim = received(0), received(TILE)

    def pick(a):
        body = [main[a : a + 32], rim[a : a + 32]]
        halo = [main[a + 32 : a + 40], rim[a + 32 : a + 40]]
        body, halo = (jnp.concatenate(v, axis=1) for v in (body, halo))
        return jnp.concatenate([body, halo, halo], axis=0)

    top = pick(0)
    leak = land * pick(64)

    def advance(w, out):
        rate = leak * (w - top)
        return jnp.maximum(w + SURFACE_STEP * (rain - rate - out), 0.0), rate

    w1, rate0 = advance(w0, out0)
    w2, rate1 = advance(w1, outflow(w1))
    rate2 = leak * (w2 - top)
    exchange = SURFACE_STEP * (rate0 + rate1 + rate2)
    body = exchange[0:32]
    square = jnp.concatenate(
        [body[:, 0:TILE]] * 2 + [exchange[32:48, 0:TILE], jnp.zeros((48, TILE), F32)], axis=0
    ).T
    outer = jnp.concatenate([body[:, TILE:]] * 4, axis=0).T
    blocks = [square[ROWS * j : ROWS * (j + 1)] for j in range(nk)]
    blocks = [outer[TILE - ROWS :]] + blocks + [outer[0:ROWS]]
    second = (lane >= 32) & (lane < 64)
    for j in range(nk):
        ends = jnp.where(sub < 4, blocks[j + 2], blocks[j])
        back_s[j] = jnp.where(second, ends, blocks[j + 1])
    back_r[k] = back_s[k]
    ring(
        lambda kk: send(back_s.at[kk], back_r.at[k], "back", at(0, 0, kk), keep=False)
    )
    w3, _ = advance(w2, outflow(w2))
    water_out[...] = w3[0:32, 0:TILE]

    packs = lax.fori_loop(cut_z, nz, second_closures, (zero, zero))
    col_s[2, 0], col_s[2, 1] = packs
    send_soil(2)

    def last_sweep(z, halo):
        for t in range(tiles):
            head_out[z, :, tile(t)] = sweep(1, z, t, halo, num[z, :, tile(t)], cap[z, :, tile(t)])

    def last_step(c):
        def step(z, carry):
            last_sweep(z, plain_halo(c, z))
            return carry

        return step

    wait_soil(1)
    lax.fori_loop(2, cut_z - 1, last_step(1), 0)
    last_sweep(cut_z - 1, plain_halo(1, cut_z - 1))
    wait_soil(2)
    lax.fori_loop(cut_z, nz, last_step(2), 0)
    drain(top_r.at[0], "topd_r", has_u)
    drain(top_r.at[1], "topu_r", has_d)
    drain(tcol_r.at[0], "tope_r", has_w)
    drain(tcol_r.at[1], "topw_r", has_e)

    drain(down_s.at[0 : nk - 1], "back_r")

    def gathered(t, group):
        v = turn(back_r[per * t], -32 * group)
        for i in range(1, per):
            v = jnp.where(lane >= 32 * i, turn(back_r[per * t + i], 32 * (i - group)), v)
        return v

    def beside(parts, gain):
        upper, lower, entry, expo, pore, scale = parts
        head = (upper + gain) / jnp.maximum(lower, 1e-6)
        _, _, q = closures(head, (entry, expo, pore, 0.0, None, scale))
        return q, q * head

    extras, rows_beside = [], []
    for t in range(tiles):
        extras.append(gathered(t, 0))
        parts = [
            jnp.where(sub < 4, top_r[1, i : i + 1, tile(t)], top_r[0, i : i + 1, tile(t)])
            for i in range(6)
        ]
        rows_beside.append(beside(parts, gathered(t, 1)))
    parts = [
        jnp.where(lane < 64, turn(tcol_r[0], -i), turn(tcol_r[1], TILE - 1 - i)) for i in range(6)
    ]
    gain = jnp.where(lane < 64, turn(back_r[0], TILE - 79), turn(back_r[nk - 1], TILE - 1 - 64))
    ends = beside(parts, gain)
    for t in range(tiles):
        head = (num[0, :, tile(t)] + extras[t]) / cap[0, :, tile(t)]
        keep(0, t, head, [par[i, 0, :, tile(t)] for i in range(PARAMS)])
        num[0, :, tile(t)] += extras[t]

    def top_rows(t):
        return [[v[7:8, :] for v in rows_beside[t]], [v[0:1, :] for v in rows_beside[t]]]

    last_sweep(0, (top_rows, [ends, ends]))
    last_sweep(1, plain_halo(1, 1))

    drain(down_s.at[0 : nk - 1], "down_s")
    drain(down_s.at[0 : nk - 1], "back_s")
    drain(down_s.at[0:nk], "down248_s", last & has_s)
    drain(down_s.at[0:nk], "down128_s", first & has_n)
    for copy, when in pending:
        if when is None:
            copy.wait_send()
        else:
            pl.when(when)(copy.wait_send)


def solution(mesh):
    sizes = tuple(mesh.shape[a] for a in ("grp", "gx", "gy"))
    nk = sizes[2]

    def local(
        pressure, soil_class, capacity_range, inverse_entry, shape_index, conductivity,
        depth, elevation, roughness, rain, land_mask, channel_mask,
    ):
        nz, _, wide = pressure.shape
        kinds = capacity_range.shape[0]
        hbm = pl.BlockSpec(memory_space=pl.ANY)
        soil = (nz, ROWS, wide)
        vmem = pltpu.VMEM
        head, water = pl.pallas_call(
            functools.partial(kernel, nz, wide, kinds, sizes, 16),
            out_shape=(
                vmem(pressure.shape, F32),
                vmem(depth.shape[::-1], F32),
            ),
            in_specs=[hbm] * 12,
            out_specs=(pl.BlockSpec(memory_space=vmem),) * 2,
            scratch_shapes=[
                pltpu.SMEM((4, kinds), F32),
                vmem(soil, F32),
                vmem(soil, jnp.int32),
                vmem((PARAMS, *soil), F32),
                vmem(soil, F32),
                vmem(soil, F32),
                vmem((2, nz + 2, ROWS, wide), F32),
                vmem((2, nz + 2, ROWS, wide), F32),
                vmem(soil, F32),
                vmem((2, 2, 2, wide // TILE, nz, TILE), F32),
                vmem((2, 2, 2, wide // TILE, nz, TILE), F32),
                vmem((2, ROWS, wide), F32),
                vmem((2, ROWS, wide), F32),
                vmem((3, 2, ROWS, TILE), F32),
                vmem((3, 2, ROWS, TILE), F32),
                vmem((2, ROWS, TILE), F32),
                vmem((2, ROWS, TILE), F32),
                vmem((4, 32, TILE), F32),
                vmem((FIELDS, 48, 2 * TILE), F32),
                vmem((FIELDS, 48, TILE), F32),
                vmem((FIELDS, 48, TILE), F32),
                vmem((nk + 2, ROWS, TILE), F32),
                vmem((2 * TILE, TILE), F32),
                vmem((2 * TILE, TILE), F32),
                vmem((nk, ROWS, TILE), F32),
                vmem((nk, ROWS, TILE), F32),
                vmem((2, 32, TILE), jnp.int32),
                pltpu.SemaphoreType.DMA((100,)),
            ],
            compiler_params=pltpu.CompilerParams(
                collective_id=0, has_side_effects=True, vmem_limit_bytes=60 * 1024 * 1024
            ),
        )(
            pressure, soil_class, capacity_range, inverse_entry, shape_index, conductivity,
            depth.T, elevation.T, roughness.T, rain.T, land_mask.T, channel_mask.T,
        )
        return head, water.T

    tile = P(None, ("grp", "gy"), "gx")
    flat = P("grp", ("gx", "gy"))
    return jax.shard_map(
        local,
        mesh=mesh,
        in_specs=(tile, tile, P(), P(), P(), P()) + (flat,) * 6,
        out_specs=(tile, flat),
        check_vma=False,
    )
```

```python
import functools

import jax
import jax.numpy as jnp
from jax import lax
from jax.experimental import pallas as pl
from jax.experimental.pallas import tpu as pltpu
from jax.sharding import PartitionSpec as P

MESH = pl.DeviceIdType.MESH
F32 = jnp.float32

STORAGE = 0.01
GRAVITY_STEP = 0.5
SUCTION_FLOOR = 0.01
SLOPE_FLOOR = 0.1
SURFACE_STEP = 0.3
LEAKANCE = 0.5

TILE = 128
ROWS = 8
FIELDS = 5
PARAMS = 6


def lanes():
    return lax.broadcasted_iota(jnp.int32, (ROWS, TILE), 1)


def sublanes():
    return lax.broadcasted_iota(jnp.int32, (ROWS, TILE), 0)


def gather(table, index):
    return jnp.take_along_axis(table, index, axis=1, mode="promise_in_bounds")


def build_tables(tab, kinds):
    lane = lanes()
    rows = []
    for i in range(4):
        row = jnp.zeros((ROWS, TILE), F32)
        for kind in range(kinds):
            row = jnp.where(lane == kind, tab[i, kind], row)
        rows.append(row)
    span, entry, shape, conduct = rows
    shape = jnp.where(lane < kinds, shape, 2.0)
    pore = 1.0 - 1.0 / shape
    expo = 1.0 / (1.0 - pore)
    return (
        -entry,
        expo,
        pore,
        span * pore * expo * entry,
        span,
        2.0 * jnp.sqrt(conduct),
    )


def closures(p, params):
    entry, expo, pore, lead, _, scale = params
    log_scaled = jnp.log(jnp.maximum(entry * p, SUCTION_FLOOR))
    up = expo * log_scaled
    log_sum = jnp.log(1.0 + jnp.exp(up))
    drop = pore * log_sum
    wet = pore * up - drop
    held = jnp.exp(wet)
    capacity = STORAGE + lead * jnp.exp(wet - log_sum)
    fourth = jnp.exp(-0.25 * drop)
    half = fourth * fourth
    root = scale * fourth * (1.0 - held)
    return capacity, half * half, root


def kernel(
    nz, wide, kinds, sizes, cut_z,
    p_in, k_in, t0_in, t1_in, t2_in, t3_in,
    s0_in, s1_in, s2_in, s3_in, s4_in, s5_in,
    head_out, water_out,
    tab, p, kind, par, cap, sat, root, flow, num,
    row_s, row_r, top_s, top_r, col_s, col_r, tcol_s, tcol_r,
    surf_in, field, below, above,
    down_s, down_r, edge_r, back_s, back_r, water,
    sem,
):
    ng, nx, nk = sizes
    tiles = wide // TILE
    per = TILE // 32
    g, x, k = (lax.axis_index(a) for a in ("grp", "gx", "gy"))
    lane, sub = lanes(), sublanes()
    first, last = k == 0, k == nk - 1
    has_n, has_s = g > 0, g < ng - 1
    has_w, has_e = x > 0, x < nx - 1

    names = {}

    def s(name):
        return sem.at[names.setdefault(name, len(names))]

    def at(dg, dx, kk):
        return {"grp": g + dg, "gx": x + dx, "gy": kk}

    def tile(t):
        return slice(t * TILE, (t + 1) * TILE)

    def load(src, dst, name):
        copy = pltpu.make_async_copy(src, dst, s(name))
        copy.start()
        return copy

    barrier = pltpu.get_barrier_semaphore()

    def greet(device):
        pl.semaphore_signal(barrier, 1, device_id=device, device_id_type=MESH)

    def ring(body):
        for away in sorted(range(1, nk), key=lambda d: -min(d, nk - d)):
            body(jnp.where(k + away >= nk, k + away - nk, k + away))

    def every(body):
        def step(i, _):
            body(i)
            return 0

        lax.fori_loop(0, nk, step, 0)

    col = x * nk + k
    has_l, has_r = col > 0, col < nx * nk - 1
    left = {"gx": jnp.maximum(col - 1, 0) // nk, "gy": lax.rem(jnp.maximum(col - 1, 0), nk)}
    right = {"gx": (col + 1) // nk, "gy": lax.rem(col + 1, nk)}
    row = g * nk + k
    has_u, has_d = row > 0, row < ng * nk - 1
    up = {"grp": jnp.maximum(row - 1, 0) // nk, "gx": x, "gy": lax.rem(jnp.maximum(row - 1, 0), nk)}
    down = {"grp": (row + 1) // nk, "gx": x, "gy": lax.rem(row + 1, nk)}

    @pl.when(has_w)
    def _():
        @pl.when(first)
        def _():
            every(lambda kk: greet(at(0, -1, kk)))

        greet(at(0, -1, k))

    @pl.when(has_e)
    def _():
        @pl.when(last)
        def _():
            every(lambda kk: greet(at(0, 1, kk)))

        greet(at(0, 1, k))

    for dg, has in ((-1, has_n), (1, has_s)):
        far = nk - 1 if dg < 0 else 0

        @pl.when(has)
        def _():
            greet(at(dg, 0, far))
            greet(at(dg, 0, k))

            @pl.when(has_l)
            def _():
                greet({"grp": g + dg, **left})

            @pl.when(has_r)
            def _():
                greet({"grp": g + dg, **right})

            @pl.when(first & has_w)
            def _():
                greet(at(dg, -1, far))

            @pl.when(last & has_e)
            def _():
                greet(at(dg, 1, far))

    ring(lambda kk: greet(at(0, 0, kk)))

    table_loads = [
        load(ref, tab.at[i], f"tab{i}")
        for i, ref in enumerate((t0_in, t1_in, t2_in, t3_in))
    ]
    top_loads = [
        load(p_in.at[0:1], p.at[0:1], "p0"),
        load(k_in.at[0:1], kind.at[0:1], "k0"),
    ]
    surf_loads = [
        load(s0_in, surf_in.at[0], "s0"),
        load(s1_in, surf_in.at[1], "s1"),
        load(s2_in, surf_in.at[2], "s2"),
        load(s3_in, surf_in.at[3], "s3"),
    ]
    mask_loads = [
        load(s4_in, water.at[0], "s4"),
        load(s5_in, water.at[1], "s5"),
    ]
    rest_loads = [
        load(p_in.at[1:nz], p.at[1:nz], "p1"),
        load(k_in.at[1:nz], kind.at[1:nz], "k1"),
    ]

    def one(flag):
        return flag.astype(jnp.int32)

    rows_to = one(has_n) + one(has_s)
    cols_to = one(has_w) + one(has_e)
    corner = one(first & has_n) + one(last & has_s)
    expected = (
        (nk - 1)
        + corner * nk
        + rows_to * (1 + one(has_l) + one(has_r))
        + 2 * cols_to
        + corner * cols_to
    )

    zero = jnp.zeros((ROWS, TILE), F32)
    for j in range(nk):
        back_r[j] = zero

    def clear(ref, rows):
        for r in range(0, rows, ROWS):
            for c in range(0, ref.shape[-1], TILE):
                ref[r : r + ROWS, c : c + TILE] = zero

    for t in range(tiles):
        for ph in range(2):
            for z in (0, nz + 1):
                root[ph, z, :, tile(t)] = zero
                flow[ph, z, :, tile(t)] = zero

    for d, has, has_g, ref in ((0, has_u, has_n, above), (1, has_d, has_s, below)):

        @pl.when(jnp.logical_not(has))
        def _():
            for ph in range(2):
                for i in range(2):
                    for t in range(tiles):
                        clear(row_r.at[ph, d, i, t], nz)
            clear(top_r.at[d], ROWS)

        @pl.when(jnp.logical_not(has_g))
        def _():
            for f in range(FIELDS):
                clear(ref.at[f], 48)
            off = 248 if d == 0 else 128
            clear(down_r.at[off : off + ROWS], ROWS)

        @pl.when(has_g & jnp.logical_not(has_r))
        def _():
            for f in range(FIELDS):
                ref[f, 32:40, :] = zero

        @pl.when(has_g & jnp.logical_not(has_l))
        def _():
            for f in range(FIELDS):
                ref[f, 40:48, :] = zero

    for d, has in ((0, has_w), (1, has_e)):

        @pl.when(jnp.logical_not(has))
        def _():
            for c in range(3):
                col_r[c, d] = zero
            tcol_r[d] = zero

    for d, has in ((0, has_r), (1, has_l)):

        @pl.when(jnp.logical_not(has))
        def _():
            for f in range(FIELDS):
                field[f, 32 + 8 * d : 40 + 8 * d, 0:TILE] = zero

    gets_edge = (first & has_w) | (last & has_e)

    @pl.when(jnp.logical_not(gets_edge))
    def _():
        clear(edge_r.at[0:TILE], TILE)

    for off, has in ((128, has_s), (248, has_n)):

        @pl.when(jnp.logical_not(gets_edge & has))
        def _():
            clear(edge_r.at[off : off + ROWS], ROWS)

    for c in table_loads:
        c.wait()
    tables = build_tables(tab, kinds)

    def layer_params(z, t):
        index = kind[z, :, tile(t)]
        return [gather(table, index) for table in tables]

    def put_row(dst_first, dst_last, i, z, t, value):
        dst_first[i, t, pl.ds(z, 1), :] = value[0:1, :]
        dst_last[i, t, pl.ds(z, 1), :] = value[7:8, :]

    def shift_to(value, frm, to):
        return pltpu.roll(value, lax.rem(to - frm + TILE, TILE), 1)

    def put_cols(packs, z, q0, r0, q1, r1):
        west, east = packs
        west = jnp.where(lane == z, shift_to(q0, 0, z), west)
        west = jnp.where(lane == z + 64, shift_to(r0, 0, z + 64), west)
        east = jnp.where(lane == z, shift_to(q1, TILE - 1, z), east)
        east = jnp.where(lane == z + 64, shift_to(r1, TILE - 1, z + 64), east)
        return west, east

    def first_closures(z, packs):
        ends = []
        for t in range(tiles):
            params = layer_params(z, t)
            for i in range(PARAMS):
                par[i, z, :, tile(t)] = params[i]
            pz = p[z, :, tile(t)]
            c, se, q = closures(pz, params)
            r = q * pz
            cap[z, :, tile(t)] = c
            sat[z, :, tile(t)] = se
            root[0, z + 1, :, tile(t)] = q
            flow[0, z + 1, :, tile(t)] = r
            put_row(row_s.at[0, 0], row_s.at[0, 1], 0, z, t, q)
            put_row(row_s.at[0, 0], row_s.at[0, 1], 1, z, t, r)
            ends.append((q, r))
        return put_cols(packs, z, *ends[0], *ends[-1])

    for c in top_loads:
        c.wait()
    packs = first_closures(0, (zero, zero))

    tops = [p[0, :, tile(t)] for t in range(tiles)]
    halves = [jnp.square(root[0, 1, :, tile(t)]) * 0.125 for t in range(tiles)]

    def turn(v, by):
        by %= TILE
        return pltpu.roll(v, by, 1) if by else v

    def cut(parts, kk, base):
        t, o = divmod(kk * 32, TILE)
        out = turn(parts[t], base - o)
        before = parts[t] if o else parts[max(t - 1, 0)]
        out = jnp.where(
            (lane >= base + 38) & (lane < base + 40), turn(before, base + 40 - o), out
        )
        if o + 32 == TILE and t + 1 < tiles:
            after = turn(parts[t + 1], base + 32)
            out = jnp.where((lane >= base + 32) & (lane < base + 34), after, out)
        return out

    for kk in range(nk):
        down_s[kk] = jnp.where(lane < 64, cut(tops, kk, 0), cut(halves, kk, 64))
    down_s[nk] = jnp.where(lane < 64, turn(tops[-1], 40), turn(halves[-1], 104))
    down_s[nk + 1] = jnp.where(lane < 64, turn(tops[0], 32), turn(halves[0], 96))
    mine = pl.multiple_of(k * ROWS, ROWS)
    down_r[pl.ds(mine, ROWS), :] = down_s[k]

    pending = []

    def send(src, dst, name, device, when=None, keep=True):
        copy = pltpu.make_async_remote_copy(
            src_ref=src,
            dst_ref=dst,
            send_sem=s(name + "_s"),
            recv_sem=s(name + "_r"),
            device_id=device,
            device_id_type=MESH,
        )
        if when is None:
            copy.start()
        else:
            pl.when(when)(copy.start)
        if keep:
            pending.append((copy, when))
        return copy

    def drain(ref, name, when=None):
        wait = pltpu.make_async_copy(ref, ref, s(name)).wait
        if when is None:
            wait()
        else:
            pl.when(when)(wait)

    for c in surf_loads + mask_loads:
        c.wait()
    field[0, 0:32, 0:TILE] = surf_in[0]
    field[1, 0:32, 0:TILE] = surf_in[1]
    field[2, 0:32, 0:TILE] = jnp.sqrt((1.0 + water[1].astype(F32)) / surf_in[2])
    field[3, 0:32, 0:TILE] = surf_in[3]
    field[4, 0:32, 0:TILE] = water[0].astype(F32)

    for c in rest_loads:
        c.wait()
    packs = lax.fori_loop(1, nz, first_closures, packs)
    col_s[0, 0], col_s[0, 1] = packs

    pl.semaphore_wait(barrier, expected)
    for dx, kk, has_x, i in ((1, 0, has_e, nk), (-1, nk - 1, has_w, nk + 1)):
        send(
            down_s.at[i], edge_r.at[pl.ds(mine, ROWS)], f"edge{dx}", at(0, dx, kk), has_x
        )
    for dg, far, has, slot in ((1, last, has_s, 248), (-1, first, has_n, 128)):

        @pl.when(far & has)
        def _():
            every(
                lambda kk: send(
                    down_s.at[kk], down_r.at[slot : slot + ROWS], f"down{slot}", at(dg, 0, kk),
                    keep=False,
                )
            )

        for dx, kk, has_x, i in ((1, 0, has_e, nk), (-1, nk - 1, has_w, nk + 1)):
            send(
                down_s.at[i], edge_r.at[slot : slot + ROWS], f"edge{slot}{dx}",
                at(dg, dx, kk), far & has & has_x,
            )
    ring(
        lambda kk: send(
            down_s.at[kk], down_r.at[pl.ds(mine, ROWS)], "down", at(0, 0, kk), keep=False
        )
    )
    chunks = ((0, 0, nz), (1, 0, cut_z), (1, cut_z, nz))

    def send_soil(c):
        ph, a, b = chunks[c]
        send(row_s.at[ph, 1, :, :, a:b], row_r.at[ph, 0, :, :, a:b], f"row{c}d", down, has_d)
        send(row_s.at[ph, 0, :, :, a:b], row_r.at[ph, 1, :, :, a:b], f"row{c}u", up, has_u)
        send(col_s.at[c, 1], col_r.at[c, 0], f"col{c}e", at(0, 1, k), has_e)
        send(col_s.at[c, 0], col_r.at[c, 1], f"col{c}w", at(0, -1, k), has_w)

    def wait_soil(c):
        ph, a, b = chunks[c]
        drain(row_r.at[ph, 0, :, :, a:b], f"row{c}d_r", has_u)
        drain(row_r.at[ph, 1, :, :, a:b], f"row{c}u_r", has_d)
        drain(col_r.at[c, 0], f"col{c}e_r", has_w)
        drain(col_r.at[c, 1], f"col{c}w_r", has_e)

    send_soil(0)

    def own(a, b):
        return field.at[:, a:b, 0:TILE]

    send(own(24, 32), own(40, 48), "right", {"grp": g, **right}, has_r)
    send(own(0, 8), own(32, 40), "left", {"grp": g, **left}, has_l)
    for dg, has, ref, n in ((1, has_s, above, "s"), (-1, has_n, below, "n")):
        send(own(0, 32), ref.at[:, 0:32], "line" + n, at(dg, 0, k), has)
        send(own(24, 32), ref.at[:, 40:48], "right" + n, {"grp": g + dg, **right}, has & has_r)
        send(own(0, 8), ref.at[:, 32:40], "left" + n, {"grp": g + dg, **left}, has & has_l)

    def sums(ph, z, t, halo_rows, halo_cols):
        both = []
        for i, ref in enumerate((root, flow)):
            mid = ref[ph, z + 1, :, tile(t)]
            total = ref[ph, z, :, tile(t)] + ref[ph, z + 2, :, tile(t)]
            above_row, below_row = halo_rows[0][i], halo_rows[1][i]
            total += jnp.where(sub == 0, above_row, pltpu.roll(mid, 1, 0))
            total += jnp.where(sub == ROWS - 1, below_row, pltpu.roll(mid, ROWS - 1, 0))
            if t > 0:
                west = pltpu.roll(ref[ph, z + 1, :, tile(t - 1)], 1, 1)
            else:
                west = halo_cols[0][i]
            if t + 1 < tiles:
                east = pltpu.roll(ref[ph, z + 1, :, tile(t + 1)], TILE - 1, 1)
            else:
                east = halo_cols[1][i]
            total += jnp.where(lane == 0, west, pltpu.roll(mid, 1, 1))
            total += jnp.where(lane == TILE - 1, east, pltpu.roll(mid, TILE - 1, 1))
            both.append(total)
        q, r = both
        r += GRAVITY_STEP * (root[ph, z, :, tile(t)] - root[ph, z + 2, :, tile(t)])
        return q, r

    def plain_halo(c, z):
        ph = chunks[c][0]

        def rows(t):
            return [
                [row_r[ph, d, i, t, pl.ds(z, 1), :] for i in range(2)] for d in range(2)
            ]

        cols = [
            [shift_to(col_r[c, d], z + 64 * i, (TILE - 1) * d) for i in range(2)]
            for d in range(2)
        ]
        return rows, cols

    def sweep_parts(ph, z, t, halo, base, weight):
        rows, cols = halo
        q, r = sums(ph, z, t, rows(t), cols)
        own_root = root[ph, z + 1, :, tile(t)]
        return base + own_root * r, weight + own_root * q

    def sweep(ph, z, t, halo, base, weight):
        above_line, below_line = sweep_parts(ph, z, t, halo, base, weight)
        return above_line / below_line

    def keep(z, t, head, params):
        c, se, q = closures(head, params)
        gap = params[4] * (se - sat[z, :, tile(t)])
        cap[z, :, tile(t)] = c
        num[z, :, tile(t)] = c * head - gap
        r = q * head
        root[1, z + 1, :, tile(t)] = q
        flow[1, z + 1, :, tile(t)] = r
        return q, r

    def second_closures(z, packs):
        halo = plain_halo(0, z)
        heads = []
        for t in range(tiles):
            c0 = cap[z, :, tile(t)]
            heads.append(sweep(0, z, t, halo, c0 * p[z, :, tile(t)], c0))
        ends = []
        for t in range(tiles):
            q, r = keep(z, t, heads[t], [par[i, z, :, tile(t)] for i in range(PARAMS)])
            put_row(row_s.at[1, 0], row_s.at[1, 1], 0, z, t, q)
            put_row(row_s.at[1, 0], row_s.at[1, 1], 1, z, t, r)
            ends.append((q, r))
        return put_cols(packs, z, *ends[0], *ends[-1])

    for t in range(tiles):
        for d in range(2):
            top_s[d, :, tile(t)] = zero
            for i in range(2):
                row_s[1, d, i, t, 0:ROWS, :] = zero
    wait_soil(0)

    halo = plain_halo(0, 0)
    west, east = zero, zero
    for t in range(tiles):
        c0 = cap[0, :, tile(t)]
        upper, lower = sweep_parts(0, 0, t, halo, c0 * p[0, :, tile(t)], c0)
        num[0, :, tile(t)] = upper
        cap[0, :, tile(t)] = lower
        for i, v in enumerate([upper, lower] + [par[j, 0, :, tile(t)] for j in (0, 1, 2, 5)]):
            top_s[0, i : i + 1, tile(t)] = v[0:1, :]
            top_s[1, i : i + 1, tile(t)] = v[ROWS - 1 : ROWS, :]
            if t == 0:
                west = jnp.where(lane == i, turn(v, i), west)
            if t == tiles - 1:
                east = jnp.where(lane == i, turn(v, i + 1), east)
    tcol_s[0], tcol_s[1] = west, east
    send(top_s.at[1], top_r.at[0], "topd", down, has_d)
    send(top_s.at[0], top_r.at[1], "topu", up, has_u)
    send(tcol_s.at[1], tcol_r.at[0], "tope", at(0, 1, k), has_e)
    send(tcol_s.at[0], tcol_r.at[1], "topw", at(0, -1, k), has_w)

    packs = lax.fori_loop(1, cut_z, second_closures, (zero, zero))
    col_s[1, 0], col_s[1, 1] = packs

    drain(own(40, 48), "right_r", has_l)
    drain(own(32, 40), "left_r", has_r)
    for has, ref, n in ((has_n, above, "s"), (has_s, below, "n")):
        drain(ref.at[:, 0:32], "line" + n + "_r", has)
        drain(ref.at[:, 40:48], "right" + n + "_r", has & has_l)
        drain(ref.at[:, 32:40], "left" + n + "_r", has & has_r)
    side = lax.broadcasted_iota(jnp.int32, (48, TILE), 1) < 64
    full = []
    for f in range(FIELDS):
        full.append(
            jnp.concatenate(
                [field[f, :, 0:TILE], jnp.where(side, below[f], above[f])], axis=1
            )
        )
    w0, level, bed, rain, land = full

    def next_of(v, axis):
        return pltpu.roll(v, v.shape[axis] - 1, axis)

    def prev_of(v, axis):
        return pltpu.roll(v, 1, axis)

    faces = [bed * next_of(bed, axis) for axis in (0, 1)]

    def outflow(w):
        carried = jnp.exp((5.0 / 3.0) * jnp.log(jnp.maximum(w, 1e-30)))
        surface = level + w
        total = None
        for axis in (0, 1):
            slope = surface - next_of(surface, axis)
            upwind = jnp.where(slope >= 0, carried, next_of(carried, axis))
            flux = faces[axis] * upwind * slope * lax.rsqrt(
                jnp.maximum(jnp.abs(slope), SLOPE_FLOOR)
            )
            net = flux - prev_of(flux, axis)
            total = net if total is None else total + net
        return total

    out0 = outflow(w0)

    drain(down_s.at[0 : nk - 1], "down_r")
    drain(down_s.at[0], "down128_r", has_s)
    drain(down_s.at[0], "down248_r", has_n)
    for dx, gets in ((1, first & has_w), (-1, last & has_e)):
        drain(edge_r.at[0:TILE], f"edge{dx}_r", gets)
        drain(down_s.at[0], f"edge128{dx}_r", gets & has_s)
        drain(down_s.at[0], f"edge248{dx}_r", gets & has_n)

    tall = lax.broadcasted_iota(jnp.int32, (TILE, TILE), 0)
    wide_lane = lax.broadcasted_iota(jnp.int32, (TILE, TILE), 1) & 63
    low = jnp.where(first, 38, 32)
    use_edge = (wide_lane >= low) & (wide_lane < low + 2) & (first | last)

    def received(a):
        rows = jnp.where(use_edge, edge_r[a : a + TILE, :], down_r[a : a + TILE, :])
        if a:
            rows = jnp.where((tall < ROWS) | (tall >= TILE - ROWS), rows, 0.0)
        return rows.T

    main, rim = received(0), received(TILE)

    def pick(a):
        body = [main[a : a + 32], rim[a : a + 32]]
        halo = [main[a + 32 : a + 40], rim[a + 32 : a + 40]]
        body, halo = (jnp.concatenate(v, axis=1) for v in (body, halo))
        return jnp.concatenate([body, halo, halo], axis=0)

    top = pick(0)
    leak = land * pick(64)

    def advance(w, out):
        rate = leak * (w - top)
        return jnp.maximum(w + SURFACE_STEP * (rain - rate - out), 0.0), rate

    w1, rate0 = advance(w0, out0)
    w2, rate1 = advance(w1, outflow(w1))
    rate2 = leak * (w2 - top)
    exchange = SURFACE_STEP * (rate0 + rate1 + rate2)
    body = exchange[0:32]
    mesh_t = [body[:, 0:TILE]] * 3 + [exchange[32:48, 0:TILE]] * 2
    square = jnp.concatenate(mesh_t, axis=0).T
    outer = jnp.concatenate([body[:, TILE:]] * 4, axis=0).T
    blocks = [square[ROWS * j : ROWS * (j + 1)] for j in range(nk)]
    blocks = [outer[TILE - ROWS :]] + blocks + [outer[0:ROWS]]
    folded = [pltpu.roll(v, 4, 0) for v in blocks]
    fold = ((lane >= 32) & (lane < 64)) | (lane >= 112)
    rim = (lane >= 64) & (lane < 96)
    for j in range(nk):
        ends = jnp.where(sub < 2, blocks[j + 2], folded[j])
        back_s[j] = jnp.where(rim, ends, jnp.where(fold, folded[j + 1], blocks[j + 1]))
    back_r[k] = back_s[k]
    ring(
        lambda kk: send(back_s.at[kk, 0:4], back_r.at[k, 0:4], "back", at(0, 0, kk), keep=False)
    )
    send_soil(1)
    w3, _ = advance(w2, outflow(w2))
    water_out[...] = w3[0:32, 0:TILE]

    packs = lax.fori_loop(cut_z, nz, second_closures, (zero, zero))
    col_s[2, 0], col_s[2, 1] = packs
    send_soil(2)

    def last_sweep(z, halo):
        for t in range(tiles):
            head_out[z, :, tile(t)] = sweep(1, z, t, halo, num[z, :, tile(t)], cap[z, :, tile(t)])

    def last_step(c):
        def step(z, carry):
            last_sweep(z, plain_halo(c, z))
            return carry

        return step

    wait_soil(1)
    lax.fori_loop(2, cut_z - 1, last_step(1), 0)
    last_sweep(cut_z - 1, plain_halo(1, cut_z - 1))
    wait_soil(2)
    lax.fori_loop(cut_z, nz, last_step(2), 0)
    drain(top_r.at[0], "topd_r", has_u)
    drain(top_r.at[1], "topu_r", has_d)
    drain(tcol_r.at[0], "tope_r", has_w)
    drain(tcol_r.at[1], "topw_r", has_e)

    drain(down_s.at[0 : nk - 1, 0:4], "back_r")

    def gathered(t, group):
        v = turn(back_r[per * t], -32 * group)
        for i in range(1, per):
            v = jnp.where(lane >= 32 * i, turn(back_r[per * t + i], 32 * (i - group)), v)
        return v

    def unfold(a, b):
        return jnp.where(sub < 4, a, pltpu.roll(b, 4, 0))

    def beside(parts, gain):
        upper, lower, entry, expo, pore, scale = parts
        head = (upper + gain) / jnp.maximum(lower, 1e-6)
        _, _, q = closures(head, (entry, expo, pore, 0.0, None, scale))
        return q, q * head

    extras, rows_beside = [], []
    for t in range(tiles):
        extras.append(unfold(gathered(t, 0), gathered(t, 1)))
        parts = [
            jnp.where(sub < 2, top_r[1, i : i + 1, tile(t)], top_r[0, i : i + 1, tile(t)])
            for i in range(6)
        ]
        rows_beside.append(beside(parts, gathered(t, 2)))
    parts = [
        jnp.where(lane < 64, turn(tcol_r[0], -i), turn(tcol_r[1], TILE - 1 - i)) for i in range(6)
    ]
    west, east = back_r[0], back_r[nk - 1]
    gain = unfold(
        jnp.where(lane < 64, turn(west, -111), turn(east, 31)),
        jnp.where(lane < 64, turn(west, -127), turn(east, 15)),
    )
    ends = beside(parts, gain)
    for t in range(tiles):
        head = (num[0, :, tile(t)] + extras[t]) / cap[0, :, tile(t)]
        keep(0, t, head, [par[i, 0, :, tile(t)] for i in range(PARAMS)])
        num[0, :, tile(t)] += extras[t]

    def top_rows(t):
        return [[v[3:4, :] for v in rows_beside[t]], [v[0:1, :] for v in rows_beside[t]]]

    last_sweep(0, (top_rows, [ends, ends]))
    last_sweep(1, plain_halo(1, 1))

    drain(down_s.at[0 : nk - 1], "down_s")
    drain(down_s.at[0 : nk - 1, 0:4], "back_s")
    drain(down_s.at[0:nk], "down248_s", last & has_s)
    drain(down_s.at[0:nk], "down128_s", first & has_n)
    for copy, when in pending:
        if when is None:
            copy.wait_send()
        else:
            pl.when(when)(copy.wait_send)


def solution(mesh):
    sizes = tuple(mesh.shape[a] for a in ("grp", "gx", "gy"))
    nk = sizes[2]

    def local(
        pressure, soil_class, capacity_range, inverse_entry, shape_index, conductivity,
        depth, elevation, roughness, rain, land_mask, channel_mask,
    ):
        nz, _, wide = pressure.shape
        kinds = capacity_range.shape[0]
        hbm = pl.BlockSpec(memory_space=pl.ANY)
        soil = (nz, ROWS, wide)
        vmem = pltpu.VMEM
        head, water = pl.pallas_call(
            functools.partial(kernel, nz, wide, kinds, sizes, 16),
            out_shape=(
                vmem(pressure.shape, F32),
                vmem(depth.shape[::-1], F32),
            ),
            in_specs=[hbm] * 12,
            out_specs=(pl.BlockSpec(memory_space=vmem),) * 2,
            scratch_shapes=[
                pltpu.SMEM((4, kinds), F32),
                vmem(soil, F32),
                vmem(soil, jnp.int32),
                vmem((PARAMS, *soil), F32),
                vmem(soil, F32),
                vmem(soil, F32),
                vmem((2, nz + 2, ROWS, wide), F32),
                vmem((2, nz + 2, ROWS, wide), F32),
                vmem(soil, F32),
                vmem((2, 2, 2, wide // TILE, nz, TILE), F32),
                vmem((2, 2, 2, wide // TILE, nz, TILE), F32),
                vmem((2, ROWS, wide), F32),
                vmem((2, ROWS, wide), F32),
                vmem((3, 2, ROWS, TILE), F32),
                vmem((3, 2, ROWS, TILE), F32),
                vmem((2, ROWS, TILE), F32),
                vmem((2, ROWS, TILE), F32),
                vmem((4, 32, TILE), F32),
                vmem((FIELDS, 48, 2 * TILE), F32),
                vmem((FIELDS, 48, TILE), F32),
                vmem((FIELDS, 48, TILE), F32),
                vmem((nk + 2, ROWS, TILE), F32),
                vmem((2 * TILE, TILE), F32),
                vmem((2 * TILE, TILE), F32),
                vmem((nk, ROWS, TILE), F32),
                vmem((nk, ROWS, TILE), F32),
                vmem((2, 32, TILE), jnp.int32),
                pltpu.SemaphoreType.DMA((100,)),
            ],
            compiler_params=pltpu.CompilerParams(
                collective_id=0, has_side_effects=True, vmem_limit_bytes=60 * 1024 * 1024
            ),
        )(
            pressure, soil_class, capacity_range, inverse_entry, shape_index, conductivity,
            depth.T, elevation.T, roughness.T, rain.T, land_mask.T, channel_mask.T,
        )
        return head, water.T

    tile = P(None, ("grp", "gy"), "gx")
    flat = P("grp", ("gx", "gy"))
    return jax.shard_map(
        local,
        mesh=mesh,
        in_specs=(tile, tile, P(), P(), P(), P()) + (flat,) * 6,
        out_specs=(tile, flat),
        check_vma=False,
    )
```

```python
import functools

import jax
import jax.numpy as jnp
from jax import lax
from jax.experimental import pallas as pl
from jax.experimental.pallas import tpu as pltpu
from jax.sharding import PartitionSpec as P

MESH = pl.DeviceIdType.MESH
F32 = jnp.float32

STORAGE = 0.01
GRAVITY_STEP = 0.5
SUCTION_FLOOR = 0.01
SLOPE_FLOOR = 0.1
SURFACE_STEP = 0.3
LEAKANCE = 0.5

TILE = 128
ROWS = 8
FIELDS = 5
PARAMS = 6


def lanes():
    return lax.broadcasted_iota(jnp.int32, (ROWS, TILE), 1)


def sublanes():
    return lax.broadcasted_iota(jnp.int32, (ROWS, TILE), 0)


def gather(table, index):
    return jnp.take_along_axis(table, index, axis=1, mode="promise_in_bounds")


def build_tables(tab, kinds):
    lane = lanes()
    rows = []
    for i in range(4):
        row = jnp.zeros((ROWS, TILE), F32)
        for kind in range(kinds):
            row = jnp.where(lane == kind, tab[i, kind], row)
        rows.append(row)
    span, entry, shape, conduct = rows
    shape = jnp.where(lane < kinds, shape, 2.0)
    pore = 1.0 - 1.0 / shape
    expo = 1.0 / (1.0 - pore)
    return (
        -entry,
        expo,
        pore,
        span * pore * expo * entry,
        span,
        2.0 * jnp.sqrt(conduct),
    )


def closures(p, params):
    entry, expo, pore, lead, _, scale = params
    log_scaled = jnp.log(jnp.maximum(entry * p, SUCTION_FLOOR))
    up = expo * log_scaled
    log_sum = jnp.log(1.0 + jnp.exp(up))
    drop = pore * log_sum
    wet = pore * up - drop
    held = jnp.exp(wet)
    capacity = STORAGE + lead * jnp.exp(wet - log_sum)
    fourth = jnp.exp(-0.25 * drop)
    half = fourth * fourth
    root = scale * fourth * (1.0 - held)
    return capacity, half * half, root


def kernel(
    nz, wide, kinds, sizes, cut_z,
    p_in, k_in, t0_in, t1_in, t2_in, t3_in,
    s0_in, s1_in, s2_in, s3_in, s4_in, s5_in,
    head_out, water_out,
    tab, p, kind, par, cap, sat, root, flow, num,
    row_s, row_r, top_s, top_r, col_s, col_r, tcol_s, tcol_r,
    surf_in, field, below, above,
    down_s, down_r, edge_r, back_s, back_r, water,
    sem,
):
    ng, nx, nk = sizes
    tiles = wide // TILE
    per = TILE // 32
    g, x, k = (lax.axis_index(a) for a in ("grp", "gx", "gy"))
    lane, sub = lanes(), sublanes()
    first, last = k == 0, k == nk - 1
    has_n, has_s = g > 0, g < ng - 1
    has_w, has_e = x > 0, x < nx - 1

    names = {}

    def s(name):
        return sem.at[names.setdefault(name, len(names))]

    def at(dg, dx, kk):
        return {"grp": g + dg, "gx": x + dx, "gy": kk}

    def tile(t):
        return slice(t * TILE, (t + 1) * TILE)

    def load(src, dst, name):
        copy = pltpu.make_async_copy(src, dst, s(name))
        copy.start()
        return copy

    barrier = pltpu.get_barrier_semaphore()

    def greet(device):
        pl.semaphore_signal(barrier, 1, device_id=device, device_id_type=MESH)

    def ring(body):
        for away in sorted(range(1, nk), key=lambda d: -min(d, nk - d)):
            body(jnp.where(k + away >= nk, k + away - nk, k + away))

    def every(body):
        def step(i, _):
            body(i)
            return 0

        lax.fori_loop(0, nk, step, 0)

    col = x * nk + k
    has_l, has_r = col > 0, col < nx * nk - 1
    left = {"gx": jnp.maximum(col - 1, 0) // nk, "gy": lax.rem(jnp.maximum(col - 1, 0), nk)}
    right = {"gx": (col + 1) // nk, "gy": lax.rem(col + 1, nk)}
    row = g * nk + k
    has_u, has_d = row > 0, row < ng * nk - 1
    up = {"grp": jnp.maximum(row - 1, 0) // nk, "gx": x, "gy": lax.rem(jnp.maximum(row - 1, 0), nk)}
    down = {"grp": (row + 1) // nk, "gx": x, "gy": lax.rem(row + 1, nk)}

    @pl.when(has_w)
    def _():
        @pl.when(first)
        def _():
            every(lambda kk: greet(at(0, -1, kk)))

        greet(at(0, -1, k))

    @pl.when(has_e)
    def _():
        @pl.when(last)
        def _():
            every(lambda kk: greet(at(0, 1, kk)))

        greet(at(0, 1, k))

    for dg, has in ((-1, has_n), (1, has_s)):
        far = nk - 1 if dg < 0 else 0

        @pl.when(has)
        def _():
            greet(at(dg, 0, far))
            greet(at(dg, 0, k))

            @pl.when(has_l)
            def _():
                greet({"grp": g + dg, **left})

            @pl.when(has_r)
            def _():
                greet({"grp": g + dg, **right})

            @pl.when(first & has_w)
            def _():
                greet(at(dg, -1, far))

            @pl.when(last & has_e)
            def _():
                greet(at(dg, 1, far))

    ring(lambda kk: greet(at(0, 0, kk)))

    table_loads = [
        load(ref, tab.at[i], f"tab{i}")
        for i, ref in enumerate((t0_in, t1_in, t2_in, t3_in))
    ]
    top_loads = [
        load(p_in.at[0:1], p.at[0:1], "p0"),
        load(k_in.at[0:1], kind.at[0:1], "k0"),
    ]
    surf_loads = [
        load(s0_in, surf_in.at[0], "s0"),
        load(s1_in, surf_in.at[1], "s1"),
        load(s2_in, surf_in.at[2], "s2"),
        load(s3_in, surf_in.at[3], "s3"),
    ]
    mask_loads = [
        load(s4_in, water.at[0], "s4"),
        load(s5_in, water.at[1], "s5"),
    ]
    rest_loads = [
        load(p_in.at[1:nz], p.at[1:nz], "p1"),
        load(k_in.at[1:nz], kind.at[1:nz], "k1"),
    ]

    def one(flag):
        return flag.astype(jnp.int32)

    rows_to = one(has_n) + one(has_s)
    cols_to = one(has_w) + one(has_e)
    corner = one(first & has_n) + one(last & has_s)
    expected = (
        (nk - 1)
        + corner * nk
        + rows_to * (1 + one(has_l) + one(has_r))
        + 2 * cols_to
        + corner * cols_to
    )

    zero = jnp.zeros((ROWS, TILE), F32)
    for j in range(nk):
        back_r[j] = zero

    def clear(ref, rows):
        for r in range(0, rows, ROWS):
            for c in range(0, ref.shape[-1], TILE):
                ref[r : r + ROWS, c : c + TILE] = zero

    for t in range(tiles):
        for ph in range(2):
            for z in (0, nz + 1):
                root[ph, z, :, tile(t)] = zero
                flow[ph, z, :, tile(t)] = zero

    for d, has, has_g, ref in ((0, has_u, has_n, above), (1, has_d, has_s, below)):

        @pl.when(jnp.logical_not(has))
        def _():
            for ph in range(2):
                for i in range(2):
                    for t in range(tiles):
                        clear(row_r.at[ph, d, i, t], nz)
            clear(top_r.at[d], ROWS)

        @pl.when(jnp.logical_not(has_g))
        def _():
            for f in range(FIELDS):
                clear(ref.at[f], 48)
            off = 248 if d == 0 else 128
            clear(down_r.at[off : off + ROWS], ROWS)

        @pl.when(has_g & jnp.logical_not(has_r))
        def _():
            for f in range(FIELDS):
                ref[f, 32:40, :] = zero

        @pl.when(has_g & jnp.logical_not(has_l))
        def _():
            for f in range(FIELDS):
                ref[f, 40:48, :] = zero

    for d, has in ((0, has_w), (1, has_e)):

        @pl.when(jnp.logical_not(has))
        def _():
            for c in range(3):
                col_r[c, d] = zero
            tcol_r[d] = zero

    for d, has in ((0, has_r), (1, has_l)):

        @pl.when(jnp.logical_not(has))
        def _():
            for f in range(FIELDS):
                field[f, 32 + 8 * d : 40 + 8 * d, 0:TILE] = zero

    gets_edge = (first & has_w) | (last & has_e)

    @pl.when(jnp.logical_not(gets_edge))
    def _():
        clear(edge_r.at[0:TILE], TILE)

    for off, has in ((128, has_s), (248, has_n)):

        @pl.when(jnp.logical_not(gets_edge & has))
        def _():
            clear(edge_r.at[off : off + ROWS], ROWS)

    for c in table_loads:
        c.wait()
    tables = build_tables(tab, kinds)

    def layer_params(z, t):
        index = kind[z, :, tile(t)]
        return [gather(table, index) for table in tables]

    def put_row(dst_first, dst_last, i, z, t, value):
        dst_first[i, t, pl.ds(z, 1), :] = value[0:1, :]
        dst_last[i, t, pl.ds(z, 1), :] = value[7:8, :]

    def shift_to(value, frm, to):
        return pltpu.roll(value, lax.rem(to - frm + TILE, TILE), 1)

    def put_cols(packs, z, q0, r0, q1, r1):
        west, east = packs
        west = jnp.where(lane == z, shift_to(q0, 0, z), west)
        west = jnp.where(lane == z + 64, shift_to(r0, 0, z + 64), west)
        east = jnp.where(lane == z, shift_to(q1, TILE - 1, z), east)
        east = jnp.where(lane == z + 64, shift_to(r1, TILE - 1, z + 64), east)
        return west, east

    def first_closures(z, packs):
        ends = []
        for t in range(tiles):
            params = layer_params(z, t)
            for i in range(PARAMS):
                par[i, z, :, tile(t)] = params[i]
            pz = p[z, :, tile(t)]
            c, se, q = closures(pz, params)
            r = q * pz
            cap[z, :, tile(t)] = c
            sat[z, :, tile(t)] = se
            root[0, z + 1, :, tile(t)] = q
            flow[0, z + 1, :, tile(t)] = r
            put_row(row_s.at[0, 0], row_s.at[0, 1], 0, z, t, q)
            put_row(row_s.at[0, 0], row_s.at[0, 1], 1, z, t, r)
            ends.append((q, r))
        return put_cols(packs, z, *ends[0], *ends[-1])

    for c in top_loads:
        c.wait()
    packs = first_closures(0, (zero, zero))

    tops = [p[0, :, tile(t)] for t in range(tiles)]
    halves = [jnp.square(root[0, 1, :, tile(t)]) * 0.125 for t in range(tiles)]

    def turn(v, by):
        by %= TILE
        return pltpu.roll(v, by, 1) if by else v

    def cut(parts, kk, base):
        t, o = divmod(kk * 32, TILE)
        out = turn(parts[t], base - o)
        before = parts[t] if o else parts[max(t - 1, 0)]
        out = jnp.where(
            (lane >= base + 38) & (lane < base + 40), turn(before, base + 40 - o), out
        )
        if o + 32 == TILE and t + 1 < tiles:
            after = turn(parts[t + 1], base + 32)
            out = jnp.where((lane >= base + 32) & (lane < base + 34), after, out)
        return out

    for kk in range(nk):
        down_s[kk] = jnp.where(lane < 64, cut(tops, kk, 0), cut(halves, kk, 64))
    down_s[nk] = jnp.where(lane < 64, turn(tops[-1], 40), turn(halves[-1], 104))
    down_s[nk + 1] = jnp.where(lane < 64, turn(tops[0], 32), turn(halves[0], 96))
    mine = pl.multiple_of(k * ROWS, ROWS)
    down_r[pl.ds(mine, ROWS), :] = down_s[k]

    pending = []

    def send(src, dst, name, device, when=None, keep=True):
        copy = pltpu.make_async_remote_copy(
            src_ref=src,
            dst_ref=dst,
            send_sem=s(name + "_s"),
            recv_sem=s(name + "_r"),
            device_id=device,
            device_id_type=MESH,
        )
        if when is None:
            copy.start()
        else:
            pl.when(when)(copy.start)
        if keep:
            pending.append((copy, when))
        return copy

    def drain(ref, name, when=None):
        wait = pltpu.make_async_copy(ref, ref, s(name)).wait
        if when is None:
            wait()
        else:
            pl.when(when)(wait)

    for c in surf_loads + mask_loads:
        c.wait()
    field[0, 0:32, 0:TILE] = surf_in[0]
    field[1, 0:32, 0:TILE] = surf_in[1]
    field[2, 0:32, 0:TILE] = jnp.sqrt((1.0 + water[1].astype(F32)) / surf_in[2])
    field[3, 0:32, 0:TILE] = surf_in[3]
    field[4, 0:32, 0:TILE] = water[0].astype(F32)

    for c in rest_loads:
        c.wait()
    packs = lax.fori_loop(1, nz, first_closures, packs, unroll=4)
    col_s[0, 0], col_s[0, 1] = packs

    pl.semaphore_wait(barrier, expected)
    for dx, kk, has_x, i in ((1, 0, has_e, nk), (-1, nk - 1, has_w, nk + 1)):
        send(
            down_s.at[i], edge_r.at[pl.ds(mine, ROWS)], f"edge{dx}", at(0, dx, kk), has_x
        )
    for dg, far, has, slot in ((1, last, has_s, 248), (-1, first, has_n, 128)):

        @pl.when(far & has)
        def _():
            every(
                lambda kk: send(
                    down_s.at[kk], down_r.at[slot : slot + ROWS], f"down{slot}", at(dg, 0, kk),
                    keep=False,
                )
            )

        for dx, kk, has_x, i in ((1, 0, has_e, nk), (-1, nk - 1, has_w, nk + 1)):
            send(
                down_s.at[i], edge_r.at[slot : slot + ROWS], f"edge{slot}{dx}",
                at(dg, dx, kk), far & has & has_x,
            )
    ring(
        lambda kk: send(
            down_s.at[kk], down_r.at[pl.ds(mine, ROWS)], "down", at(0, 0, kk), keep=False
        )
    )
    chunks = ((0, 0, nz), (1, 0, cut_z), (1, cut_z, nz))

    def send_soil(c):
        ph, a, b = chunks[c]
        send(row_s.at[ph, 1, :, :, a:b], row_r.at[ph, 0, :, :, a:b], f"row{c}d", down, has_d)
        send(row_s.at[ph, 0, :, :, a:b], row_r.at[ph, 1, :, :, a:b], f"row{c}u", up, has_u)
        send(col_s.at[c, 1], col_r.at[c, 0], f"col{c}e", at(0, 1, k), has_e)
        send(col_s.at[c, 0], col_r.at[c, 1], f"col{c}w", at(0, -1, k), has_w)

    def wait_soil(c):
        ph, a, b = chunks[c]
        drain(row_r.at[ph, 0, :, :, a:b], f"row{c}d_r", has_u)
        drain(row_r.at[ph, 1, :, :, a:b], f"row{c}u_r", has_d)
        drain(col_r.at[c, 0], f"col{c}e_r", has_w)
        drain(col_r.at[c, 1], f"col{c}w_r", has_e)

    send_soil(0)

    def own(a, b):
        return field.at[:, a:b, 0:TILE]

    send(own(24, 32), own(40, 48), "right", {"grp": g, **right}, has_r)
    send(own(0, 8), own(32, 40), "left", {"grp": g, **left}, has_l)
    for dg, has, ref, n in ((1, has_s, above, "s"), (-1, has_n, below, "n")):
        send(own(0, 32), ref.at[:, 0:32], "line" + n, at(dg, 0, k), has)
        send(own(24, 32), ref.at[:, 40:48], "right" + n, {"grp": g + dg, **right}, has & has_r)
        send(own(0, 8), ref.at[:, 32:40], "left" + n, {"grp": g + dg, **left}, has & has_l)

    def sums(ph, z, halo):
        rows, cols = halo
        both = []
        for i, ref in enumerate((root, flow)):
            mid = [ref[ph, z + 1, :, tile(t)] for t in range(tiles)]
            from_west = [cols[0][i]] + [pltpu.roll(v, 1, 1) for v in mid]
            from_east = [pltpu.roll(v, TILE - 1, 1) for v in mid] + [cols[1][i]]
            totals = []
            for t in range(tiles):
                high, low = ref[ph, z, :, tile(t)], ref[ph, z + 2, :, tile(t)]
                ends = rows(t)
                north = jnp.where(sub == 0, ends[0][i], pltpu.roll(mid[t], 1, 0))
                south = jnp.where(sub == ROWS - 1, ends[1][i], pltpu.roll(mid[t], ROWS - 1, 0))
                west = jnp.where(lane == 0, from_west[t], from_west[t + 1])
                east = jnp.where(lane == TILE - 1, from_east[t + 1], from_east[t])
                totals.append(((high + low) + (north + south)) + (west + east))
                if i == 0:
                    both.append(GRAVITY_STEP * (high - low))
            both.append((mid, totals))
        own_root, q = both[tiles]
        r = both[tiles + 1][1]
        return own_root, q, [r[t] + both[t] for t in range(tiles)]

    def plain_halo(c, z):
        ph = chunks[c][0]

        def rows(t):
            return [
                [row_r[ph, d, i, t, pl.ds(z, 1), :] for i in range(2)] for d in range(2)
            ]

        cols = [
            [shift_to(col_r[c, d], z + 64 * i, (TILE - 1) * d) for i in range(2)]
            for d in range(2)
        ]
        return rows, cols

    def sweep_parts(ph, z, halo, base, weight):
        own_root, q, r = sums(ph, z, halo)
        return [
            (base[t] + own_root[t] * r[t], weight[t] + own_root[t] * q[t]) for t in range(tiles)
        ]

    def first_parts(z, halo):
        weight = [cap[z, :, tile(t)] for t in range(tiles)]
        base = [weight[t] * p[z, :, tile(t)] for t in range(tiles)]
        return sweep_parts(0, z, halo, base, weight)

    def keep(z, t, head, params):
        c, se, q = closures(head, params)
        gap = params[4] * (se - sat[z, :, tile(t)])
        cap[z, :, tile(t)] = c
        num[z, :, tile(t)] = c * head - gap
        r = q * head
        root[1, z + 1, :, tile(t)] = q
        flow[1, z + 1, :, tile(t)] = r
        return q, r

    def second_closures(z, packs):
        halo = plain_halo(0, z)
        heads = [upper / lower for upper, lower in first_parts(z, halo)]
        ends = []
        for t in range(tiles):
            q, r = keep(z, t, heads[t], [par[i, z, :, tile(t)] for i in range(PARAMS)])
            put_row(row_s.at[1, 0], row_s.at[1, 1], 0, z, t, q)
            put_row(row_s.at[1, 0], row_s.at[1, 1], 1, z, t, r)
            ends.append((q, r))
        return put_cols(packs, z, *ends[0], *ends[-1])

    for t in range(tiles):
        for d in range(2):
            top_s[d, :, tile(t)] = zero
            for i in range(2):
                row_s[1, d, i, t, 0:ROWS, :] = zero
    wait_soil(0)

    halo = plain_halo(0, 0)
    west, east = zero, zero
    for t, (upper, lower) in enumerate(first_parts(0, halo)):
        num[0, :, tile(t)] = upper
        cap[0, :, tile(t)] = lower
        for i, v in enumerate([upper, lower] + [par[j, 0, :, tile(t)] for j in (0, 1, 2, 5)]):
            top_s[0, i : i + 1, tile(t)] = v[0:1, :]
            top_s[1, i : i + 1, tile(t)] = v[ROWS - 1 : ROWS, :]
            if t == 0:
                west = jnp.where(lane == i, turn(v, i), west)
            if t == tiles - 1:
                east = jnp.where(lane == i, turn(v, i + 1), east)
    tcol_s[0], tcol_s[1] = west, east
    send(top_s.at[1], top_r.at[0], "topd", down, has_d)
    send(top_s.at[0], top_r.at[1], "topu", up, has_u)
    send(tcol_s.at[1], tcol_r.at[0], "tope", at(0, 1, k), has_e)
    send(tcol_s.at[0], tcol_r.at[1], "topw", at(0, -1, k), has_w)

    packs = lax.fori_loop(1, cut_z, second_closures, (zero, zero), unroll=4)
    col_s[1, 0], col_s[1, 1] = packs

    drain(own(40, 48), "right_r", has_l)
    drain(own(32, 40), "left_r", has_r)
    for has, ref, n in ((has_n, above, "s"), (has_s, below, "n")):
        drain(ref.at[:, 0:32], "line" + n + "_r", has)
        drain(ref.at[:, 40:48], "right" + n + "_r", has & has_l)
        drain(ref.at[:, 32:40], "left" + n + "_r", has & has_r)
    side = lax.broadcasted_iota(jnp.int32, (48, TILE), 1) < 64
    full = []
    for f in range(FIELDS):
        full.append(
            jnp.concatenate(
                [field[f, :, 0:TILE], jnp.where(side, below[f], above[f])], axis=1
            )
        )
    w0, level, bed, rain, land = full

    def next_of(v, axis):
        return pltpu.roll(v, v.shape[axis] - 1, axis)

    def prev_of(v, axis):
        return pltpu.roll(v, 1, axis)

    faces = [bed * next_of(bed, axis) for axis in (0, 1)]

    def outflow(w):
        carried = jnp.exp((5.0 / 3.0) * jnp.log(jnp.maximum(w, 1e-30)))
        surface = level + w
        total = None
        for axis in (0, 1):
            slope = surface - next_of(surface, axis)
            upwind = jnp.where(slope >= 0, carried, next_of(carried, axis))
            flux = faces[axis] * upwind * slope * lax.rsqrt(
                jnp.maximum(jnp.abs(slope), SLOPE_FLOOR)
            )
            net = flux - prev_of(flux, axis)
            total = net if total is None else total + net
        return total

    out0 = outflow(w0)

    drain(down_s.at[0 : nk - 1], "down_r")
    drain(down_s.at[0], "down128_r", has_s)
    drain(down_s.at[0], "down248_r", has_n)
    for dx, gets in ((1, first & has_w), (-1, last & has_e)):
        drain(edge_r.at[0:TILE], f"edge{dx}_r", gets)
        drain(down_s.at[0], f"edge128{dx}_r", gets & has_s)
        drain(down_s.at[0], f"edge248{dx}_r", gets & has_n)

    tall = lax.broadcasted_iota(jnp.int32, (TILE, TILE), 0)
    wide_lane = lax.broadcasted_iota(jnp.int32, (TILE, TILE), 1) & 63
    low = jnp.where(first, 38, 32)
    use_edge = (wide_lane >= low) & (wide_lane < low + 2) & (first | last)

    def received(a):
        rows = jnp.where(use_edge, edge_r[a : a + TILE, :], down_r[a : a + TILE, :])
        if a:
            rows = jnp.where((tall < ROWS) | (tall >= TILE - ROWS), rows, 0.0)
        return rows.T

    main, rim = received(0), received(TILE)

    def pick(a):
        body = [main[a : a + 32], rim[a : a + 32]]
        halo = [main[a + 32 : a + 40], rim[a + 32 : a + 40]]
        body, halo = (jnp.concatenate(v, axis=1) for v in (body, halo))
        return jnp.concatenate([body, halo, halo], axis=0)

    top = pick(0)
    leak = land * pick(64)

    def advance(w, out):
        rate = leak * (w - top)
        return jnp.maximum(w + SURFACE_STEP * (rain - rate - out), 0.0), rate

    w1, rate0 = advance(w0, out0)
    w2, rate1 = advance(w1, outflow(w1))
    rate2 = leak * (w2 - top)
    exchange = SURFACE_STEP * (rate0 + rate1 + rate2)
    body = exchange[0:32]
    mesh_t = [body[:, 0:TILE]] * 3 + [exchange[32:48, 0:TILE]] * 2
    square = jnp.concatenate(mesh_t, axis=0).T
    outer = jnp.concatenate([body[:, TILE:]] * 4, axis=0).T
    blocks = [square[ROWS * j : ROWS * (j + 1)] for j in range(nk)]
    blocks = [outer[TILE - ROWS :]] + blocks + [outer[0:ROWS]]
    folded = [pltpu.roll(v, 4, 0) for v in blocks]
    fold = ((lane >= 32) & (lane < 64)) | (lane >= 112)
    rim = (lane >= 64) & (lane < 96)
    for j in range(nk):
        ends = jnp.where(sub < 2, blocks[j + 2], folded[j])
        back_s[j] = jnp.where(rim, ends, jnp.where(fold, folded[j + 1], blocks[j + 1]))
    back_r[k] = back_s[k]
    ring(
        lambda kk: send(back_s.at[kk, 0:4], back_r.at[k, 0:4], "back", at(0, 0, kk), keep=False)
    )
    send_soil(1)
    w3, _ = advance(w2, outflow(w2))
    water_out[...] = w3[0:32, 0:TILE]

    packs = lax.fori_loop(cut_z, nz, second_closures, (zero, zero), unroll=4)
    col_s[2, 0], col_s[2, 1] = packs
    send_soil(2)

    def last_sweep(z, halo):
        base = [num[z, :, tile(t)] for t in range(tiles)]
        weight = [cap[z, :, tile(t)] for t in range(tiles)]
        for t, (upper, lower) in enumerate(sweep_parts(1, z, halo, base, weight)):
            head_out[z, :, tile(t)] = upper / lower

    def last_step(c):
        def step(z, carry):
            last_sweep(z, plain_halo(c, z))
            return carry

        return step

    wait_soil(1)
    lax.fori_loop(2, cut_z - 1, last_step(1), 0, unroll=4)
    last_sweep(cut_z - 1, plain_halo(1, cut_z - 1))
    wait_soil(2)
    lax.fori_loop(cut_z, nz, last_step(2), 0, unroll=4)
    drain(top_r.at[0], "topd_r", has_u)
    drain(top_r.at[1], "topu_r", has_d)
    drain(tcol_r.at[0], "tope_r", has_w)
    drain(tcol_r.at[1], "topw_r", has_e)

    drain(down_s.at[0 : nk - 1, 0:4], "back_r")

    def gathered(t, group):
        v = turn(back_r[per * t], -32 * group)
        for i in range(1, per):
            v = jnp.where(lane >= 32 * i, turn(back_r[per * t + i], 32 * (i - group)), v)
        return v

    def unfold(a, b):
        return jnp.where(sub < 4, a, pltpu.roll(b, 4, 0))

    def beside(parts, gain):
        upper, lower, entry, expo, pore, scale = parts
        head = (upper + gain) / jnp.maximum(lower, 1e-6)
        _, _, q = closures(head, (entry, expo, pore, 0.0, None, scale))
        return q, q * head

    extras, rows_beside = [], []
    for t in range(tiles):
        extras.append(unfold(gathered(t, 0), gathered(t, 1)))
        parts = [
            jnp.where(sub < 2, top_r[1, i : i + 1, tile(t)], top_r[0, i : i + 1, tile(t)])
            for i in range(6)
        ]
        rows_beside.append(beside(parts, gathered(t, 2)))
    parts = [
        jnp.where(lane < 64, turn(tcol_r[0], -i), turn(tcol_r[1], TILE - 1 - i)) for i in range(6)
    ]
    west, east = back_r[0], back_r[nk - 1]
    gain = unfold(
        jnp.where(lane < 64, turn(west, -111), turn(east, 31)),
        jnp.where(lane < 64, turn(west, -127), turn(east, 15)),
    )
    ends = beside(parts, gain)
    for t in range(tiles):
        head = (num[0, :, tile(t)] + extras[t]) / cap[0, :, tile(t)]
        keep(0, t, head, [par[i, 0, :, tile(t)] for i in range(PARAMS)])
        num[0, :, tile(t)] += extras[t]

    def top_rows(t):
        return [[v[3:4, :] for v in rows_beside[t]], [v[0:1, :] for v in rows_beside[t]]]

    last_sweep(0, (top_rows, [ends, ends]))
    last_sweep(1, plain_halo(1, 1))

    drain(down_s.at[0 : nk - 1], "down_s")
    drain(down_s.at[0 : nk - 1, 0:4], "back_s")
    drain(down_s.at[0:nk], "down248_s", last & has_s)
    drain(down_s.at[0:nk], "down128_s", first & has_n)
    for copy, when in pending:
        if when is None:
            copy.wait_send()
        else:
            pl.when(when)(copy.wait_send)


def solution(mesh):
    sizes = tuple(mesh.shape[a] for a in ("grp", "gx", "gy"))
    nk = sizes[2]

    def local(
        pressure, soil_class, capacity_range, inverse_entry, shape_index, conductivity,
        depth, elevation, roughness, rain, land_mask, channel_mask,
    ):
        nz, _, wide = pressure.shape
        kinds = capacity_range.shape[0]
        hbm = pl.BlockSpec(memory_space=pl.ANY)
        soil = (nz, ROWS, wide)
        vmem = pltpu.VMEM
        head, water = pl.pallas_call(
            functools.partial(kernel, nz, wide, kinds, sizes, 16),
            out_shape=(
                vmem(pressure.shape, F32),
                vmem(depth.shape[::-1], F32),
            ),
            in_specs=[hbm] * 12,
            out_specs=(pl.BlockSpec(memory_space=vmem),) * 2,
            scratch_shapes=[
                pltpu.SMEM((4, kinds), F32),
                vmem(soil, F32),
                vmem(soil, jnp.int32),
                vmem((PARAMS, *soil), F32),
                vmem(soil, F32),
                vmem(soil, F32),
                vmem((2, nz + 2, ROWS, wide), F32),
                vmem((2, nz + 2, ROWS, wide), F32),
                vmem(soil, F32),
                vmem((2, 2, 2, wide // TILE, nz, TILE), F32),
                vmem((2, 2, 2, wide // TILE, nz, TILE), F32),
                vmem((2, ROWS, wide), F32),
                vmem((2, ROWS, wide), F32),
                vmem((3, 2, ROWS, TILE), F32),
                vmem((3, 2, ROWS, TILE), F32),
                vmem((2, ROWS, TILE), F32),
                vmem((2, ROWS, TILE), F32),
                vmem((4, 32, TILE), F32),
                vmem((FIELDS, 48, 2 * TILE), F32),
                vmem((FIELDS, 48, TILE), F32),
                vmem((FIELDS, 48, TILE), F32),
                vmem((nk + 2, ROWS, TILE), F32),
                vmem((2 * TILE, TILE), F32),
                vmem((2 * TILE, TILE), F32),
                vmem((nk, ROWS, TILE), F32),
                vmem((nk, ROWS, TILE), F32),
                vmem((2, 32, TILE), jnp.int32),
                pltpu.SemaphoreType.DMA((100,)),
            ],
            compiler_params=pltpu.CompilerParams(
                collective_id=0, has_side_effects=True, vmem_limit_bytes=60 * 1024 * 1024
            ),
        )(
            pressure, soil_class, capacity_range, inverse_entry, shape_index, conductivity,
            depth.T, elevation.T, roughness.T, rain.T, land_mask.T, channel_mask.T,
        )
        return head, water.T

    tile = P(None, ("grp", "gy"), "gx")
    flat = P("grp", ("gx", "gy"))
    return jax.shard_map(
        local,
        mesh=mesh,
        in_specs=(tile, tile, P(), P(), P(), P()) + (flat,) * 6,
        out_specs=(tile, flat),
        check_vma=False,
    )
```

```python
import functools

import jax
import jax.numpy as jnp
from jax import lax
from jax.experimental import pallas as pl
from jax.experimental.pallas import tpu as pltpu
from jax.sharding import PartitionSpec as P

MESH = pl.DeviceIdType.MESH
F32 = jnp.float32

STORAGE = 0.01
GRAVITY_STEP = 0.5
SUCTION_FLOOR = 0.01
SLOPE_FLOOR = 0.1
SURFACE_STEP = 0.3
LEAKANCE = 0.5

TILE = 128
ROWS = 8
FIELDS = 5
PARAMS = 6


def lanes():
    return lax.broadcasted_iota(jnp.int32, (ROWS, TILE), 1)


def sublanes():
    return lax.broadcasted_iota(jnp.int32, (ROWS, TILE), 0)


def gather(table, index):
    return jnp.take_along_axis(table, index, axis=1, mode="promise_in_bounds")


def build_tables(tab, kinds):
    lane = lanes()
    rows = []
    for i in range(4):
        row = jnp.zeros((ROWS, TILE), F32)
        for kind in range(kinds):
            row = jnp.where(lane == kind, tab[i, kind], row)
        rows.append(row)
    span, entry, shape, conduct = rows
    shape = jnp.where(lane < kinds, shape, 2.0)
    pore = 1.0 - 1.0 / shape
    expo = 1.0 / (1.0 - pore)
    return (
        -entry,
        expo,
        pore,
        span * pore * expo * entry,
        span,
        2.0 * jnp.sqrt(conduct),
    )


def closures(p, params):
    entry, expo, pore, lead, _, scale = params
    log_scaled = jnp.log(jnp.maximum(entry * p, SUCTION_FLOOR))
    up = expo * log_scaled
    log_sum = jnp.log(1.0 + jnp.exp(up))
    drop = pore * log_sum
    wet = pore * up - drop
    held = jnp.exp(wet)
    capacity = STORAGE + lead * jnp.exp(wet - log_sum)
    fourth = jnp.exp(-0.25 * drop)
    half = fourth * fourth
    root = scale * fourth * (1.0 - held)
    return capacity, half * half, root


def kernel(
    nz, wide, kinds, sizes, cut_z,
    p_in, k_in, t0_in, t1_in, t2_in, t3_in,
    s0_in, s1_in, s2_in, s3_in, s4_in, s5_in,
    head_out, water_out,
    tab, p, kind, par, cap, sat, root, flow, num,
    row_s, row_r, top_s, top_r, col_s, col_r, tcol_s, tcol_r,
    surf_in, field, below, above,
    down_s, down_r, edge_r, back_s, back_r, water,
    sem,
):
    ng, nx, nk = sizes
    tiles = wide // TILE
    per = TILE // 32
    g, x, k = (lax.axis_index(a) for a in ("grp", "gx", "gy"))
    lane, sub = lanes(), sublanes()
    first, last = k == 0, k == nk - 1
    has_n, has_s = g > 0, g < ng - 1
    has_w, has_e = x > 0, x < nx - 1

    names = {}

    def s(name):
        return sem.at[names.setdefault(name, len(names))]

    def at(dg, dx, kk):
        return {"grp": g + dg, "gx": x + dx, "gy": kk}

    def tile(t):
        return slice(t * TILE, (t + 1) * TILE)

    def load(src, dst, name):
        copy = pltpu.make_async_copy(src, dst, s(name))
        copy.start()
        return copy

    barrier = pltpu.get_barrier_semaphore()

    def greet(device):
        pl.semaphore_signal(barrier, 1, device_id=device, device_id_type=MESH)

    def ring(body):
        for away in sorted(range(1, nk), key=lambda d: -min(d, nk - d)):
            body(jnp.where(k + away >= nk, k + away - nk, k + away))

    def every(body):
        def step(i, _):
            body(i)
            return 0

        lax.fori_loop(0, nk, step, 0)

    col = x * nk + k
    has_l, has_r = col > 0, col < nx * nk - 1
    left = {"gx": jnp.maximum(col - 1, 0) // nk, "gy": lax.rem(jnp.maximum(col - 1, 0), nk)}
    right = {"gx": (col + 1) // nk, "gy": lax.rem(col + 1, nk)}
    row = g * nk + k
    has_u, has_d = row > 0, row < ng * nk - 1
    up = {"grp": jnp.maximum(row - 1, 0) // nk, "gx": x, "gy": lax.rem(jnp.maximum(row - 1, 0), nk)}
    down = {"grp": (row + 1) // nk, "gx": x, "gy": lax.rem(row + 1, nk)}

    @pl.when(has_w)
    def _():
        @pl.when(first)
        def _():
            every(lambda kk: greet(at(0, -1, kk)))

        greet(at(0, -1, k))

    @pl.when(has_e)
    def _():
        @pl.when(last)
        def _():
            every(lambda kk: greet(at(0, 1, kk)))

        greet(at(0, 1, k))

    for dg, has in ((-1, has_n), (1, has_s)):
        far = nk - 1 if dg < 0 else 0

        @pl.when(has)
        def _():
            greet(at(dg, 0, far))
            greet(at(dg, 0, k))

            @pl.when(has_l)
            def _():
                greet({"grp": g + dg, **left})

            @pl.when(has_r)
            def _():
                greet({"grp": g + dg, **right})

            @pl.when(first & has_w)
            def _():
                greet(at(dg, -1, far))

            @pl.when(last & has_e)
            def _():
                greet(at(dg, 1, far))

    ring(lambda kk: greet(at(0, 0, kk)))

    table_loads = [
        load(ref, tab.at[i], f"tab{i}")
        for i, ref in enumerate((t0_in, t1_in, t2_in, t3_in))
    ]
    top_loads = [
        load(p_in.at[0:1], p.at[0:1], "p0"),
        load(k_in.at[0:1], kind.at[0:1], "k0"),
    ]
    surf_loads = [
        load(s0_in, surf_in.at[0], "s0"),
        load(s1_in, surf_in.at[1], "s1"),
        load(s2_in, surf_in.at[2], "s2"),
        load(s3_in, surf_in.at[3], "s3"),
    ]
    mask_loads = [
        load(s4_in, water.at[0], "s4"),
        load(s5_in, water.at[1], "s5"),
    ]
    rest_loads = [
        load(p_in.at[1:nz], p.at[1:nz], "p1"),
        load(k_in.at[1:nz], kind.at[1:nz], "k1"),
    ]

    def one(flag):
        return flag.astype(jnp.int32)

    rows_to = one(has_n) + one(has_s)
    cols_to = one(has_w) + one(has_e)
    corner = one(first & has_n) + one(last & has_s)
    expected = (
        (nk - 1)
        + corner * nk
        + rows_to * (1 + one(has_l) + one(has_r))
        + 2 * cols_to
        + corner * cols_to
    )

    zero = jnp.zeros((ROWS, TILE), F32)
    for j in range(nk):
        back_r[j] = zero

    def clear(ref, rows):
        for r in range(0, rows, ROWS):
            for c in range(0, ref.shape[-1], TILE):
                ref[r : r + ROWS, c : c + TILE] = zero

    for t in range(tiles):
        for ph in range(2):
            for z in (0, nz + 1):
                root[ph, z, :, tile(t)] = zero
                flow[ph, z, :, tile(t)] = zero

    for d, has, has_g, ref in ((0, has_u, has_n, above), (1, has_d, has_s, below)):

        @pl.when(jnp.logical_not(has))
        def _():
            for ph in range(2):
                for i in range(2):
                    for t in range(tiles):
                        clear(row_r.at[ph, d, i, t], nz)
            clear(top_r.at[d], ROWS)

        @pl.when(jnp.logical_not(has_g))
        def _():
            for f in range(FIELDS):
                clear(ref.at[f], 48)
            off = 248 if d == 0 else 128
            clear(down_r.at[off : off + ROWS], ROWS)

        @pl.when(has_g & jnp.logical_not(has_r))
        def _():
            for f in range(FIELDS):
                ref[f, 32:40, :] = zero

        @pl.when(has_g & jnp.logical_not(has_l))
        def _():
            for f in range(FIELDS):
                ref[f, 40:48, :] = zero

    for d, has in ((0, has_w), (1, has_e)):

        @pl.when(jnp.logical_not(has))
        def _():
            for c in range(3):
                col_r[c, d] = zero
            tcol_r[d] = zero

    for d, has in ((0, has_r), (1, has_l)):

        @pl.when(jnp.logical_not(has))
        def _():
            for f in range(FIELDS):
                field[f, 32 + 8 * d : 40 + 8 * d, 0:TILE] = zero

    gets_edge = (first & has_w) | (last & has_e)

    @pl.when(jnp.logical_not(gets_edge))
    def _():
        clear(edge_r.at[0:TILE], TILE)

    for off, has in ((128, has_s), (248, has_n)):

        @pl.when(jnp.logical_not(gets_edge & has))
        def _():
            clear(edge_r.at[off : off + ROWS], ROWS)

    for c in table_loads:
        c.wait()
    tables = build_tables(tab, kinds)

    def layer_params(z, t):
        index = kind[z, :, tile(t)]
        return [gather(table, index) for table in tables]

    def put_row(dst_first, dst_last, i, z, t, value):
        dst_first[i, t, pl.ds(z, 1), :] = value[0:1, :]
        dst_last[i, t, pl.ds(z, 1), :] = value[7:8, :]

    def shift_to(value, frm, to):
        return pltpu.roll(value, lax.rem(to - frm + TILE, TILE), 1)

    def put_cols(packs, z, q0, r0, q1, r1):
        west, east = packs
        west = jnp.where(lane == z, shift_to(q0, 0, z), west)
        west = jnp.where(lane == z + 64, shift_to(r0, 0, z + 64), west)
        east = jnp.where(lane == z, shift_to(q1, TILE - 1, z), east)
        east = jnp.where(lane == z + 64, shift_to(r1, TILE - 1, z + 64), east)
        return west, east

    def first_closures(z, packs):
        ends = []
        for t in range(tiles):
            params = layer_params(z, t)
            for i in range(PARAMS):
                par[i, z, :, tile(t)] = params[i]
            pz = p[z, :, tile(t)]
            c, se, q = closures(pz, params)
            r = q * pz
            cap[z, :, tile(t)] = c
            sat[z, :, tile(t)] = se
            root[0, z + 1, :, tile(t)] = q
            flow[0, z + 1, :, tile(t)] = r
            put_row(row_s.at[0, 0], row_s.at[0, 1], 0, z, t, q)
            put_row(row_s.at[0, 0], row_s.at[0, 1], 1, z, t, r)
            ends.append((q, r))
        return put_cols(packs, z, *ends[0], *ends[-1])

    for c in top_loads:
        c.wait()
    packs = first_closures(0, (zero, zero))

    tops = [p[0, :, tile(t)] for t in range(tiles)]
    halves = [jnp.square(root[0, 1, :, tile(t)]) * 0.125 for t in range(tiles)]

    def turn(v, by):
        by %= TILE
        return pltpu.roll(v, by, 1) if by else v

    def cut(parts, kk, base):
        t, o = divmod(kk * 32, TILE)
        out = turn(parts[t], base - o)
        before = parts[t] if o else parts[max(t - 1, 0)]
        out = jnp.where(
            (lane >= base + 38) & (lane < base + 40), turn(before, base + 40 - o), out
        )
        if o + 32 == TILE and t + 1 < tiles:
            after = turn(parts[t + 1], base + 32)
            out = jnp.where((lane >= base + 32) & (lane < base + 34), after, out)
        return out

    for kk in range(nk):
        down_s[kk] = jnp.where(lane < 64, cut(tops, kk, 0), cut(halves, kk, 64))
    down_s[nk] = jnp.where(lane < 64, turn(tops[-1], 40), turn(halves[-1], 104))
    down_s[nk + 1] = jnp.where(lane < 64, turn(tops[0], 32), turn(halves[0], 96))
    mine = pl.multiple_of(k * ROWS, ROWS)
    down_r[pl.ds(mine, ROWS), :] = down_s[k]

    pending = []

    def send(src, dst, name, device, when=None, keep=True):
        copy = pltpu.make_async_remote_copy(
            src_ref=src,
            dst_ref=dst,
            send_sem=s(name + "_s"),
            recv_sem=s(name + "_r"),
            device_id=device,
            device_id_type=MESH,
        )
        if when is None:
            copy.start()
        else:
            pl.when(when)(copy.start)
        if keep:
            pending.append((copy, when))
        return copy

    def drain(ref, name, when=None):
        wait = pltpu.make_async_copy(ref, ref, s(name)).wait
        if when is None:
            wait()
        else:
            pl.when(when)(wait)

    for c in surf_loads + mask_loads:
        c.wait()
    field[0, 0:32, 0:TILE] = surf_in[0]
    field[1, 0:32, 0:TILE] = surf_in[1]
    field[2, 0:32, 0:TILE] = jnp.sqrt((1.0 + water[1].astype(F32)) / surf_in[2])
    field[3, 0:32, 0:TILE] = surf_in[3]
    field[4, 0:32, 0:TILE] = water[0].astype(F32)

    for c in rest_loads:
        c.wait()
    packs = lax.fori_loop(1, nz, first_closures, packs, unroll=4)
    col_s[0, 0], col_s[0, 1] = packs

    pl.semaphore_wait(barrier, expected)
    for dx, kk, has_x, i in ((1, 0, has_e, nk), (-1, nk - 1, has_w, nk + 1)):
        send(
            down_s.at[i], edge_r.at[pl.ds(mine, ROWS)], f"edge{dx}", at(0, dx, kk), has_x
        )
    for dg, far, has, slot in ((1, last, has_s, 248), (-1, first, has_n, 128)):

        @pl.when(far & has)
        def _():
            every(
                lambda kk: send(
                    down_s.at[kk], down_r.at[slot : slot + ROWS], f"down{slot}", at(dg, 0, kk),
                    keep=False,
                )
            )

        for dx, kk, has_x, i in ((1, 0, has_e, nk), (-1, nk - 1, has_w, nk + 1)):
            send(
                down_s.at[i], edge_r.at[slot : slot + ROWS], f"edge{slot}{dx}",
                at(dg, dx, kk), far & has & has_x,
            )
    ring(
        lambda kk: send(
            down_s.at[kk], down_r.at[pl.ds(mine, ROWS)], "down", at(0, 0, kk), keep=False
        )
    )
    chunks = ((0, 0, nz), (1, 0, cut_z), (1, cut_z, nz))

    def send_soil(c):
        ph, a, b = chunks[c]
        send(row_s.at[ph, 1, :, :, a:b], row_r.at[ph, 0, :, :, a:b], f"row{c}d", down, has_d)
        send(row_s.at[ph, 0, :, :, a:b], row_r.at[ph, 1, :, :, a:b], f"row{c}u", up, has_u)
        send(col_s.at[c, 1], col_r.at[c, 0], f"col{c}e", at(0, 1, k), has_e)
        send(col_s.at[c, 0], col_r.at[c, 1], f"col{c}w", at(0, -1, k), has_w)

    def wait_soil(c):
        ph, a, b = chunks[c]
        drain(row_r.at[ph, 0, :, :, a:b], f"row{c}d_r", has_u)
        drain(row_r.at[ph, 1, :, :, a:b], f"row{c}u_r", has_d)
        drain(col_r.at[c, 0], f"col{c}e_r", has_w)
        drain(col_r.at[c, 1], f"col{c}w_r", has_e)

    send_soil(0)

    def own(a, b):
        return field.at[:, a:b, 0:TILE]

    send(own(24, 32), own(40, 48), "right", {"grp": g, **right}, has_r)
    send(own(0, 8), own(32, 40), "left", {"grp": g, **left}, has_l)
    for dg, has, ref, n in ((1, has_s, above, "s"), (-1, has_n, below, "n")):
        send(own(0, 32), ref.at[:, 0:32], "line" + n, at(dg, 0, k), has)
        send(own(24, 32), ref.at[:, 40:48], "right" + n, {"grp": g + dg, **right}, has & has_r)
        send(own(0, 8), ref.at[:, 32:40], "left" + n, {"grp": g + dg, **left}, has & has_l)

    def sums(ph, z, halo):
        rows, cols = halo
        both = []
        for i, ref in enumerate((root, flow)):
            mid = [ref[ph, z + 1, :, tile(t)] for t in range(tiles)]
            from_west = [cols[0][i]] + [pltpu.roll(v, 1, 1) for v in mid]
            from_east = [pltpu.roll(v, TILE - 1, 1) for v in mid] + [cols[1][i]]
            totals = []
            for t in range(tiles):
                high, low = ref[ph, z, :, tile(t)], ref[ph, z + 2, :, tile(t)]
                ends = rows(t)
                north = jnp.where(sub == 0, ends[0][i], pltpu.roll(mid[t], 1, 0))
                south = jnp.where(sub == ROWS - 1, ends[1][i], pltpu.roll(mid[t], ROWS - 1, 0))
                west = jnp.where(lane == 0, from_west[t], from_west[t + 1])
                east = jnp.where(lane == TILE - 1, from_east[t + 1], from_east[t])
                totals.append(((high + low) + (north + south)) + (west + east))
                if i == 0:
                    both.append(GRAVITY_STEP * (high - low))
            both.append((mid, totals))
        own_root, q = both[tiles]
        r = both[tiles + 1][1]
        return own_root, q, [r[t] + both[t] for t in range(tiles)]

    def plain_halo(c, z):
        ph = chunks[c][0]

        def rows(t):
            return [
                [row_r[ph, d, i, t, pl.ds(z, 1), :] for i in range(2)] for d in range(2)
            ]

        cols = [
            [shift_to(col_r[c, d], z + 64 * i, (TILE - 1) * d) for i in range(2)]
            for d in range(2)
        ]
        return rows, cols

    def sweep_parts(ph, z, halo, base, weight):
        own_root, q, r = sums(ph, z, halo)
        return [
            (base[t] + own_root[t] * r[t], weight[t] + own_root[t] * q[t]) for t in range(tiles)
        ]

    def first_parts(z, halo):
        weight = [cap[z, :, tile(t)] for t in range(tiles)]
        base = [weight[t] * p[z, :, tile(t)] for t in range(tiles)]
        return sweep_parts(0, z, halo, base, weight)

    def keep(z, t, head, params):
        c, se, q = closures(head, params)
        gap = params[4] * (se - sat[z, :, tile(t)])
        cap[z, :, tile(t)] = c
        num[z, :, tile(t)] = c * head - gap
        r = q * head
        root[1, z + 1, :, tile(t)] = q
        flow[1, z + 1, :, tile(t)] = r
        return q, r

    def second_closures(z, packs):
        halo = plain_halo(0, z)
        heads = [upper / lower for upper, lower in first_parts(z, halo)]
        ends = []
        for t in range(tiles):
            q, r = keep(z, t, heads[t], [par[i, z, :, tile(t)] for i in range(PARAMS)])
            put_row(row_s.at[1, 0], row_s.at[1, 1], 0, z, t, q)
            put_row(row_s.at[1, 0], row_s.at[1, 1], 1, z, t, r)
            ends.append((q, r))
        return put_cols(packs, z, *ends[0], *ends[-1])

    for t in range(tiles):
        for d in range(2):
            top_s[d, :, tile(t)] = zero
            for i in range(2):
                row_s[1, d, i, t, 0:ROWS, :] = zero
    wait_soil(0)

    halo = plain_halo(0, 0)
    west, east = zero, zero
    for t, (upper, lower) in enumerate(first_parts(0, halo)):
        num[0, :, tile(t)] = upper
        cap[0, :, tile(t)] = lower
        for i, v in enumerate([upper, lower] + [par[j, 0, :, tile(t)] for j in (0, 1, 2, 5)]):
            top_s[0, i : i + 1, tile(t)] = v[0:1, :]
            top_s[1, i : i + 1, tile(t)] = v[ROWS - 1 : ROWS, :]
            if t == 0:
                west = jnp.where(lane == i, turn(v, i), west)
            if t == tiles - 1:
                east = jnp.where(lane == i, turn(v, i + 1), east)
    tcol_s[0], tcol_s[1] = west, east
    send(top_s.at[1], top_r.at[0], "topd", down, has_d)
    send(top_s.at[0], top_r.at[1], "topu", up, has_u)
    send(tcol_s.at[1], tcol_r.at[0], "tope", at(0, 1, k), has_e)
    send(tcol_s.at[0], tcol_r.at[1], "topw", at(0, -1, k), has_w)

    packs = lax.fori_loop(1, cut_z, second_closures, (zero, zero), unroll=4)
    col_s[1, 0], col_s[1, 1] = packs

    drain(own(40, 48), "right_r", has_l)
    drain(own(32, 40), "left_r", has_r)
    for has, ref, n in ((has_n, above, "s"), (has_s, below, "n")):
        drain(ref.at[:, 0:32], "line" + n + "_r", has)
        drain(ref.at[:, 40:48], "right" + n + "_r", has & has_l)
        drain(ref.at[:, 32:40], "left" + n + "_r", has & has_r)
    side = lax.broadcasted_iota(jnp.int32, (48, TILE), 1) < 64
    full = []
    for f in range(FIELDS):
        full.append(
            jnp.concatenate(
                [field[f, :, 0:TILE], jnp.where(side, below[f], above[f])], axis=1
            )
        )
    w0, level, bed, rain, land = full

    def next_of(v, axis):
        return pltpu.roll(v, v.shape[axis] - 1, axis)

    def prev_of(v, axis):
        return pltpu.roll(v, 1, axis)

    faces = [bed * next_of(bed, axis) for axis in (0, 1)]

    def outflow(w):
        carried = jnp.exp((5.0 / 3.0) * jnp.log(jnp.maximum(w, 1e-30)))
        surface = level + w
        total = None
        for axis in (0, 1):
            slope = surface - next_of(surface, axis)
            upwind = jnp.where(slope >= 0, carried, next_of(carried, axis))
            flux = faces[axis] * upwind * slope * lax.rsqrt(
                jnp.maximum(jnp.abs(slope), SLOPE_FLOOR)
            )
            net = flux - prev_of(flux, axis)
            total = net if total is None else total + net
        return total

    out0 = outflow(w0)

    drain(down_s.at[0 : nk - 1], "down_r")
    drain(down_s.at[0], "down128_r", has_s)
    drain(down_s.at[0], "down248_r", has_n)
    for dx, gets in ((1, first & has_w), (-1, last & has_e)):
        drain(edge_r.at[0:TILE], f"edge{dx}_r", gets)
        drain(down_s.at[0], f"edge128{dx}_r", gets & has_s)
        drain(down_s.at[0], f"edge248{dx}_r", gets & has_n)

    tall = lax.broadcasted_iota(jnp.int32, (TILE, TILE), 0)
    wide_lane = lax.broadcasted_iota(jnp.int32, (TILE, TILE), 1) & 63
    low = jnp.where(first, 38, 32)
    use_edge = (wide_lane >= low) & (wide_lane < low + 2) & (first | last)

    def received(a):
        rows = jnp.where(use_edge, edge_r[a : a + TILE, :], down_r[a : a + TILE, :])
        if a:
            rows = jnp.where((tall < ROWS) | (tall >= TILE - ROWS), rows, 0.0)
        return rows.T

    main, rim = received(0), received(TILE)

    def pick(a):
        body = [main[a : a + 32], rim[a : a + 32]]
        halo = [main[a + 32 : a + 40], rim[a + 32 : a + 40]]
        body, halo = (jnp.concatenate(v, axis=1) for v in (body, halo))
        return jnp.concatenate([body, halo, halo], axis=0)

    top = pick(0)
    leak = land * pick(64)

    def advance(w, out):
        rate = leak * (w - top)
        return jnp.maximum(w + SURFACE_STEP * (rain - rate - out), 0.0), rate

    w1, rate0 = advance(w0, out0)
    w2, rate1 = advance(w1, outflow(w1))
    rate2 = leak * (w2 - top)
    exchange = SURFACE_STEP * (rate0 + rate1 + rate2)
    body = exchange[0:32]
    mesh_t = [body[:, 0:TILE]] * 3 + [exchange[32:48, 0:TILE]] * 2
    square = jnp.concatenate(mesh_t, axis=0).T
    outer = jnp.concatenate([body[:, TILE:]] * 4, axis=0).T
    blocks = [square[ROWS * j : ROWS * (j + 1)] for j in range(nk)]
    blocks = [outer[TILE - ROWS :]] + blocks + [outer[0:ROWS]]
    folded = [pltpu.roll(v, 4, 0) for v in blocks]
    fold = ((lane >= 32) & (lane < 64)) | (lane >= 112)
    rim = (lane >= 64) & (lane < 96)
    for j in range(nk):
        ends = jnp.where(sub < 2, blocks[j + 2], folded[j])
        back_s[j] = jnp.where(rim, ends, jnp.where(fold, folded[j + 1], blocks[j + 1]))
    back_r[k] = back_s[k]
    ring(
        lambda kk: send(back_s.at[kk, 0:4], back_r.at[k, 0:4], "back", at(0, 0, kk), keep=False)
    )
    send_soil(1)
    w3, _ = advance(w2, outflow(w2))
    water_out[...] = w3[0:32, 0:TILE]

    packs = lax.fori_loop(cut_z, nz, second_closures, (zero, zero), unroll=4)
    col_s[2, 0], col_s[2, 1] = packs
    send_soil(2)

    def last_sweep(z, halo):
        base = [num[z, :, tile(t)] for t in range(tiles)]
        weight = [cap[z, :, tile(t)] for t in range(tiles)]
        for t, (upper, lower) in enumerate(sweep_parts(1, z, halo, base, weight)):
            head_out[z, :, tile(t)] = upper / lower

    def last_step(c):
        def step(z, carry):
            last_sweep(z, plain_halo(c, z))
            return carry

        return step

    wait_soil(1)
    lax.fori_loop(2, cut_z - 1, last_step(1), 0, unroll=4)
    last_sweep(cut_z - 1, plain_halo(1, cut_z - 1))
    wait_soil(2)
    lax.fori_loop(cut_z, nz, last_step(2), 0, unroll=4)
    drain(top_r.at[0], "topd_r", has_u)
    drain(top_r.at[1], "topu_r", has_d)
    drain(tcol_r.at[0], "tope_r", has_w)
    drain(tcol_r.at[1], "topw_r", has_e)

    drain(down_s.at[0 : nk - 1], "down_s")
    drain(down_s.at[0 : nk - 1, 0:4], "back_s")
    drain(down_s.at[0:nk], "down248_s", last & has_s)
    drain(down_s.at[0:nk], "down128_s", first & has_n)
    for copy, when in pending:
        if when is None:
            copy.wait_send()
        else:
            pl.when(when)(copy.wait_send)

    drain(down_s.at[0 : nk - 1, 0:4], "back_r")

    def gathered(t, group):
        v = turn(back_r[per * t], -32 * group)
        for i in range(1, per):
            v = jnp.where(lane >= 32 * i, turn(back_r[per * t + i], 32 * (i - group)), v)
        return v

    def unfold(a, b):
        return jnp.where(sub < 4, a, pltpu.roll(b, 4, 0))

    def beside(parts, gain):
        upper, lower, entry, expo, pore, scale = parts
        head = (upper + gain) / jnp.maximum(lower, 1e-6)
        _, _, q = closures(head, (entry, expo, pore, 0.0, None, scale))
        return q, q * head

    extras, rows_beside = [], []
    for t in range(tiles):
        extras.append(unfold(gathered(t, 0), gathered(t, 1)))
        parts = [
            jnp.where(sub < 2, top_r[1, i : i + 1, tile(t)], top_r[0, i : i + 1, tile(t)])
            for i in range(6)
        ]
        rows_beside.append(beside(parts, gathered(t, 2)))
    parts = [
        jnp.where(lane < 64, turn(tcol_r[0], -i), turn(tcol_r[1], TILE - 1 - i)) for i in range(6)
    ]
    west, east = back_r[0], back_r[nk - 1]
    gain = unfold(
        jnp.where(lane < 64, turn(west, -111), turn(east, 31)),
        jnp.where(lane < 64, turn(west, -127), turn(east, 15)),
    )
    ends = beside(parts, gain)
    for t in range(tiles):
        head = (num[0, :, tile(t)] + extras[t]) / cap[0, :, tile(t)]
        keep(0, t, head, [par[i, 0, :, tile(t)] for i in range(PARAMS)])
        num[0, :, tile(t)] += extras[t]

    def top_rows(t):
        return [[v[3:4, :] for v in rows_beside[t]], [v[0:1, :] for v in rows_beside[t]]]

    last_sweep(0, (top_rows, [ends, ends]))
    last_sweep(1, plain_halo(1, 1))


def deliver(head, water, head_out, water_out, sem):
    copies = [
        pltpu.make_async_copy(head, head_out, sem.at[0]),
        pltpu.make_async_copy(water, water_out, sem.at[1]),
    ]
    for c in copies:
        c.start()
    for c in copies:
        c.wait()


def solution(mesh):
    sizes = tuple(mesh.shape[a] for a in ("grp", "gx", "gy"))
    nk = sizes[2]

    def local(
        pressure, soil_class, capacity_range, inverse_entry, shape_index, conductivity,
        depth, elevation, roughness, rain, land_mask, channel_mask,
    ):
        nz, _, wide = pressure.shape
        kinds = capacity_range.shape[0]
        hbm = pl.BlockSpec(memory_space=pl.ANY)
        soil = (nz, ROWS, wide)
        vmem = pltpu.VMEM
        head, water = pl.pallas_call(
            functools.partial(kernel, nz, wide, kinds, sizes, 16),
            out_shape=(
                vmem(pressure.shape, F32),
                vmem(depth.shape[::-1], F32),
            ),
            in_specs=[hbm] * 12,
            out_specs=(pl.BlockSpec(memory_space=vmem),) * 2,
            scratch_shapes=[
                pltpu.SMEM((4, kinds), F32),
                vmem(soil, F32),
                vmem(soil, jnp.int32),
                vmem((PARAMS, *soil), F32),
                vmem(soil, F32),
                vmem(soil, F32),
                vmem((2, nz + 2, ROWS, wide), F32),
                vmem((2, nz + 2, ROWS, wide), F32),
                vmem(soil, F32),
                vmem((2, 2, 2, wide // TILE, nz, TILE), F32),
                vmem((2, 2, 2, wide // TILE, nz, TILE), F32),
                vmem((2, ROWS, wide), F32),
                vmem((2, ROWS, wide), F32),
                vmem((3, 2, ROWS, TILE), F32),
                vmem((3, 2, ROWS, TILE), F32),
                vmem((2, ROWS, TILE), F32),
                vmem((2, ROWS, TILE), F32),
                vmem((4, 32, TILE), F32),
                vmem((FIELDS, 48, 2 * TILE), F32),
                vmem((FIELDS, 48, TILE), F32),
                vmem((FIELDS, 48, TILE), F32),
                vmem((nk + 2, ROWS, TILE), F32),
                vmem((2 * TILE, TILE), F32),
                vmem((2 * TILE, TILE), F32),
                vmem((nk, ROWS, TILE), F32),
                vmem((nk, ROWS, TILE), F32),
                vmem((2, 32, TILE), jnp.int32),
                pltpu.SemaphoreType.DMA((100,)),
            ],
            compiler_params=pltpu.CompilerParams(
                collective_id=0, has_side_effects=True, vmem_limit_bytes=60 * 1024 * 1024
            ),
        )(
            pressure, soil_class, capacity_range, inverse_entry, shape_index, conductivity,
            depth.T, elevation.T, roughness.T, rain.T, land_mask.T, channel_mask.T,
        )
        head, water = pl.pallas_call(
            deliver,
            out_shape=(
                pltpu.HBM(head.shape, F32),
                pltpu.HBM(water.shape, F32),
            ),
            in_specs=[pl.BlockSpec(memory_space=vmem)] * 2,
            out_specs=(hbm, hbm),
            scratch_shapes=[pltpu.SemaphoreType.DMA((2,))],
            compiler_params=pltpu.CompilerParams(vmem_limit_bytes=2 * 1024 * 1024),
        )(head, water)
        return head, water.T

    tile = P(None, ("grp", "gy"), "gx")
    flat = P("grp", ("gx", "gy"))
    return jax.shard_map(
        local,
        mesh=mesh,
        in_specs=(tile, tile, P(), P(), P(), P()) + (flat,) * 6,
        out_specs=(tile, flat),
        check_vma=False,
    )
```

```python
import functools

import jax
import jax.numpy as jnp
from jax import lax
from jax.experimental import pallas as pl
from jax.experimental.pallas import tpu as pltpu
from jax.sharding import PartitionSpec as P

MESH = pl.DeviceIdType.MESH
F32 = jnp.float32

STORAGE = 0.01
GRAVITY_STEP = 0.5
SUCTION_FLOOR = 0.01
SLOPE_FLOOR = 0.1
SURFACE_STEP = 0.3
LEAKANCE = 0.5

TILE = 128
ROWS = 8
FIELDS = 5
PARAMS = 6


def lanes():
    return lax.broadcasted_iota(jnp.int32, (ROWS, TILE), 1)


def sublanes():
    return lax.broadcasted_iota(jnp.int32, (ROWS, TILE), 0)


def gather(table, index):
    return jnp.take_along_axis(table, index, axis=1, mode="promise_in_bounds")


def build_tables(tab, kinds):
    lane = lanes()
    rows = []
    for i in range(4):
        row = jnp.zeros((ROWS, TILE), F32)
        for kind in range(kinds):
            row = jnp.where(lane == kind, tab[i, kind], row)
        rows.append(row)
    span, entry, shape, conduct = rows
    shape = jnp.where(lane < kinds, shape, 2.0)
    pore = 1.0 - 1.0 / shape
    expo = 1.0 / (1.0 - pore)
    return (
        -entry,
        expo,
        pore,
        span * pore * expo * entry,
        span,
        2.0 * jnp.sqrt(conduct),
    )


def closures(p, params):
    entry, expo, pore, lead, _, scale = params
    log_scaled = jnp.log(jnp.maximum(entry * p, SUCTION_FLOOR))
    up = expo * log_scaled
    log_sum = jnp.log(1.0 + jnp.exp(up))
    drop = pore * log_sum
    wet = pore * up - drop
    held = jnp.exp(wet)
    capacity = STORAGE + lead * jnp.exp(wet - log_sum)
    fourth = jnp.exp(-0.25 * drop)
    half = fourth * fourth
    root = scale * fourth * (1.0 - held)
    return capacity, half * half, root


def kernel(
    nz, wide, kinds, sizes, cut_z,
    p_in, k_in, t0_in, t1_in, t2_in, t3_in,
    s0_in, s1_in, s2_in, s3_in, s4_in, s5_in,
    head_out, water_out,
    tab, p, kind, par, cap, sat, root, flow, num,
    row_s, row_r, top_s, top_r, col_s, col_r, tcol_s, tcol_r,
    surf_in, field, below, above,
    down_s, down_r, edge_r, back_s, back_r, water,
    sem,
):
    ng, nx, nk = sizes
    tiles = wide // TILE
    per = TILE // 32
    g, x, k = (lax.axis_index(a) for a in ("grp", "gx", "gy"))
    lane, sub = lanes(), sublanes()
    first, last = k == 0, k == nk - 1
    has_n, has_s = g > 0, g < ng - 1
    has_w, has_e = x > 0, x < nx - 1

    names = {}

    def s(name):
        return sem.at[names.setdefault(name, len(names))]

    def at(dg, dx, kk):
        return {"grp": g + dg, "gx": x + dx, "gy": kk}

    def tile(t):
        return slice(t * TILE, (t + 1) * TILE)

    def load(src, dst, name):
        copy = pltpu.make_async_copy(src, dst, s(name))
        copy.start()
        return copy

    barrier = pltpu.get_barrier_semaphore()

    def greet(device):
        pl.semaphore_signal(barrier, 1, device_id=device, device_id_type=MESH)

    def ring(body):
        for away in sorted(range(1, nk), key=lambda d: -min(d, nk - d)):
            body(jnp.where(k + away >= nk, k + away - nk, k + away))

    def every(body):
        def step(i, _):
            body(i)
            return 0

        lax.fori_loop(0, nk, step, 0)

    col = x * nk + k
    has_l, has_r = col > 0, col < nx * nk - 1
    left = {"gx": jnp.maximum(col - 1, 0) // nk, "gy": lax.rem(jnp.maximum(col - 1, 0), nk)}
    right = {"gx": (col + 1) // nk, "gy": lax.rem(col + 1, nk)}
    row = g * nk + k
    has_u, has_d = row > 0, row < ng * nk - 1
    up = {"grp": jnp.maximum(row - 1, 0) // nk, "gx": x, "gy": lax.rem(jnp.maximum(row - 1, 0), nk)}
    down = {"grp": (row + 1) // nk, "gx": x, "gy": lax.rem(row + 1, nk)}

    @pl.when(has_w)
    def _():
        @pl.when(first)
        def _():
            every(lambda kk: greet(at(0, -1, kk)))

        greet(at(0, -1, k))

    @pl.when(has_e)
    def _():
        @pl.when(last)
        def _():
            every(lambda kk: greet(at(0, 1, kk)))

        greet(at(0, 1, k))

    for dg, has in ((-1, has_n), (1, has_s)):
        far = nk - 1 if dg < 0 else 0

        @pl.when(has)
        def _():
            greet(at(dg, 0, far))
            greet(at(dg, 0, k))

            @pl.when(has_l)
            def _():
                greet({"grp": g + dg, **left})

            @pl.when(has_r)
            def _():
                greet({"grp": g + dg, **right})

            @pl.when(first & has_w)
            def _():
                greet(at(dg, -1, far))

            @pl.when(last & has_e)
            def _():
                greet(at(dg, 1, far))

    ring(lambda kk: greet(at(0, 0, kk)))

    table_loads = [
        load(ref, tab.at[i], f"tab{i}")
        for i, ref in enumerate((t0_in, t1_in, t2_in, t3_in))
    ]
    top_loads = [
        load(p_in.at[0:1], p.at[0:1], "p0"),
        load(k_in.at[0:1], kind.at[0:1], "k0"),
    ]
    surf_loads = [
        load(s0_in, surf_in.at[0], "s0"),
        load(s1_in, surf_in.at[1], "s1"),
        load(s2_in, surf_in.at[2], "s2"),
        load(s3_in, surf_in.at[3], "s3"),
    ]
    mask_loads = [
        load(s4_in, water.at[0], "s4"),
        load(s5_in, water.at[1], "s5"),
    ]
    rest_loads = [
        load(p_in.at[1:nz], p.at[1:nz], "p1"),
        load(k_in.at[1:nz], kind.at[1:nz], "k1"),
    ]

    def one(flag):
        return flag.astype(jnp.int32)

    rows_to = one(has_n) + one(has_s)
    cols_to = one(has_w) + one(has_e)
    corner = one(first & has_n) + one(last & has_s)
    expected = (
        (nk - 1)
        + corner * nk
        + rows_to * (1 + one(has_l) + one(has_r))
        + 2 * cols_to
        + corner * cols_to
    )

    zero = jnp.zeros((ROWS, TILE), F32)
    for j in range(nk):
        back_r[j] = zero

    def clear(ref, rows):
        for r in range(0, rows, ROWS):
            for c in range(0, ref.shape[-1], TILE):
                ref[r : r + ROWS, c : c + TILE] = zero

    for t in range(tiles):
        for ph in range(2):
            for z in (0, nz + 1):
                root[ph, z, :, tile(t)] = zero
                flow[ph, z, :, tile(t)] = zero

    for d, has, has_g, ref in ((0, has_u, has_n, above), (1, has_d, has_s, below)):

        @pl.when(jnp.logical_not(has))
        def _():
            for ph in range(2):
                for i in range(2):
                    for t in range(tiles):
                        clear(row_r.at[ph, d, i, t], nz)
            clear(top_r.at[d], ROWS)

        @pl.when(jnp.logical_not(has_g))
        def _():
            for f in range(FIELDS):
                clear(ref.at[f], 48)
            off = 248 if d == 0 else 128
            clear(down_r.at[off : off + ROWS], ROWS)

        @pl.when(has_g & jnp.logical_not(has_r))
        def _():
            for f in range(FIELDS):
                ref[f, 32:40, :] = zero

        @pl.when(has_g & jnp.logical_not(has_l))
        def _():
            for f in range(FIELDS):
                ref[f, 40:48, :] = zero

    for d, has in ((0, has_w), (1, has_e)):

        @pl.when(jnp.logical_not(has))
        def _():
            for c in range(3):
                col_r[c, d] = zero
            tcol_r[d] = zero

    for d, has in ((0, has_r), (1, has_l)):

        @pl.when(jnp.logical_not(has))
        def _():
            for f in range(FIELDS):
                field[f, 32 + 8 * d : 40 + 8 * d, 0:TILE] = zero

    gets_edge = (first & has_w) | (last & has_e)

    @pl.when(jnp.logical_not(gets_edge))
    def _():
        clear(edge_r.at[0:TILE], TILE)

    for off, has in ((128, has_s), (248, has_n)):

        @pl.when(jnp.logical_not(gets_edge & has))
        def _():
            clear(edge_r.at[off : off + ROWS], ROWS)

    for c in table_loads:
        c.wait()
    tables = build_tables(tab, kinds)

    def layer_params(z, t):
        index = kind[z, :, tile(t)]
        return [gather(table, index) for table in tables]

    def put_row(dst_first, dst_last, i, z, t, value):
        dst_first[i, t, pl.ds(z, 1), :] = value[0:1, :]
        dst_last[i, t, pl.ds(z, 1), :] = value[7:8, :]

    def shift_to(value, frm, to):
        return pltpu.roll(value, lax.rem(to - frm + TILE, TILE), 1)

    def put_cols(packs, z, q0, r0, q1, r1):
        west, east = packs
        west = jnp.where(lane == z, shift_to(q0, 0, z), west)
        west = jnp.where(lane == z + 64, shift_to(r0, 0, z + 64), west)
        east = jnp.where(lane == z, shift_to(q1, TILE - 1, z), east)
        east = jnp.where(lane == z + 64, shift_to(r1, TILE - 1, z + 64), east)
        return west, east

    def first_closures(z, packs):
        ends = []
        for t in range(tiles):
            params = layer_params(z, t)
            for i in range(PARAMS):
                par[i, z, :, tile(t)] = params[i]
            pz = p[z, :, tile(t)]
            c, se, q = closures(pz, params)
            r = q * pz
            cap[z, :, tile(t)] = c
            sat[z, :, tile(t)] = se
            root[0, z + 1, :, tile(t)] = q
            flow[0, z + 1, :, tile(t)] = r
            put_row(row_s.at[0, 0], row_s.at[0, 1], 0, z, t, q)
            put_row(row_s.at[0, 0], row_s.at[0, 1], 1, z, t, r)
            ends.append((q, r))
        return put_cols(packs, z, *ends[0], *ends[-1])

    for c in top_loads:
        c.wait()
    packs = first_closures(0, (zero, zero))

    tops = [p[0, :, tile(t)] for t in range(tiles)]
    halves = [jnp.square(root[0, 1, :, tile(t)]) * 0.125 for t in range(tiles)]

    def turn(v, by):
        by %= TILE
        return pltpu.roll(v, by, 1) if by else v

    def cut(parts, kk, base):
        t, o = divmod(kk * 32, TILE)
        out = turn(parts[t], base - o)
        before = parts[t] if o else parts[max(t - 1, 0)]
        out = jnp.where(
            (lane >= base + 38) & (lane < base + 40), turn(before, base + 40 - o), out
        )
        if o + 32 == TILE and t + 1 < tiles:
            after = turn(parts[t + 1], base + 32)
            out = jnp.where((lane >= base + 32) & (lane < base + 34), after, out)
        return out

    for kk in range(nk):
        down_s[kk] = jnp.where(lane < 64, cut(tops, kk, 0), cut(halves, kk, 64))
    down_s[nk] = jnp.where(lane < 64, turn(tops[-1], 40), turn(halves[-1], 104))
    down_s[nk + 1] = jnp.where(lane < 64, turn(tops[0], 32), turn(halves[0], 96))
    mine = pl.multiple_of(k * ROWS, ROWS)
    down_r[pl.ds(mine, ROWS), :] = down_s[k]

    pending = []

    def send(src, dst, name, device, when=None, keep=True):
        copy = pltpu.make_async_remote_copy(
            src_ref=src,
            dst_ref=dst,
            send_sem=s(name + "_s"),
            recv_sem=s(name + "_r"),
            device_id=device,
            device_id_type=MESH,
        )
        if when is None:
            copy.start()
        else:
            pl.when(when)(copy.start)
        if keep:
            pending.append((copy, when))
        return copy

    def drain(ref, name, when=None):
        wait = pltpu.make_async_copy(ref, ref, s(name)).wait
        if when is None:
            wait()
        else:
            pl.when(when)(wait)

    for c in surf_loads + mask_loads:
        c.wait()
    field[0, 0:32, 0:TILE] = surf_in[0]
    field[1, 0:32, 0:TILE] = surf_in[1]
    field[2, 0:32, 0:TILE] = jnp.sqrt((1.0 + water[1].astype(F32)) / surf_in[2])
    field[3, 0:32, 0:TILE] = surf_in[3]
    field[4, 0:32, 0:TILE] = water[0].astype(F32)

    for c in rest_loads:
        c.wait()
    packs = lax.fori_loop(1, nz, first_closures, packs, unroll=4)
    col_s[0, 0], col_s[0, 1] = packs

    pl.semaphore_wait(barrier, expected)
    for dx, kk, has_x, i in ((1, 0, has_e, nk), (-1, nk - 1, has_w, nk + 1)):
        send(
            down_s.at[i], edge_r.at[pl.ds(mine, ROWS)], f"edge{dx}", at(0, dx, kk), has_x
        )
    for dg, far, has, slot in ((1, last, has_s, 248), (-1, first, has_n, 128)):

        @pl.when(far & has)
        def _():
            every(
                lambda kk: send(
                    down_s.at[kk], down_r.at[slot : slot + ROWS], f"down{slot}", at(dg, 0, kk),
                    keep=False,
                )
            )

        for dx, kk, has_x, i in ((1, 0, has_e, nk), (-1, nk - 1, has_w, nk + 1)):
            send(
                down_s.at[i], edge_r.at[slot : slot + ROWS], f"edge{slot}{dx}",
                at(dg, dx, kk), far & has & has_x,
            )
    ring(
        lambda kk: send(
            down_s.at[kk], down_r.at[pl.ds(mine, ROWS)], "down", at(0, 0, kk), keep=False
        )
    )
    chunks = ((0, 0, nz), (1, 0, cut_z), (1, cut_z, nz))

    def send_soil(c):
        ph, a, b = chunks[c]
        send(row_s.at[ph, 1, :, :, a:b], row_r.at[ph, 0, :, :, a:b], f"row{c}d", down, has_d)
        send(row_s.at[ph, 0, :, :, a:b], row_r.at[ph, 1, :, :, a:b], f"row{c}u", up, has_u)
        send(col_s.at[c, 1], col_r.at[c, 0], f"col{c}e", at(0, 1, k), has_e)
        send(col_s.at[c, 0], col_r.at[c, 1], f"col{c}w", at(0, -1, k), has_w)

    def wait_soil(c):
        ph, a, b = chunks[c]
        drain(row_r.at[ph, 0, :, :, a:b], f"row{c}d_r", has_u)
        drain(row_r.at[ph, 1, :, :, a:b], f"row{c}u_r", has_d)
        drain(col_r.at[c, 0], f"col{c}e_r", has_w)
        drain(col_r.at[c, 1], f"col{c}w_r", has_e)

    send_soil(0)

    def own(a, b):
        return field.at[:, a:b, 0:TILE]

    send(own(24, 32), own(40, 48), "right", {"grp": g, **right}, has_r)
    send(own(0, 8), own(32, 40), "left", {"grp": g, **left}, has_l)
    for dg, has, ref, n in ((1, has_s, above, "s"), (-1, has_n, below, "n")):
        send(own(0, 32), ref.at[:, 0:32], "line" + n, at(dg, 0, k), has)
        send(own(24, 32), ref.at[:, 40:48], "right" + n, {"grp": g + dg, **right}, has & has_r)
        send(own(0, 8), ref.at[:, 32:40], "left" + n, {"grp": g + dg, **left}, has & has_l)

    def sums(ph, z, halo):
        rows, cols = halo
        both = []
        for i, ref in enumerate((root, flow)):
            mid = [ref[ph, z + 1, :, tile(t)] for t in range(tiles)]
            from_west = [cols[0][i]] + [pltpu.roll(v, 1, 1) for v in mid]
            from_east = [pltpu.roll(v, TILE - 1, 1) for v in mid] + [cols[1][i]]
            totals = []
            for t in range(tiles):
                high, low = ref[ph, z, :, tile(t)], ref[ph, z + 2, :, tile(t)]
                ends = rows(t)
                north = jnp.where(sub == 0, ends[0][i], pltpu.roll(mid[t], 1, 0))
                south = jnp.where(sub == ROWS - 1, ends[1][i], pltpu.roll(mid[t], ROWS - 1, 0))
                west = jnp.where(lane == 0, from_west[t], from_west[t + 1])
                east = jnp.where(lane == TILE - 1, from_east[t + 1], from_east[t])
                totals.append(((high + low) + (north + south)) + (west + east))
                if i == 0:
                    both.append(GRAVITY_STEP * (high - low))
            both.append((mid, totals))
        own_root, q = both[tiles]
        r = both[tiles + 1][1]
        return own_root, q, [r[t] + both[t] for t in range(tiles)]

    def plain_halo(c, z):
        ph = chunks[c][0]

        def rows(t):
            return [
                [row_r[ph, d, i, t, pl.ds(z, 1), :] for i in range(2)] for d in range(2)
            ]

        cols = [
            [shift_to(col_r[c, d], z + 64 * i, (TILE - 1) * d) for i in range(2)]
            for d in range(2)
        ]
        return rows, cols

    def sweep_parts(ph, z, halo, base, weight):
        own_root, q, r = sums(ph, z, halo)
        return [
            (base[t] + own_root[t] * r[t], weight[t] + own_root[t] * q[t]) for t in range(tiles)
        ]

    def first_parts(z, halo):
        weight = [cap[z, :, tile(t)] for t in range(tiles)]
        base = [weight[t] * p[z, :, tile(t)] for t in range(tiles)]
        return sweep_parts(0, z, halo, base, weight)

    def keep(z, t, head, params):
        c, se, q = closures(head, params)
        gap = params[4] * (se - sat[z, :, tile(t)])
        cap[z, :, tile(t)] = c
        num[z, :, tile(t)] = c * head - gap
        r = q * head
        root[1, z + 1, :, tile(t)] = q
        flow[1, z + 1, :, tile(t)] = r
        return q, r

    def second_closures(z, packs):
        halo = plain_halo(0, z)
        heads = [upper / lower for upper, lower in first_parts(z, halo)]
        ends = []
        for t in range(tiles):
            q, r = keep(z, t, heads[t], [par[i, z, :, tile(t)] for i in range(PARAMS)])
            put_row(row_s.at[1, 0], row_s.at[1, 1], 0, z, t, q)
            put_row(row_s.at[1, 0], row_s.at[1, 1], 1, z, t, r)
            ends.append((q, r))
        return put_cols(packs, z, *ends[0], *ends[-1])

    for t in range(tiles):
        for d in range(2):
            top_s[d, :, tile(t)] = zero
            for i in range(2):
                row_s[1, d, i, t, 0:ROWS, :] = zero
    wait_soil(0)

    halo = plain_halo(0, 0)
    west, east = zero, zero
    for t, (upper, lower) in enumerate(first_parts(0, halo)):
        num[0, :, tile(t)] = upper
        cap[0, :, tile(t)] = lower
        for i, v in enumerate([upper, lower] + [par[j, 0, :, tile(t)] for j in (0, 1, 2, 5)]):
            top_s[0, i : i + 1, tile(t)] = v[0:1, :]
            top_s[1, i : i + 1, tile(t)] = v[ROWS - 1 : ROWS, :]
            if t == 0:
                west = jnp.where(lane == i, turn(v, i), west)
            if t == tiles - 1:
                east = jnp.where(lane == i, turn(v, i + 1), east)
    tcol_s[0], tcol_s[1] = west, east
    send(top_s.at[1], top_r.at[0], "topd", down, has_d)
    send(top_s.at[0], top_r.at[1], "topu", up, has_u)
    send(tcol_s.at[1], tcol_r.at[0], "tope", at(0, 1, k), has_e)
    send(tcol_s.at[0], tcol_r.at[1], "topw", at(0, -1, k), has_w)

    packs = lax.fori_loop(1, cut_z, second_closures, (zero, zero), unroll=4)
    col_s[1, 0], col_s[1, 1] = packs

    drain(own(40, 48), "right_r", has_l)
    drain(own(32, 40), "left_r", has_r)
    for has, ref, n in ((has_n, above, "s"), (has_s, below, "n")):
        drain(ref.at[:, 0:32], "line" + n + "_r", has)
        drain(ref.at[:, 40:48], "right" + n + "_r", has & has_l)
        drain(ref.at[:, 32:40], "left" + n + "_r", has & has_r)
    side = lax.broadcasted_iota(jnp.int32, (48, TILE), 1) < 64
    full = []
    for f in range(FIELDS):
        full.append(
            jnp.concatenate(
                [field[f, :, 0:TILE], jnp.where(side, below[f], above[f])], axis=1
            )
        )
    w0, level, bed, rain, land = full

    def next_of(v, axis):
        return pltpu.roll(v, v.shape[axis] - 1, axis)

    def prev_of(v, axis):
        return pltpu.roll(v, 1, axis)

    faces = [bed * next_of(bed, axis) for axis in (0, 1)]

    def outflow(w):
        carried = jnp.exp((5.0 / 3.0) * jnp.log(jnp.maximum(w, 1e-30)))
        surface = level + w
        total = None
        for axis in (0, 1):
            slope = surface - next_of(surface, axis)
            upwind = jnp.where(slope >= 0, carried, next_of(carried, axis))
            flux = faces[axis] * upwind * slope * lax.rsqrt(
                jnp.maximum(jnp.abs(slope), SLOPE_FLOOR)
            )
            net = flux - prev_of(flux, axis)
            total = net if total is None else total + net
        return total

    out0 = outflow(w0)

    drain(down_s.at[0 : nk - 1], "down_r")
    drain(down_s.at[0], "down128_r", has_s)
    drain(down_s.at[0], "down248_r", has_n)
    for dx, gets in ((1, first & has_w), (-1, last & has_e)):
        drain(edge_r.at[0:TILE], f"edge{dx}_r", gets)
        drain(down_s.at[0], f"edge128{dx}_r", gets & has_s)
        drain(down_s.at[0], f"edge248{dx}_r", gets & has_n)

    tall = lax.broadcasted_iota(jnp.int32, (TILE, TILE), 0)
    wide_lane = lax.broadcasted_iota(jnp.int32, (TILE, TILE), 1) & 63
    low = jnp.where(first, 38, 32)
    use_edge = (wide_lane >= low) & (wide_lane < low + 2) & (first | last)

    def received(a):
        rows = jnp.where(use_edge, edge_r[a : a + TILE, :], down_r[a : a + TILE, :])
        if a:
            rows = jnp.where((tall < ROWS) | (tall >= TILE - ROWS), rows, 0.0)
        return rows.T

    main, rim = received(0), received(TILE)

    def pick(a):
        body = [main[a : a + 32], rim[a : a + 32]]
        halo = [main[a + 32 : a + 40], rim[a + 32 : a + 40]]
        body, halo = (jnp.concatenate(v, axis=1) for v in (body, halo))
        return jnp.concatenate([body, halo, halo], axis=0)

    top = pick(0)
    leak = land * pick(64)

    def advance(w, out):
        rate = leak * (w - top)
        return jnp.maximum(w + SURFACE_STEP * (rain - rate - out), 0.0), rate

    w1, rate0 = advance(w0, out0)
    w2, rate1 = advance(w1, outflow(w1))
    rate2 = leak * (w2 - top)
    exchange = SURFACE_STEP * (rate0 + rate1 + rate2)
    body = exchange[0:32]
    mesh_t = [body[:, 0:TILE]] * 3 + [exchange[32:48, 0:TILE]] * 2
    square = jnp.concatenate(mesh_t, axis=0).T
    outer = jnp.concatenate([body[:, TILE:]] * 4, axis=0).T
    blocks = [square[ROWS * j : ROWS * (j + 1)] for j in range(nk)]
    blocks = [outer[TILE - ROWS :]] + blocks + [outer[0:ROWS]]
    folded = [pltpu.roll(v, 4, 0) for v in blocks]
    fold = ((lane >= 32) & (lane < 64)) | (lane >= 112)
    rim = (lane >= 64) & (lane < 96)
    for j in range(nk):
        ends = jnp.where(sub < 2, blocks[j + 2], folded[j])
        back_s[j] = jnp.where(rim, ends, jnp.where(fold, folded[j + 1], blocks[j + 1]))
    back_r[k] = back_s[k]
    ring(
        lambda kk: send(back_s.at[kk, 0:4], back_r.at[k, 0:4], "back", at(0, 0, kk), keep=False)
    )
    send_soil(1)
    w3, _ = advance(w2, outflow(w2))
    water_out[...] = w3[0:32, 0:TILE]

    packs = lax.fori_loop(cut_z, nz, second_closures, (zero, zero), unroll=4)
    col_s[2, 0], col_s[2, 1] = packs
    send_soil(2)

    def last_sweep(z, halo):
        base = [num[z, :, tile(t)] for t in range(tiles)]
        weight = [cap[z, :, tile(t)] for t in range(tiles)]
        for t, (upper, lower) in enumerate(sweep_parts(1, z, halo, base, weight)):
            head_out[z, :, tile(t)] = upper / lower

    def last_step(c):
        def step(z, carry):
            last_sweep(z, plain_halo(c, z))
            return carry

        return step

    wait_soil(1)
    lax.fori_loop(2, cut_z - 1, last_step(1), 0, unroll=4)
    last_sweep(cut_z - 1, plain_halo(1, cut_z - 1))
    wait_soil(2)
    lax.fori_loop(cut_z, nz, last_step(2), 0, unroll=4)
    drain(top_r.at[0], "topd_r", has_u)
    drain(top_r.at[1], "topu_r", has_d)
    drain(tcol_r.at[0], "tope_r", has_w)
    drain(tcol_r.at[1], "topw_r", has_e)

    drain(down_s.at[0 : nk - 1], "down_s")
    drain(down_s.at[0 : nk - 1, 0:4], "back_s")
    drain(down_s.at[0:nk], "down248_s", last & has_s)
    drain(down_s.at[0:nk], "down128_s", first & has_n)
    for copy, when in pending:
        if when is None:
            copy.wait_send()
        else:
            pl.when(when)(copy.wait_send)

    drain(down_s.at[0 : nk - 1, 0:4], "back_r")

    def gathered(t, group):
        v = turn(back_r[per * t], -32 * group)
        for i in range(1, per):
            v = jnp.where(lane >= 32 * i, turn(back_r[per * t + i], 32 * (i - group)), v)
        return v

    def unfold(a, b):
        return jnp.where(sub < 4, a, pltpu.roll(b, 4, 0))

    def beside(parts, gain):
        upper, lower, entry, expo, pore, scale = parts
        head = (upper + gain) / jnp.maximum(lower, 1e-6)
        _, _, q = closures(head, (entry, expo, pore, 0.0, None, scale))
        return q, q * head

    extras, rows_beside = [], []
    for t in range(tiles):
        extras.append(unfold(gathered(t, 0), gathered(t, 1)))
        parts = [
            jnp.where(sub < 2, top_r[1, i : i + 1, tile(t)], top_r[0, i : i + 1, tile(t)])
            for i in range(6)
        ]
        rows_beside.append(beside(parts, gathered(t, 2)))
    parts = [
        jnp.where(lane < 64, turn(tcol_r[0], -i), turn(tcol_r[1], TILE - 1 - i)) for i in range(6)
    ]
    west, east = back_r[0], back_r[nk - 1]
    gain = unfold(
        jnp.where(lane < 64, turn(west, -111), turn(east, 31)),
        jnp.where(lane < 64, turn(west, -127), turn(east, 15)),
    )
    ends = beside(parts, gain)
    for t in range(tiles):
        head = (num[0, :, tile(t)] + extras[t]) / cap[0, :, tile(t)]
        keep(0, t, head, [par[i, 0, :, tile(t)] for i in range(PARAMS)])
        num[0, :, tile(t)] += extras[t]

    def top_rows(t):
        return [[v[3:4, :] for v in rows_beside[t]], [v[0:1, :] for v in rows_beside[t]]]

    last_sweep(0, (top_rows, [ends, ends]))
    last_sweep(1, plain_halo(1, 1))


def deliver(head, water, head_out, water_out, sem):
    copies = [
        pltpu.make_async_copy(head, head_out, sem.at[0]),
        pltpu.make_async_copy(water, water_out, sem.at[1]),
    ]
    for c in copies:
        c.start()
    for c in copies:
        c.wait()


def solution(mesh):
    sizes = tuple(mesh.shape[a] for a in ("grp", "gx", "gy"))
    nk = sizes[2]

    def local(
        pressure, soil_class, capacity_range, inverse_entry, shape_index, conductivity,
        depth, elevation, roughness, rain, land_mask, channel_mask,
    ):
        nz, _, wide = pressure.shape
        kinds = capacity_range.shape[0]
        hbm = pl.BlockSpec(memory_space=pl.ANY)
        soil = (nz, ROWS, wide)
        vmem = pltpu.VMEM
        head, water = pl.pallas_call(
            functools.partial(kernel, nz, wide, kinds, sizes, 8),
            out_shape=(
                vmem(pressure.shape, F32),
                vmem(depth.shape[::-1], F32),
            ),
            in_specs=[hbm] * 12,
            out_specs=(pl.BlockSpec(memory_space=vmem),) * 2,
            scratch_shapes=[
                pltpu.SMEM((4, kinds), F32),
                vmem(soil, F32),
                vmem(soil, jnp.int32),
                vmem((PARAMS, *soil), F32),
                vmem(soil, F32),
                vmem(soil, F32),
                vmem((2, nz + 2, ROWS, wide), F32),
                vmem((2, nz + 2, ROWS, wide), F32),
                vmem(soil, F32),
                vmem((2, 2, 2, wide // TILE, nz, TILE), F32),
                vmem((2, 2, 2, wide // TILE, nz, TILE), F32),
                vmem((2, ROWS, wide), F32),
                vmem((2, ROWS, wide), F32),
                vmem((3, 2, ROWS, TILE), F32),
                vmem((3, 2, ROWS, TILE), F32),
                vmem((2, ROWS, TILE), F32),
                vmem((2, ROWS, TILE), F32),
                vmem((4, 32, TILE), F32),
                vmem((FIELDS, 48, 2 * TILE), F32),
                vmem((FIELDS, 48, TILE), F32),
                vmem((FIELDS, 48, TILE), F32),
                vmem((nk + 2, ROWS, TILE), F32),
                vmem((2 * TILE, TILE), F32),
                vmem((2 * TILE, TILE), F32),
                vmem((nk, ROWS, TILE), F32),
                vmem((nk, ROWS, TILE), F32),
                vmem((2, 32, TILE), jnp.int32),
                pltpu.SemaphoreType.DMA((100,)),
            ],
            compiler_params=pltpu.CompilerParams(
                collective_id=0, has_side_effects=True, vmem_limit_bytes=60 * 1024 * 1024
            ),
        )(
            pressure, soil_class, capacity_range, inverse_entry, shape_index, conductivity,
            depth.T, elevation.T, roughness.T, rain.T, land_mask.T, channel_mask.T,
        )
        head, water = pl.pallas_call(
            deliver,
            out_shape=(
                pltpu.HBM(head.shape, F32),
                pltpu.HBM(water.shape, F32),
            ),
            in_specs=[pl.BlockSpec(memory_space=vmem)] * 2,
            out_specs=(hbm, hbm),
            scratch_shapes=[pltpu.SemaphoreType.DMA((2,))],
            compiler_params=pltpu.CompilerParams(vmem_limit_bytes=2 * 1024 * 1024),
        )(head, water)
        return head, water.T

    tile = P(None, ("grp", "gy"), "gx")
    flat = P("grp", ("gx", "gy"))
    return jax.shard_map(
        local,
        mesh=mesh,
        in_specs=(tile, tile, P(), P(), P(), P()) + (flat,) * 6,
        out_specs=(tile, flat),
        check_vma=False,
    )
```

```python
import functools

import jax
import jax.numpy as jnp
from jax import lax
from jax.experimental import pallas as pl
from jax.experimental.pallas import tpu as pltpu
from jax.sharding import PartitionSpec as P

MESH = pl.DeviceIdType.MESH
F32 = jnp.float32

STORAGE = 0.01
GRAVITY_STEP = 0.5
SUCTION_FLOOR = 0.01
SLOPE_FLOOR = 0.1
SURFACE_STEP = 0.3
LEAKANCE = 0.5

TILE = 128
ROWS = 8
FIELDS = 5
PARAMS = 6


def lanes():
    return lax.broadcasted_iota(jnp.int32, (ROWS, TILE), 1)


def sublanes():
    return lax.broadcasted_iota(jnp.int32, (ROWS, TILE), 0)


def gather(table, index):
    return jnp.take_along_axis(table, index, axis=1, mode="promise_in_bounds")


def build_tables(tab, kinds):
    lane = lanes()
    rows = []
    for i in range(4):
        row = jnp.zeros((ROWS, TILE), F32)
        for kind in range(kinds):
            row = jnp.where(lane == kind, tab[i, kind], row)
        rows.append(row)
    span, entry, shape, conduct = rows
    shape = jnp.where(lane < kinds, shape, 2.0)
    pore = 1.0 - 1.0 / shape
    expo = 1.0 / (1.0 - pore)
    return (
        -entry,
        expo,
        pore,
        span * pore * expo * entry,
        span,
        2.0 * jnp.sqrt(conduct),
    )


def closures(p, params):
    entry, expo, pore, lead, _, scale = params
    log_scaled = jnp.log(jnp.maximum(entry * p, SUCTION_FLOOR))
    up = expo * log_scaled
    log_sum = jnp.log(1.0 + jnp.exp(up))
    drop = pore * log_sum
    wet = pore * up - drop
    held = jnp.exp(wet)
    capacity = STORAGE + lead * jnp.exp(wet - log_sum)
    fourth = jnp.exp(-0.25 * drop)
    half = fourth * fourth
    root = scale * fourth * (1.0 - held)
    return capacity, half * half, root


def kernel(
    nz, wide, kinds, sizes, cut_z,
    p_in, k_in, t0_in, t1_in, t2_in, t3_in,
    s0_in, s1_in, s2_in, s3_in, s4_in, s5_in,
    head_out, water_out,
    tab, p, kind, par, cap, sat, root, flow, num,
    row_s, row_r, top_s, top_r, col_s, col_r, tcol_s, tcol_r,
    surf_in, field, below, above,
    down_s, down_r, edge_r, back_s, back_r, water,
    sem,
):
    ng, nx, nk = sizes
    tiles = wide // TILE
    per = TILE // 32
    g, x, k = (lax.axis_index(a) for a in ("grp", "gx", "gy"))
    lane, sub = lanes(), sublanes()
    first, last = k == 0, k == nk - 1
    has_n, has_s = g > 0, g < ng - 1
    has_w, has_e = x > 0, x < nx - 1

    names = {}

    def s(name):
        return sem.at[names.setdefault(name, len(names))]

    def at(dg, dx, kk):
        return {"grp": g + dg, "gx": x + dx, "gy": kk}

    def tile(t):
        return slice(t * TILE, (t + 1) * TILE)

    def load(src, dst, name):
        copy = pltpu.make_async_copy(src, dst, s(name))
        copy.start()
        return copy

    barrier = pltpu.get_barrier_semaphore()

    def greet(device):
        pl.semaphore_signal(barrier, 1, device_id=device, device_id_type=MESH)

    def ring(body):
        for away in sorted(range(1, nk), key=lambda d: -min(d, nk - d)):
            body(jnp.where(k + away >= nk, k + away - nk, k + away))

    def every(body):
        def step(i, _):
            body(i)
            return 0

        lax.fori_loop(0, nk, step, 0)

    col = x * nk + k
    has_l, has_r = col > 0, col < nx * nk - 1
    left = {"gx": jnp.maximum(col - 1, 0) // nk, "gy": lax.rem(jnp.maximum(col - 1, 0), nk)}
    right = {"gx": (col + 1) // nk, "gy": lax.rem(col + 1, nk)}
    row = g * nk + k
    has_u, has_d = row > 0, row < ng * nk - 1
    up = {"grp": jnp.maximum(row - 1, 0) // nk, "gx": x, "gy": lax.rem(jnp.maximum(row - 1, 0), nk)}
    down = {"grp": (row + 1) // nk, "gx": x, "gy": lax.rem(row + 1, nk)}

    @pl.when(has_w)
    def _():
        @pl.when(first)
        def _():
            every(lambda kk: greet(at(0, -1, kk)))

        greet(at(0, -1, k))

    @pl.when(has_e)
    def _():
        @pl.when(last)
        def _():
            every(lambda kk: greet(at(0, 1, kk)))

        greet(at(0, 1, k))

    for dg, has in ((-1, has_n), (1, has_s)):
        far = nk - 1 if dg < 0 else 0

        @pl.when(has)
        def _():
            greet(at(dg, 0, far))
            greet(at(dg, 0, k))

            @pl.when(has_l)
            def _():
                greet({"grp": g + dg, **left})

            @pl.when(has_r)
            def _():
                greet({"grp": g + dg, **right})

            @pl.when(first & has_w)
            def _():
                greet(at(dg, -1, far))

            @pl.when(last & has_e)
            def _():
                greet(at(dg, 1, far))

    ring(lambda kk: greet(at(0, 0, kk)))

    table_loads = [
        load(ref, tab.at[i], f"tab{i}")
        for i, ref in enumerate((t0_in, t1_in, t2_in, t3_in))
    ]
    top_loads = [
        load(p_in.at[0:1], p.at[0:1], "p0"),
        load(k_in.at[0:1], kind.at[0:1], "k0"),
    ]
    surf_loads = [
        load(s0_in, surf_in.at[0], "s0"),
        load(s1_in, surf_in.at[1], "s1"),
        load(s2_in, surf_in.at[2], "s2"),
        load(s3_in, surf_in.at[3], "s3"),
    ]
    mask_loads = [
        load(s4_in, water.at[0], "s4"),
        load(s5_in, water.at[1], "s5"),
    ]
    rest_loads = [
        load(p_in.at[1:nz], p.at[1:nz], "p1"),
        load(k_in.at[1:nz], kind.at[1:nz], "k1"),
    ]

    def one(flag):
        return flag.astype(jnp.int32)

    rows_to = one(has_n) + one(has_s)
    cols_to = one(has_w) + one(has_e)
    corner = one(first & has_n) + one(last & has_s)
    expected = (
        (nk - 1)
        + corner * nk
        + rows_to * (1 + one(has_l) + one(has_r))
        + 2 * cols_to
        + corner * cols_to
    )

    zero = jnp.zeros((ROWS, TILE), F32)
    for j in range(nk):
        back_r[j] = zero

    def clear(ref, rows):
        for r in range(0, rows, ROWS):
            for c in range(0, ref.shape[-1], TILE):
                ref[r : r + ROWS, c : c + TILE] = zero

    for t in range(tiles):
        for ph in range(2):
            for z in (0, nz + 1):
                root[ph, z, :, tile(t)] = zero
                flow[ph, z, :, tile(t)] = zero

    for d, has, has_g, ref in ((0, has_u, has_n, above), (1, has_d, has_s, below)):

        @pl.when(jnp.logical_not(has))
        def _():
            for ph in range(2):
                for i in range(2):
                    for t in range(tiles):
                        clear(row_r.at[ph, d, i, t], nz)
            clear(top_r.at[d], ROWS)

        @pl.when(jnp.logical_not(has_g))
        def _():
            for f in range(FIELDS):
                clear(ref.at[f], 48)
            off = 248 if d == 0 else 128
            clear(down_r.at[off : off + ROWS], ROWS)

        @pl.when(has_g & jnp.logical_not(has_r))
        def _():
            for f in range(FIELDS):
                ref[f, 32:40, :] = zero

        @pl.when(has_g & jnp.logical_not(has_l))
        def _():
            for f in range(FIELDS):
                ref[f, 40:48, :] = zero

    for d, has in ((0, has_w), (1, has_e)):

        @pl.when(jnp.logical_not(has))
        def _():
            for c in range(3):
                col_r[c, d] = zero
            tcol_r[d] = zero

    for d, has in ((0, has_r), (1, has_l)):

        @pl.when(jnp.logical_not(has))
        def _():
            for f in range(FIELDS):
                field[f, 32 + 8 * d : 40 + 8 * d, 0:TILE] = zero

    gets_edge = (first & has_w) | (last & has_e)

    @pl.when(jnp.logical_not(gets_edge))
    def _():
        clear(edge_r.at[0:TILE], TILE)

    for off, has in ((128, has_s), (248, has_n)):

        @pl.when(jnp.logical_not(gets_edge & has))
        def _():
            clear(edge_r.at[off : off + ROWS], ROWS)

    for c in table_loads:
        c.wait()
    tables = build_tables(tab, kinds)

    def layer_params(z, t):
        index = kind[z, :, tile(t)]
        return [gather(table, index) for table in tables]

    def put_row(dst_first, dst_last, i, z, t, value):
        dst_first[i, t, pl.ds(z, 1), :] = value[0:1, :]
        dst_last[i, t, pl.ds(z, 1), :] = value[7:8, :]

    def shift_to(value, frm, to):
        return pltpu.roll(value, lax.rem(to - frm + TILE, TILE), 1)

    def put_cols(packs, z, q0, r0, q1, r1):
        west, east = packs
        west = jnp.where(lane == z, shift_to(q0, 0, z), west)
        west = jnp.where(lane == z + 64, shift_to(r0, 0, z + 64), west)
        east = jnp.where(lane == z, shift_to(q1, TILE - 1, z), east)
        east = jnp.where(lane == z + 64, shift_to(r1, TILE - 1, z + 64), east)
        return west, east

    def first_closures(z, packs):
        ends = []
        for t in range(tiles):
            params = layer_params(z, t)
            for i in range(PARAMS):
                par[i, z, :, tile(t)] = params[i]
            pz = p[z, :, tile(t)]
            c, se, q = closures(pz, params)
            r = q * pz
            cap[z, :, tile(t)] = c
            sat[z, :, tile(t)] = se
            root[0, z + 1, :, tile(t)] = q
            flow[0, z + 1, :, tile(t)] = r
            put_row(row_s.at[0, 0], row_s.at[0, 1], 0, z, t, q)
            put_row(row_s.at[0, 0], row_s.at[0, 1], 1, z, t, r)
            ends.append((q, r))
        return put_cols(packs, z, *ends[0], *ends[-1])

    for c in top_loads:
        c.wait()
    packs = first_closures(0, (zero, zero))

    tops = [p[0, :, tile(t)] for t in range(tiles)]
    halves = [jnp.square(root[0, 1, :, tile(t)]) * 0.125 for t in range(tiles)]

    def turn(v, by):
        by %= TILE
        return pltpu.roll(v, by, 1) if by else v

    def cut(parts, kk, base):
        t, o = divmod(kk * 32, TILE)
        out = turn(parts[t], base - o)
        before = parts[t] if o else parts[max(t - 1, 0)]
        out = jnp.where(
            (lane >= base + 38) & (lane < base + 40), turn(before, base + 40 - o), out
        )
        if o + 32 == TILE and t + 1 < tiles:
            after = turn(parts[t + 1], base + 32)
            out = jnp.where((lane >= base + 32) & (lane < base + 34), after, out)
        return out

    for kk in range(nk):
        down_s[kk] = jnp.where(lane < 64, cut(tops, kk, 0), cut(halves, kk, 64))
    down_s[nk] = jnp.where(lane < 64, turn(tops[-1], 40), turn(halves[-1], 104))
    down_s[nk + 1] = jnp.where(lane < 64, turn(tops[0], 32), turn(halves[0], 96))
    mine = pl.multiple_of(k * ROWS, ROWS)
    down_r[pl.ds(mine, ROWS), :] = down_s[k]

    pending = []

    def send(src, dst, name, device, when=None, keep=True):
        copy = pltpu.make_async_remote_copy(
            src_ref=src,
            dst_ref=dst,
            send_sem=s(name + "_s"),
            recv_sem=s(name + "_r"),
            device_id=device,
            device_id_type=MESH,
        )
        if when is None:
            copy.start()
        else:
            pl.when(when)(copy.start)
        if keep:
            pending.append((copy, when))
        return copy

    def drain(ref, name, when=None):
        wait = pltpu.make_async_copy(ref, ref, s(name)).wait
        if when is None:
            wait()
        else:
            pl.when(when)(wait)

    for c in surf_loads + mask_loads:
        c.wait()
    field[0, 0:32, 0:TILE] = surf_in[0]
    field[1, 0:32, 0:TILE] = surf_in[1]
    field[2, 0:32, 0:TILE] = jnp.sqrt((1.0 + water[1].astype(F32)) / surf_in[2])
    field[3, 0:32, 0:TILE] = surf_in[3]
    field[4, 0:32, 0:TILE] = water[0].astype(F32)

    for c in rest_loads:
        c.wait()
    packs = lax.fori_loop(1, nz, first_closures, packs, unroll=4)
    col_s[0, 0], col_s[0, 1] = packs

    pl.semaphore_wait(barrier, expected)
    chunks = ((0, 0, nz), (1, 0, cut_z), (1, cut_z, nz))

    def send_soil(c):
        ph, a, b = chunks[c]
        send(row_s.at[ph, 1, :, :, a:b], row_r.at[ph, 0, :, :, a:b], f"row{c}d", down, has_d)
        send(row_s.at[ph, 0, :, :, a:b], row_r.at[ph, 1, :, :, a:b], f"row{c}u", up, has_u)
        send(col_s.at[c, 1], col_r.at[c, 0], f"col{c}e", at(0, 1, k), has_e)
        send(col_s.at[c, 0], col_r.at[c, 1], f"col{c}w", at(0, -1, k), has_w)

    def wait_soil(c):
        ph, a, b = chunks[c]
        drain(row_r.at[ph, 0, :, :, a:b], f"row{c}d_r", has_u)
        drain(row_r.at[ph, 1, :, :, a:b], f"row{c}u_r", has_d)
        drain(col_r.at[c, 0], f"col{c}e_r", has_w)
        drain(col_r.at[c, 1], f"col{c}w_r", has_e)

    send_soil(0)

    for dx, kk, has_x, i in ((1, 0, has_e, nk), (-1, nk - 1, has_w, nk + 1)):
        send(
            down_s.at[i], edge_r.at[pl.ds(mine, ROWS)], f"edge{dx}", at(0, dx, kk), has_x
        )
    for dg, far, has, slot in ((1, last, has_s, 248), (-1, first, has_n, 128)):

        @pl.when(far & has)
        def _():
            every(
                lambda kk: send(
                    down_s.at[kk], down_r.at[slot : slot + ROWS], f"down{slot}", at(dg, 0, kk),
                    keep=False,
                )
            )

        for dx, kk, has_x, i in ((1, 0, has_e, nk), (-1, nk - 1, has_w, nk + 1)):
            send(
                down_s.at[i], edge_r.at[slot : slot + ROWS], f"edge{slot}{dx}",
                at(dg, dx, kk), far & has & has_x,
            )
    ring(
        lambda kk: send(
            down_s.at[kk], down_r.at[pl.ds(mine, ROWS)], "down", at(0, 0, kk), keep=False
        )
    )

    def own(a, b):
        return field.at[:, a:b, 0:TILE]

    send(own(24, 32), own(40, 48), "right", {"grp": g, **right}, has_r)
    send(own(0, 8), own(32, 40), "left", {"grp": g, **left}, has_l)
    for dg, has, ref, n in ((1, has_s, above, "s"), (-1, has_n, below, "n")):
        send(own(0, 32), ref.at[:, 0:32], "line" + n, at(dg, 0, k), has)
        send(own(24, 32), ref.at[:, 40:48], "right" + n, {"grp": g + dg, **right}, has & has_r)
        send(own(0, 8), ref.at[:, 32:40], "left" + n, {"grp": g + dg, **left}, has & has_l)

    def sums(ph, z, halo):
        rows, cols = halo
        both = []
        for i, ref in enumerate((root, flow)):
            mid = [ref[ph, z + 1, :, tile(t)] for t in range(tiles)]
            from_west = [cols[0][i]] + [pltpu.roll(v, 1, 1) for v in mid]
            from_east = [pltpu.roll(v, TILE - 1, 1) for v in mid] + [cols[1][i]]
            totals = []
            for t in range(tiles):
                high, low = ref[ph, z, :, tile(t)], ref[ph, z + 2, :, tile(t)]
                ends = rows(t)
                north = jnp.where(sub == 0, ends[0][i], pltpu.roll(mid[t], 1, 0))
                south = jnp.where(sub == ROWS - 1, ends[1][i], pltpu.roll(mid[t], ROWS - 1, 0))
                west = jnp.where(lane == 0, from_west[t], from_west[t + 1])
                east = jnp.where(lane == TILE - 1, from_east[t + 1], from_east[t])
                totals.append(((high + low) + (north + south)) + (west + east))
                if i == 0:
                    both.append(GRAVITY_STEP * (high - low))
            both.append((mid, totals))
        own_root, q = both[tiles]
        r = both[tiles + 1][1]
        return own_root, q, [r[t] + both[t] for t in range(tiles)]

    def plain_halo(c, z):
        ph = chunks[c][0]

        def rows(t):
            return [
                [row_r[ph, d, i, t, pl.ds(z, 1), :] for i in range(2)] for d in range(2)
            ]

        cols = [
            [shift_to(col_r[c, d], z + 64 * i, (TILE - 1) * d) for i in range(2)]
            for d in range(2)
        ]
        return rows, cols

    def sweep_parts(ph, z, halo, base, weight):
        own_root, q, r = sums(ph, z, halo)
        return [
            (base[t] + own_root[t] * r[t], weight[t] + own_root[t] * q[t]) for t in range(tiles)
        ]

    def first_parts(z, halo):
        weight = [cap[z, :, tile(t)] for t in range(tiles)]
        base = [weight[t] * p[z, :, tile(t)] for t in range(tiles)]
        return sweep_parts(0, z, halo, base, weight)

    def keep(z, t, head, params):
        c, se, q = closures(head, params)
        gap = params[4] * (se - sat[z, :, tile(t)])
        cap[z, :, tile(t)] = c
        num[z, :, tile(t)] = c * head - gap
        r = q * head
        root[1, z + 1, :, tile(t)] = q
        flow[1, z + 1, :, tile(t)] = r
        return q, r

    def second_closures(z, packs):
        halo = plain_halo(0, z)
        heads = [upper / lower for upper, lower in first_parts(z, halo)]
        ends = []
        for t in range(tiles):
            q, r = keep(z, t, heads[t], [par[i, z, :, tile(t)] for i in range(PARAMS)])
            put_row(row_s.at[1, 0], row_s.at[1, 1], 0, z, t, q)
            put_row(row_s.at[1, 0], row_s.at[1, 1], 1, z, t, r)
            ends.append((q, r))
        return put_cols(packs, z, *ends[0], *ends[-1])

    for t in range(tiles):
        for d in range(2):
            top_s[d, :, tile(t)] = zero
            for i in range(2):
                row_s[1, d, i, t, 0:ROWS, :] = zero
    wait_soil(0)

    halo = plain_halo(0, 0)
    west, east = zero, zero
    for t, (upper, lower) in enumerate(first_parts(0, halo)):
        num[0, :, tile(t)] = upper
        cap[0, :, tile(t)] = lower
        for i, v in enumerate([upper, lower] + [par[j, 0, :, tile(t)] for j in (0, 1, 2, 5)]):
            top_s[0, i : i + 1, tile(t)] = v[0:1, :]
            top_s[1, i : i + 1, tile(t)] = v[ROWS - 1 : ROWS, :]
            if t == 0:
                west = jnp.where(lane == i, turn(v, i), west)
            if t == tiles - 1:
                east = jnp.where(lane == i, turn(v, i + 1), east)
    tcol_s[0], tcol_s[1] = west, east
    send(top_s.at[1], top_r.at[0], "topd", down, has_d)
    send(top_s.at[0], top_r.at[1], "topu", up, has_u)
    send(tcol_s.at[1], tcol_r.at[0], "tope", at(0, 1, k), has_e)
    send(tcol_s.at[0], tcol_r.at[1], "topw", at(0, -1, k), has_w)

    packs = lax.fori_loop(1, cut_z, second_closures, (zero, zero), unroll=4)
    col_s[1, 0], col_s[1, 1] = packs

    drain(own(40, 48), "right_r", has_l)
    drain(own(32, 40), "left_r", has_r)
    for has, ref, n in ((has_n, above, "s"), (has_s, below, "n")):
        drain(ref.at[:, 0:32], "line" + n + "_r", has)
        drain(ref.at[:, 40:48], "right" + n + "_r", has & has_l)
        drain(ref.at[:, 32:40], "left" + n + "_r", has & has_r)
    side = lax.broadcasted_iota(jnp.int32, (48, TILE), 1) < 64
    full = []
    for f in range(FIELDS):
        full.append(
            jnp.concatenate(
                [field[f, :, 0:TILE], jnp.where(side, below[f], above[f])], axis=1
            )
        )
    w0, level, bed, rain, land = full

    def next_of(v, axis):
        return pltpu.roll(v, v.shape[axis] - 1, axis)

    def prev_of(v, axis):
        return pltpu.roll(v, 1, axis)

    faces = [bed * next_of(bed, axis) for axis in (0, 1)]

    def outflow(w):
        carried = jnp.exp((5.0 / 3.0) * jnp.log(jnp.maximum(w, 1e-30)))
        surface = level + w
        total = None
        for axis in (0, 1):
            slope = surface - next_of(surface, axis)
            upwind = jnp.where(slope >= 0, carried, next_of(carried, axis))
            flux = faces[axis] * upwind * slope * lax.rsqrt(
                jnp.maximum(jnp.abs(slope), SLOPE_FLOOR)
            )
            net = flux - prev_of(flux, axis)
            total = net if total is None else total + net
        return total

    out0 = outflow(w0)

    drain(down_s.at[0 : nk - 1], "down_r")
    drain(down_s.at[0], "down128_r", has_s)
    drain(down_s.at[0], "down248_r", has_n)
    for dx, gets in ((1, first & has_w), (-1, last & has_e)):
        drain(edge_r.at[0:TILE], f"edge{dx}_r", gets)
        drain(down_s.at[0], f"edge128{dx}_r", gets & has_s)
        drain(down_s.at[0], f"edge248{dx}_r", gets & has_n)

    tall = lax.broadcasted_iota(jnp.int32, (TILE, TILE), 0)
    wide_lane = lax.broadcasted_iota(jnp.int32, (TILE, TILE), 1) & 63
    low = jnp.where(first, 38, 32)
    use_edge = (wide_lane >= low) & (wide_lane < low + 2) & (first | last)

    def received(a):
        rows = jnp.where(use_edge, edge_r[a : a + TILE, :], down_r[a : a + TILE, :])
        if a:
            rows = jnp.where((tall < ROWS) | (tall >= TILE - ROWS), rows, 0.0)
        return rows.T

    main, rim = received(0), received(TILE)

    def pick(a):
        body = [main[a : a + 32], rim[a : a + 32]]
        halo = [main[a + 32 : a + 40], rim[a + 32 : a + 40]]
        body, halo = (jnp.concatenate(v, axis=1) for v in (body, halo))
        return jnp.concatenate([body, halo, halo], axis=0)

    top = pick(0)
    leak = land * pick(64)

    def advance(w, out):
        rate = leak * (w - top)
        return jnp.maximum(w + SURFACE_STEP * (rain - rate - out), 0.0), rate

    w1, rate0 = advance(w0, out0)
    w2, rate1 = advance(w1, outflow(w1))
    rate2 = leak * (w2 - top)
    exchange = SURFACE_STEP * (rate0 + rate1 + rate2)
    body = exchange[0:32]
    mesh_t = [body[:, 0:TILE]] * 3 + [exchange[32:48, 0:TILE]] * 2
    square = jnp.concatenate(mesh_t, axis=0).T
    outer = jnp.concatenate([body[:, TILE:]] * 4, axis=0).T
    blocks = [square[ROWS * j : ROWS * (j + 1)] for j in range(nk)]
    blocks = [outer[TILE - ROWS :]] + blocks + [outer[0:ROWS]]
    folded = [pltpu.roll(v, 4, 0) for v in blocks]
    fold = ((lane >= 32) & (lane < 64)) | (lane >= 112)
    rim = (lane >= 64) & (lane < 96)
    for j in range(nk):
        ends = jnp.where(sub < 2, blocks[j + 2], folded[j])
        back_s[j] = jnp.where(rim, ends, jnp.where(fold, folded[j + 1], blocks[j + 1]))
    back_r[k] = back_s[k]
    ring(
        lambda kk: send(back_s.at[kk, 0:4], back_r.at[k, 0:4], "back", at(0, 0, kk), keep=False)
    )
    send_soil(1)
    w3, _ = advance(w2, outflow(w2))
    water_out[...] = w3[0:32, 0:TILE]

    packs = lax.fori_loop(cut_z, nz, second_closures, (zero, zero), unroll=4)
    col_s[2, 0], col_s[2, 1] = packs
    send_soil(2)

    def last_sweep(z, halo):
        base = [num[z, :, tile(t)] for t in range(tiles)]
        weight = [cap[z, :, tile(t)] for t in range(tiles)]
        for t, (upper, lower) in enumerate(sweep_parts(1, z, halo, base, weight)):
            head_out[z, :, tile(t)] = upper / lower

    def last_step(c):
        def step(z, carry):
            last_sweep(z, plain_halo(c, z))
            return carry

        return step

    wait_soil(1)
    lax.fori_loop(2, cut_z - 1, last_step(1), 0, unroll=4)
    last_sweep(cut_z - 1, plain_halo(1, cut_z - 1))
    wait_soil(2)
    lax.fori_loop(cut_z, nz, last_step(2), 0, unroll=4)
    drain(top_r.at[0], "topd_r", has_u)
    drain(top_r.at[1], "topu_r", has_d)
    drain(tcol_r.at[0], "tope_r", has_w)
    drain(tcol_r.at[1], "topw_r", has_e)

    drain(down_s.at[0 : nk - 1], "down_s")
    drain(down_s.at[0 : nk - 1, 0:4], "back_s")
    drain(down_s.at[0:nk], "down248_s", last & has_s)
    drain(down_s.at[0:nk], "down128_s", first & has_n)
    for copy, when in pending:
        if when is None:
            copy.wait_send()
        else:
            pl.when(when)(copy.wait_send)

    drain(down_s.at[0 : nk - 1, 0:4], "back_r")

    def gathered(t, group):
        v = turn(back_r[per * t], -32 * group)
        for i in range(1, per):
            v = jnp.where(lane >= 32 * i, turn(back_r[per * t + i], 32 * (i - group)), v)
        return v

    def unfold(a, b):
        return jnp.where(sub < 4, a, pltpu.roll(b, 4, 0))

    def beside(parts, gain):
        upper, lower, entry, expo, pore, scale = parts
        head = (upper + gain) / jnp.maximum(lower, 1e-6)
        _, _, q = closures(head, (entry, expo, pore, 0.0, None, scale))
        return q, q * head

    extras, rows_beside = [], []
    for t in range(tiles):
        extras.append(unfold(gathered(t, 0), gathered(t, 1)))
        parts = [
            jnp.where(sub < 2, top_r[1, i : i + 1, tile(t)], top_r[0, i : i + 1, tile(t)])
            for i in range(6)
        ]
        rows_beside.append(beside(parts, gathered(t, 2)))
    parts = [
        jnp.where(lane < 64, turn(tcol_r[0], -i), turn(tcol_r[1], TILE - 1 - i)) for i in range(6)
    ]
    west, east = back_r[0], back_r[nk - 1]
    gain = unfold(
        jnp.where(lane < 64, turn(west, -111), turn(east, 31)),
        jnp.where(lane < 64, turn(west, -127), turn(east, 15)),
    )
    ends = beside(parts, gain)
    for t in range(tiles):
        head = (num[0, :, tile(t)] + extras[t]) / cap[0, :, tile(t)]
        keep(0, t, head, [par[i, 0, :, tile(t)] for i in range(PARAMS)])
        num[0, :, tile(t)] += extras[t]

    def top_rows(t):
        return [[v[3:4, :] for v in rows_beside[t]], [v[0:1, :] for v in rows_beside[t]]]

    last_sweep(0, (top_rows, [ends, ends]))
    last_sweep(1, plain_halo(1, 1))


def deliver(head, water, head_out, water_out, sem):
    copies = [
        pltpu.make_async_copy(head, head_out, sem.at[0]),
        pltpu.make_async_copy(water, water_out, sem.at[1]),
    ]
    for c in copies:
        c.start()
    for c in copies:
        c.wait()


def solution(mesh):
    sizes = tuple(mesh.shape[a] for a in ("grp", "gx", "gy"))
    nk = sizes[2]

    def local(
        pressure, soil_class, capacity_range, inverse_entry, shape_index, conductivity,
        depth, elevation, roughness, rain, land_mask, channel_mask,
    ):
        nz, _, wide = pressure.shape
        kinds = capacity_range.shape[0]
        hbm = pl.BlockSpec(memory_space=pl.ANY)
        soil = (nz, ROWS, wide)
        vmem = pltpu.VMEM
        head, water = pl.pallas_call(
            functools.partial(kernel, nz, wide, kinds, sizes, 16),
            out_shape=(
                vmem(pressure.shape, F32),
                vmem(depth.shape[::-1], F32),
            ),
            in_specs=[hbm] * 12,
            out_specs=(pl.BlockSpec(memory_space=vmem),) * 2,
            scratch_shapes=[
                pltpu.SMEM((4, kinds), F32),
                vmem(soil, F32),
                vmem(soil, jnp.int32),
                vmem((PARAMS, *soil), F32),
                vmem(soil, F32),
                vmem(soil, F32),
                vmem((2, nz + 2, ROWS, wide), F32),
                vmem((2, nz + 2, ROWS, wide), F32),
                vmem(soil, F32),
                vmem((2, 2, 2, wide // TILE, nz, TILE), F32),
                vmem((2, 2, 2, wide // TILE, nz, TILE), F32),
                vmem((2, ROWS, wide), F32),
                vmem((2, ROWS, wide), F32),
                vmem((3, 2, ROWS, TILE), F32),
                vmem((3, 2, ROWS, TILE), F32),
                vmem((2, ROWS, TILE), F32),
                vmem((2, ROWS, TILE), F32),
                vmem((4, 32, TILE), F32),
                vmem((FIELDS, 48, 2 * TILE), F32),
                vmem((FIELDS, 48, TILE), F32),
                vmem((FIELDS, 48, TILE), F32),
                vmem((nk + 2, ROWS, TILE), F32),
                vmem((2 * TILE, TILE), F32),
                vmem((2 * TILE, TILE), F32),
                vmem((nk, ROWS, TILE), F32),
                vmem((nk, ROWS, TILE), F32),
                vmem((2, 32, TILE), jnp.int32),
                pltpu.SemaphoreType.DMA((100,)),
            ],
            compiler_params=pltpu.CompilerParams(
                collective_id=0, has_side_effects=True, vmem_limit_bytes=60 * 1024 * 1024
            ),
        )(
            pressure, soil_class, capacity_range, inverse_entry, shape_index, conductivity,
            depth.T, elevation.T, roughness.T, rain.T, land_mask.T, channel_mask.T,
        )
        head, water = pl.pallas_call(
            deliver,
            out_shape=(
                pltpu.HBM(head.shape, F32),
                pltpu.HBM(water.shape, F32),
            ),
            in_specs=[pl.BlockSpec(memory_space=vmem)] * 2,
            out_specs=(hbm, hbm),
            scratch_shapes=[pltpu.SemaphoreType.DMA((2,))],
            compiler_params=pltpu.CompilerParams(vmem_limit_bytes=2 * 1024 * 1024),
        )(head, water)
        return head, water.T

    tile = P(None, ("grp", "gy"), "gx")
    flat = P("grp", ("gx", "gy"))
    return jax.shard_map(
        local,
        mesh=mesh,
        in_specs=(tile, tile, P(), P(), P(), P()) + (flat,) * 6,
        out_specs=(tile, flat),
        check_vma=False,
    )
```

```python
import functools

import jax
import jax.numpy as jnp
from jax import lax
from jax.experimental import pallas as pl
from jax.experimental.pallas import tpu as pltpu
from jax.sharding import PartitionSpec as P

MESH = pl.DeviceIdType.MESH
F32 = jnp.float32

STORAGE = 0.01
GRAVITY_STEP = 0.5
SUCTION_FLOOR = 0.01
SLOPE_FLOOR = 0.1
SURFACE_STEP = 0.3
LEAKANCE = 0.5

TILE = 128
ROWS = 8
FIELDS = 5
PARAMS = 6


def lanes():
    return lax.broadcasted_iota(jnp.int32, (ROWS, TILE), 1)


def sublanes():
    return lax.broadcasted_iota(jnp.int32, (ROWS, TILE), 0)


def gather(table, index):
    return jnp.take_along_axis(table, index, axis=1, mode="promise_in_bounds")


def build_tables(tab, kinds):
    lane = lanes()
    rows = []
    for i in range(4):
        row = jnp.zeros((ROWS, TILE), F32)
        for kind in range(kinds):
            row = jnp.where(lane == kind, tab[i, kind], row)
        rows.append(row)
    span, entry, shape, conduct = rows
    shape = jnp.where(lane < kinds, shape, 2.0)
    pore = 1.0 - 1.0 / shape
    expo = 1.0 / (1.0 - pore)
    return (
        -entry,
        expo,
        pore,
        span * pore * expo * entry,
        span,
        2.0 * jnp.sqrt(conduct),
    )


def closures(p, params):
    entry, expo, pore, lead, _, scale = params
    log_scaled = jnp.log(jnp.maximum(entry * p, SUCTION_FLOOR))
    up = expo * log_scaled
    log_sum = jnp.log(1.0 + jnp.exp(up))
    drop = pore * log_sum
    wet = pore * up - drop
    held = jnp.exp(wet)
    capacity = STORAGE + lead * jnp.exp(wet - log_sum)
    fourth = jnp.exp(-0.25 * drop)
    half = fourth * fourth
    root = scale * fourth * (1.0 - held)
    return capacity, half * half, root


def kernel(
    nz, wide, kinds, sizes, cut_z,
    p_in, k_in, t0_in, t1_in, t2_in, t3_in,
    s0_in, s1_in, s2_in, s3_in, s4_in, s5_in,
    head_out, water_out,
    tab, p, kind, par, cap, sat, root, flow, num,
    row_s, row_r, top_s, top_r, col_s, col_r, tcol_s, tcol_r,
    surf_in, field, below, above,
    down_s, down_r, edge_r, back_s, back_r, water,
    sem,
):
    ng, nx, nk = sizes
    tiles = wide // TILE
    per = TILE // 32
    g, x, k = (lax.axis_index(a) for a in ("grp", "gx", "gy"))
    lane, sub = lanes(), sublanes()
    first, last = k == 0, k == nk - 1
    has_n, has_s = g > 0, g < ng - 1
    has_w, has_e = x > 0, x < nx - 1

    names = {}

    def s(name):
        return sem.at[names.setdefault(name, len(names))]

    def at(dg, dx, kk):
        return {"grp": g + dg, "gx": x + dx, "gy": kk}

    def tile(t):
        return slice(t * TILE, (t + 1) * TILE)

    def load(src, dst, name):
        copy = pltpu.make_async_copy(src, dst, s(name))
        copy.start()
        return copy

    barrier = pltpu.get_barrier_semaphore()

    def greet(device):
        pl.semaphore_signal(barrier, 1, device_id=device, device_id_type=MESH)

    def ring(body):
        for away in sorted(range(1, nk), key=lambda d: -min(d, nk - d)):
            body(jnp.where(k + away >= nk, k + away - nk, k + away))

    def every(body):
        def step(i, _):
            body(i)
            return 0

        lax.fori_loop(0, nk, step, 0)

    col = x * nk + k
    has_l, has_r = col > 0, col < nx * nk - 1
    left = {"gx": jnp.maximum(col - 1, 0) // nk, "gy": lax.rem(jnp.maximum(col - 1, 0), nk)}
    right = {"gx": (col + 1) // nk, "gy": lax.rem(col + 1, nk)}
    row = g * nk + k
    has_u, has_d = row > 0, row < ng * nk - 1
    up = {"grp": jnp.maximum(row - 1, 0) // nk, "gx": x, "gy": lax.rem(jnp.maximum(row - 1, 0), nk)}
    down = {"grp": (row + 1) // nk, "gx": x, "gy": lax.rem(row + 1, nk)}

    @pl.when(has_w)
    def _():
        @pl.when(first)
        def _():
            every(lambda kk: greet(at(0, -1, kk)))

        greet(at(0, -1, k))

    @pl.when(has_e)
    def _():
        @pl.when(last)
        def _():
            every(lambda kk: greet(at(0, 1, kk)))

        greet(at(0, 1, k))

    for dg, has in ((-1, has_n), (1, has_s)):
        far = nk - 1 if dg < 0 else 0

        @pl.when(has)
        def _():
            greet(at(dg, 0, far))
            greet(at(dg, 0, k))

            @pl.when(has_l)
            def _():
                greet({"grp": g + dg, **left})

            @pl.when(has_r)
            def _():
                greet({"grp": g + dg, **right})

            @pl.when(first & has_w)
            def _():
                greet(at(dg, -1, far))

            @pl.when(last & has_e)
            def _():
                greet(at(dg, 1, far))

    ring(lambda kk: greet(at(0, 0, kk)))

    table_loads = [
        load(ref, tab.at[i], f"tab{i}")
        for i, ref in enumerate((t0_in, t1_in, t2_in, t3_in))
    ]
    top_loads = [
        load(p_in.at[0:1], p.at[0:1], "p0"),
        load(k_in.at[0:1], kind.at[0:1], "k0"),
    ]
    surf_loads = [
        load(s0_in, surf_in.at[0], "s0"),
        load(s1_in, surf_in.at[1], "s1"),
        load(s2_in, surf_in.at[2], "s2"),
        load(s3_in, surf_in.at[3], "s3"),
    ]
    mask_loads = [
        load(s4_in, water.at[0], "s4"),
        load(s5_in, water.at[1], "s5"),
    ]
    rest_loads = [
        load(p_in.at[1:nz], p.at[1:nz], "p1"),
        load(k_in.at[1:nz], kind.at[1:nz], "k1"),
    ]

    def one(flag):
        return flag.astype(jnp.int32)

    rows_to = one(has_n) + one(has_s)
    cols_to = one(has_w) + one(has_e)
    corner = one(first & has_n) + one(last & has_s)
    expected = (
        (nk - 1)
        + corner * nk
        + rows_to * (1 + one(has_l) + one(has_r))
        + 2 * cols_to
        + corner * cols_to
    )

    zero = jnp.zeros((ROWS, TILE), F32)
    for j in range(nk):
        back_r[j] = zero

    def clear(ref, rows):
        for r in range(0, rows, ROWS):
            for c in range(0, ref.shape[-1], TILE):
                ref[r : r + ROWS, c : c + TILE] = zero

    for t in range(tiles):
        for ph in range(2):
            for z in (0, nz + 1):
                root[ph, z, :, tile(t)] = zero
                flow[ph, z, :, tile(t)] = zero

    for d, has, has_g, ref in ((0, has_u, has_n, above), (1, has_d, has_s, below)):

        @pl.when(jnp.logical_not(has))
        def _():
            for ph in range(2):
                for i in range(2):
                    for t in range(tiles):
                        clear(row_r.at[ph, d, i, t], nz)
            clear(top_r.at[d], ROWS)

        @pl.when(jnp.logical_not(has_g))
        def _():
            for f in range(FIELDS):
                clear(ref.at[f], 48)
            off = 248 if d == 0 else 128
            clear(down_r.at[off : off + ROWS], ROWS)

        @pl.when(has_g & jnp.logical_not(has_r))
        def _():
            for f in range(FIELDS):
                ref[f, 32:40, :] = zero

        @pl.when(has_g & jnp.logical_not(has_l))
        def _():
            for f in range(FIELDS):
                ref[f, 40:48, :] = zero

    for d, has in ((0, has_w), (1, has_e)):

        @pl.when(jnp.logical_not(has))
        def _():
            for c in range(3):
                col_r[c, d] = zero
            tcol_r[d] = zero

    for d, has in ((0, has_r), (1, has_l)):

        @pl.when(jnp.logical_not(has))
        def _():
            for f in range(FIELDS):
                field[f, 32 + 8 * d : 40 + 8 * d, 0:TILE] = zero

    gets_edge = (first & has_w) | (last & has_e)

    @pl.when(jnp.logical_not(gets_edge))
    def _():
        clear(edge_r.at[0:TILE], TILE)

    for off, has in ((128, has_s), (248, has_n)):

        @pl.when(jnp.logical_not(gets_edge & has))
        def _():
            clear(edge_r.at[off : off + ROWS], ROWS)

    for c in table_loads:
        c.wait()
    tables = build_tables(tab, kinds)

    def layer_params(z, t):
        index = kind[z, :, tile(t)]
        return [gather(table, index) for table in tables]

    def put_row(dst_first, dst_last, i, z, t, value):
        dst_first[i, t, pl.ds(z, 1), :] = value[0:1, :]
        dst_last[i, t, pl.ds(z, 1), :] = value[7:8, :]

    def shift_to(value, frm, to):
        return pltpu.roll(value, lax.rem(to - frm + TILE, TILE), 1)

    def put_cols(packs, z, q0, r0, q1, r1):
        west, east = packs
        west = jnp.where(lane == z, shift_to(q0, 0, z), west)
        west = jnp.where(lane == z + 64, shift_to(r0, 0, z + 64), west)
        east = jnp.where(lane == z, shift_to(q1, TILE - 1, z), east)
        east = jnp.where(lane == z + 64, shift_to(r1, TILE - 1, z + 64), east)
        return west, east

    def first_closures(z, packs):
        ends = []
        for t in range(tiles):
            params = layer_params(z, t)
            for i in range(PARAMS):
                par[i, z, :, tile(t)] = params[i]
            pz = p[z, :, tile(t)]
            c, se, q = closures(pz, params)
            r = q * pz
            cap[z, :, tile(t)] = c
            sat[z, :, tile(t)] = se
            root[0, z + 1, :, tile(t)] = q
            flow[0, z + 1, :, tile(t)] = r
            put_row(row_s.at[0, 0], row_s.at[0, 1], 0, z, t, q)
            put_row(row_s.at[0, 0], row_s.at[0, 1], 1, z, t, r)
            ends.append((q, r))
        return put_cols(packs, z, *ends[0], *ends[-1])

    for c in top_loads:
        c.wait()
    packs = first_closures(0, (zero, zero))

    tops = [p[0, :, tile(t)] for t in range(tiles)]
    halves = [jnp.square(root[0, 1, :, tile(t)]) * 0.125 for t in range(tiles)]

    def turn(v, by):
        by %= TILE
        return pltpu.roll(v, by, 1) if by else v

    def cut(parts, kk, base):
        t, o = divmod(kk * 32, TILE)
        out = turn(parts[t], base - o)
        before = parts[t] if o else parts[max(t - 1, 0)]
        out = jnp.where(
            (lane >= base + 38) & (lane < base + 40), turn(before, base + 40 - o), out
        )
        if o + 32 == TILE and t + 1 < tiles:
            after = turn(parts[t + 1], base + 32)
            out = jnp.where((lane >= base + 32) & (lane < base + 34), after, out)
        return out

    for kk in range(nk):
        down_s[kk] = jnp.where(lane < 64, cut(tops, kk, 0), cut(halves, kk, 64))
    down_s[nk] = jnp.where(lane < 64, turn(tops[-1], 40), turn(halves[-1], 104))
    down_s[nk + 1] = jnp.where(lane < 64, turn(tops[0], 32), turn(halves[0], 96))
    mine = pl.multiple_of(k * ROWS, ROWS)
    down_r[pl.ds(mine, ROWS), :] = down_s[k]

    pending = []

    def send(src, dst, name, device, when=None, keep=True):
        copy = pltpu.make_async_remote_copy(
            src_ref=src,
            dst_ref=dst,
            send_sem=s(name + "_s"),
            recv_sem=s(name + "_r"),
            device_id=device,
            device_id_type=MESH,
        )
        if when is None:
            copy.start()
        else:
            pl.when(when)(copy.start)
        if keep:
            pending.append((copy, when))
        return copy

    def drain(ref, name, when=None):
        wait = pltpu.make_async_copy(ref, ref, s(name)).wait
        if when is None:
            wait()
        else:
            pl.when(when)(wait)

    for c in surf_loads + mask_loads:
        c.wait()
    field[0, 0:32, 0:TILE] = surf_in[0]
    field[1, 0:32, 0:TILE] = surf_in[1]
    field[2, 0:32, 0:TILE] = jnp.sqrt((1.0 + water[1].astype(F32)) / surf_in[2])
    field[3, 0:32, 0:TILE] = surf_in[3]
    field[4, 0:32, 0:TILE] = water[0].astype(F32)

    for c in rest_loads:
        c.wait()
    packs = lax.fori_loop(1, nz, first_closures, packs, unroll=4)
    col_s[0, 0], col_s[0, 1] = packs

    pl.semaphore_wait(barrier, expected)
    for dx, kk, has_x, i in ((1, 0, has_e, nk), (-1, nk - 1, has_w, nk + 1)):
        send(
            down_s.at[i], edge_r.at[pl.ds(mine, ROWS)], f"edge{dx}", at(0, dx, kk), has_x
        )
    for dg, far, has, slot in ((1, last, has_s, 248), (-1, first, has_n, 128)):

        @pl.when(far & has)
        def _():
            every(
                lambda kk: send(
                    down_s.at[kk], down_r.at[slot : slot + ROWS], f"down{slot}", at(dg, 0, kk),
                    keep=False,
                )
            )

        for dx, kk, has_x, i in ((1, 0, has_e, nk), (-1, nk - 1, has_w, nk + 1)):
            send(
                down_s.at[i], edge_r.at[slot : slot + ROWS], f"edge{slot}{dx}",
                at(dg, dx, kk), far & has & has_x,
            )
    ring(
        lambda kk: send(
            down_s.at[kk], down_r.at[pl.ds(mine, ROWS)], "down", at(0, 0, kk), keep=False
        )
    )
    chunks = ((0, 0, nz), (1, 0, cut_z), (1, cut_z, nz))

    def send_soil(c):
        ph, a, b = chunks[c]
        send(row_s.at[ph, 1, :, :, a:b], row_r.at[ph, 0, :, :, a:b], f"row{c}d", down, has_d)
        send(row_s.at[ph, 0, :, :, a:b], row_r.at[ph, 1, :, :, a:b], f"row{c}u", up, has_u)
        send(col_s.at[c, 1], col_r.at[c, 0], f"col{c}e", at(0, 1, k), has_e)
        send(col_s.at[c, 0], col_r.at[c, 1], f"col{c}w", at(0, -1, k), has_w)

    def wait_soil(c):
        ph, a, b = chunks[c]
        drain(row_r.at[ph, 0, :, :, a:b], f"row{c}d_r", has_u)
        drain(row_r.at[ph, 1, :, :, a:b], f"row{c}u_r", has_d)
        drain(col_r.at[c, 0], f"col{c}e_r", has_w)
        drain(col_r.at[c, 1], f"col{c}w_r", has_e)

    send_soil(0)

    def own(a, b):
        return field.at[:, a:b, 0:TILE]

    send(own(24, 32), own(40, 48), "right", {"grp": g, **right}, has_r)
    send(own(0, 8), own(32, 40), "left", {"grp": g, **left}, has_l)
    for dg, has, ref, n in ((1, has_s, above, "s"), (-1, has_n, below, "n")):
        send(own(0, 32), ref.at[:, 0:32], "line" + n, at(dg, 0, k), has)
        send(own(24, 32), ref.at[:, 40:48], "right" + n, {"grp": g + dg, **right}, has & has_r)
        send(own(0, 8), ref.at[:, 32:40], "left" + n, {"grp": g + dg, **left}, has & has_l)

    def sums(ph, z, halo):
        rows, cols = halo
        both = []
        for i, ref in enumerate((root, flow)):
            mid = [ref[ph, z + 1, :, tile(t)] for t in range(tiles)]
            from_west = [cols[0][i]] + [pltpu.roll(v, 1, 1) for v in mid]
            from_east = [pltpu.roll(v, TILE - 1, 1) for v in mid] + [cols[1][i]]
            totals = []
            for t in range(tiles):
                high, low = ref[ph, z, :, tile(t)], ref[ph, z + 2, :, tile(t)]
                ends = rows(t)
                north = jnp.where(sub == 0, ends[0][i], pltpu.roll(mid[t], 1, 0))
                south = jnp.where(sub == ROWS - 1, ends[1][i], pltpu.roll(mid[t], ROWS - 1, 0))
                west = jnp.where(lane == 0, from_west[t], from_west[t + 1])
                east = jnp.where(lane == TILE - 1, from_east[t + 1], from_east[t])
                totals.append(((high + low) + (north + south)) + (west + east))
                if i == 0:
                    both.append(GRAVITY_STEP * (high - low))
            both.append((mid, totals))
        own_root, q = both[tiles]
        r = both[tiles + 1][1]
        return own_root, q, [r[t] + both[t] for t in range(tiles)]

    def plain_halo(c, z):
        ph = chunks[c][0]

        def rows(t):
            return [
                [row_r[ph, d, i, t, pl.ds(z, 1), :] for i in range(2)] for d in range(2)
            ]

        cols = [
            [shift_to(col_r[c, d], z + 64 * i, (TILE - 1) * d) for i in range(2)]
            for d in range(2)
        ]
        return rows, cols

    def sweep_parts(ph, z, halo, base, weight):
        own_root, q, r = sums(ph, z, halo)
        return [
            (base[t] + own_root[t] * r[t], weight[t] + own_root[t] * q[t]) for t in range(tiles)
        ]

    def first_parts(z, halo):
        weight = [cap[z, :, tile(t)] for t in range(tiles)]
        base = [weight[t] * p[z, :, tile(t)] for t in range(tiles)]
        return sweep_parts(0, z, halo, base, weight)

    def keep(z, t, head, params):
        c, se, q = closures(head, params)
        gap = params[4] * (se - sat[z, :, tile(t)])
        cap[z, :, tile(t)] = c
        num[z, :, tile(t)] = c * head - gap
        r = q * head
        root[1, z + 1, :, tile(t)] = q
        flow[1, z + 1, :, tile(t)] = r
        return q, r

    def second_closures(z, packs):
        halo = plain_halo(0, z)
        heads = [upper / lower for upper, lower in first_parts(z, halo)]
        ends = []
        for t in range(tiles):
            q, r = keep(z, t, heads[t], [par[i, z, :, tile(t)] for i in range(PARAMS)])
            put_row(row_s.at[1, 0], row_s.at[1, 1], 0, z, t, q)
            put_row(row_s.at[1, 0], row_s.at[1, 1], 1, z, t, r)
            ends.append((q, r))
        return put_cols(packs, z, *ends[0], *ends[-1])

    for t in range(tiles):
        for d in range(2):
            top_s[d, :, tile(t)] = zero
            for i in range(2):
                row_s[1, d, i, t, 0:ROWS, :] = zero
    wait_soil(0)

    halo = plain_halo(0, 0)
    west, east = zero, zero
    for t, (upper, lower) in enumerate(first_parts(0, halo)):
        num[0, :, tile(t)] = upper
        cap[0, :, tile(t)] = lower
        for i, v in enumerate([upper, lower] + [par[j, 0, :, tile(t)] for j in (0, 1, 2, 5)]):
            top_s[0, i : i + 1, tile(t)] = v[0:1, :]
            top_s[1, i : i + 1, tile(t)] = v[ROWS - 1 : ROWS, :]
            if t == 0:
                west = jnp.where(lane == i, turn(v, i), west)
            if t == tiles - 1:
                east = jnp.where(lane == i, turn(v, i + 1), east)
    tcol_s[0], tcol_s[1] = west, east
    send(top_s.at[1], top_r.at[0], "topd", down, has_d)
    send(top_s.at[0], top_r.at[1], "topu", up, has_u)
    send(tcol_s.at[1], tcol_r.at[0], "tope", at(0, 1, k), has_e)
    send(tcol_s.at[0], tcol_r.at[1], "topw", at(0, -1, k), has_w)

    packs = lax.fori_loop(1, cut_z, second_closures, (zero, zero), unroll=4)
    col_s[1, 0], col_s[1, 1] = packs

    drain(own(40, 48), "right_r", has_l)
    drain(own(32, 40), "left_r", has_r)
    for has, ref, n in ((has_n, above, "s"), (has_s, below, "n")):
        drain(ref.at[:, 0:32], "line" + n + "_r", has)
        drain(ref.at[:, 40:48], "right" + n + "_r", has & has_l)
        drain(ref.at[:, 32:40], "left" + n + "_r", has & has_r)
    side = lax.broadcasted_iota(jnp.int32, (48, TILE), 1) < 64
    full = []
    for f in range(FIELDS):
        full.append(
            jnp.concatenate(
                [field[f, :, 0:TILE], jnp.where(side, below[f], above[f])], axis=1
            )
        )
    w0, level, bed, rain, land = full

    def next_of(v, axis):
        return pltpu.roll(v, v.shape[axis] - 1, axis)

    def prev_of(v, axis):
        return pltpu.roll(v, 1, axis)

    faces = [bed * next_of(bed, axis) for axis in (0, 1)]

    def outflow(w):
        carried = jnp.exp((5.0 / 3.0) * jnp.log(jnp.maximum(w, 1e-30)))
        surface = level + w
        total = None
        for axis in (0, 1):
            slope = surface - next_of(surface, axis)
            upwind = jnp.where(slope >= 0, carried, next_of(carried, axis))
            flux = faces[axis] * upwind * slope * lax.rsqrt(
                jnp.maximum(jnp.abs(slope), SLOPE_FLOOR)
            )
            net = flux - prev_of(flux, axis)
            total = net if total is None else total + net
        return total

    out0 = outflow(w0)

    drain(down_s.at[0 : nk - 1], "down_r")
    drain(down_s.at[0], "down128_r", has_s)
    drain(down_s.at[0], "down248_r", has_n)
    for dx, gets in ((1, first & has_w), (-1, last & has_e)):
        drain(edge_r.at[0:TILE], f"edge{dx}_r", gets)
        drain(down_s.at[0], f"edge128{dx}_r", gets & has_s)
        drain(down_s.at[0], f"edge248{dx}_r", gets & has_n)

    tall = lax.broadcasted_iota(jnp.int32, (TILE, TILE), 0)
    wide_lane = lax.broadcasted_iota(jnp.int32, (TILE, TILE), 1) & 63
    low = jnp.where(first, 38, 32)
    use_edge = (wide_lane >= low) & (wide_lane < low + 2) & (first | last)

    def received(a):
        rows = jnp.where(use_edge, edge_r[a : a + TILE, :], down_r[a : a + TILE, :])
        if a:
            rows = jnp.where((tall < ROWS) | (tall >= TILE - ROWS), rows, 0.0)
        return rows.T

    main, rim = received(0), received(TILE)

    def pick(a):
        body = [main[a : a + 32], rim[a : a + 32]]
        halo = [main[a + 32 : a + 40], rim[a + 32 : a + 40]]
        body, halo = (jnp.concatenate(v, axis=1) for v in (body, halo))
        return jnp.concatenate([body, halo, halo], axis=0)

    top = pick(0)
    leak = land * pick(64)

    def advance(w, out):
        rate = leak * (w - top)
        return jnp.maximum(w + SURFACE_STEP * (rain - rate - out), 0.0), rate

    w1, rate0 = advance(w0, out0)
    w2, rate1 = advance(w1, outflow(w1))
    rate2 = leak * (w2 - top)
    exchange = SURFACE_STEP * (rate0 + rate1 + rate2)
    body = exchange[0:32]
    mesh_t = [body[:, 0:TILE]] * 3 + [exchange[32:48, 0:TILE]] * 2
    square = jnp.concatenate(mesh_t, axis=0).T
    outer = jnp.concatenate([body[:, TILE:]] * 4, axis=0).T
    blocks = [square[ROWS * j : ROWS * (j + 1)] for j in range(nk)]
    blocks = [outer[TILE - ROWS :]] + blocks + [outer[0:ROWS]]
    folded = [pltpu.roll(v, 4, 0) for v in blocks]
    fold = ((lane >= 32) & (lane < 64)) | (lane >= 112)
    rim = (lane >= 64) & (lane < 96)
    for j in range(nk):
        ends = jnp.where(sub < 2, blocks[j + 2], folded[j])
        back_s[j] = jnp.where(rim, ends, jnp.where(fold, folded[j + 1], blocks[j + 1]))
    back_r[k] = back_s[k]
    ring(
        lambda kk: send(back_s.at[kk, 0:4], back_r.at[k, 0:4], "back", at(0, 0, kk), keep=False)
    )
    send_soil(1)
    packs = lax.fori_loop(cut_z, nz, second_closures, (zero, zero), unroll=4)
    col_s[2, 0], col_s[2, 1] = packs
    send_soil(2)
    w3, _ = advance(w2, outflow(w2))
    water_out[...] = w3[0:32, 0:TILE]

    def last_sweep(z, halo):
        base = [num[z, :, tile(t)] for t in range(tiles)]
        weight = [cap[z, :, tile(t)] for t in range(tiles)]
        for t, (upper, lower) in enumerate(sweep_parts(1, z, halo, base, weight)):
            head_out[z, :, tile(t)] = upper / lower

    def last_step(c):
        def step(z, carry):
            last_sweep(z, plain_halo(c, z))
            return carry

        return step

    wait_soil(1)
    lax.fori_loop(2, cut_z - 1, last_step(1), 0, unroll=4)
    last_sweep(cut_z - 1, plain_halo(1, cut_z - 1))
    wait_soil(2)
    lax.fori_loop(cut_z, nz, last_step(2), 0, unroll=4)
    drain(top_r.at[0], "topd_r", has_u)
    drain(top_r.at[1], "topu_r", has_d)
    drain(tcol_r.at[0], "tope_r", has_w)
    drain(tcol_r.at[1], "topw_r", has_e)

    drain(down_s.at[0 : nk - 1], "down_s")
    drain(down_s.at[0 : nk - 1, 0:4], "back_s")
    drain(down_s.at[0:nk], "down248_s", last & has_s)
    drain(down_s.at[0:nk], "down128_s", first & has_n)
    for copy, when in pending:
        if when is None:
            copy.wait_send()
        else:
            pl.when(when)(copy.wait_send)

    drain(down_s.at[0 : nk - 1, 0:4], "back_r")

    def gathered(t, group):
        v = turn(back_r[per * t], -32 * group)
        for i in range(1, per):
            v = jnp.where(lane >= 32 * i, turn(back_r[per * t + i], 32 * (i - group)), v)
        return v

    def unfold(a, b):
        return jnp.where(sub < 4, a, pltpu.roll(b, 4, 0))

    def beside(parts, gain):
        upper, lower, entry, expo, pore, scale = parts
        head = (upper + gain) / jnp.maximum(lower, 1e-6)
        _, _, q = closures(head, (entry, expo, pore, 0.0, None, scale))
        return q, q * head

    extras, rows_beside = [], []
    for t in range(tiles):
        extras.append(unfold(gathered(t, 0), gathered(t, 1)))
        parts = [
            jnp.where(sub < 2, top_r[1, i : i + 1, tile(t)], top_r[0, i : i + 1, tile(t)])
            for i in range(6)
        ]
        rows_beside.append(beside(parts, gathered(t, 2)))
    parts = [
        jnp.where(lane < 64, turn(tcol_r[0], -i), turn(tcol_r[1], TILE - 1 - i)) for i in range(6)
    ]
    west, east = back_r[0], back_r[nk - 1]
    gain = unfold(
        jnp.where(lane < 64, turn(west, -111), turn(east, 31)),
        jnp.where(lane < 64, turn(west, -127), turn(east, 15)),
    )
    ends = beside(parts, gain)
    for t in range(tiles):
        head = (num[0, :, tile(t)] + extras[t]) / cap[0, :, tile(t)]
        keep(0, t, head, [par[i, 0, :, tile(t)] for i in range(PARAMS)])
        num[0, :, tile(t)] += extras[t]

    def top_rows(t):
        return [[v[3:4, :] for v in rows_beside[t]], [v[0:1, :] for v in rows_beside[t]]]

    last_sweep(0, (top_rows, [ends, ends]))
    last_sweep(1, plain_halo(1, 1))


def deliver(head, water, head_out, water_out, sem):
    copies = [
        pltpu.make_async_copy(head, head_out, sem.at[0]),
        pltpu.make_async_copy(water, water_out, sem.at[1]),
    ]
    for c in copies:
        c.start()
    for c in copies:
        c.wait()


def solution(mesh):
    sizes = tuple(mesh.shape[a] for a in ("grp", "gx", "gy"))
    nk = sizes[2]

    def local(
        pressure, soil_class, capacity_range, inverse_entry, shape_index, conductivity,
        depth, elevation, roughness, rain, land_mask, channel_mask,
    ):
        nz, _, wide = pressure.shape
        kinds = capacity_range.shape[0]
        hbm = pl.BlockSpec(memory_space=pl.ANY)
        soil = (nz, ROWS, wide)
        vmem = pltpu.VMEM
        head, water = pl.pallas_call(
            functools.partial(kernel, nz, wide, kinds, sizes, 16),
            out_shape=(
                vmem(pressure.shape, F32),
                vmem(depth.shape[::-1], F32),
            ),
            in_specs=[hbm] * 12,
            out_specs=(pl.BlockSpec(memory_space=vmem),) * 2,
            scratch_shapes=[
                pltpu.SMEM((4, kinds), F32),
                vmem(soil, F32),
                vmem(soil, jnp.int32),
                vmem((PARAMS, *soil), F32),
                vmem(soil, F32),
                vmem(soil, F32),
                vmem((2, nz + 2, ROWS, wide), F32),
                vmem((2, nz + 2, ROWS, wide), F32),
                vmem(soil, F32),
                vmem((2, 2, 2, wide // TILE, nz, TILE), F32),
                vmem((2, 2, 2, wide // TILE, nz, TILE), F32),
                vmem((2, ROWS, wide), F32),
                vmem((2, ROWS, wide), F32),
                vmem((3, 2, ROWS, TILE), F32),
                vmem((3, 2, ROWS, TILE), F32),
                vmem((2, ROWS, TILE), F32),
                vmem((2, ROWS, TILE), F32),
                vmem((4, 32, TILE), F32),
                vmem((FIELDS, 48, 2 * TILE), F32),
                vmem((FIELDS, 48, TILE), F32),
                vmem((FIELDS, 48, TILE), F32),
                vmem((nk + 2, ROWS, TILE), F32),
                vmem((2 * TILE, TILE), F32),
                vmem((2 * TILE, TILE), F32),
                vmem((nk, ROWS, TILE), F32),
                vmem((nk, ROWS, TILE), F32),
                vmem((2, 32, TILE), jnp.int32),
                pltpu.SemaphoreType.DMA((100,)),
            ],
            compiler_params=pltpu.CompilerParams(
                collective_id=0, has_side_effects=True, vmem_limit_bytes=60 * 1024 * 1024
            ),
        )(
            pressure, soil_class, capacity_range, inverse_entry, shape_index, conductivity,
            depth.T, elevation.T, roughness.T, rain.T, land_mask.T, channel_mask.T,
        )
        head, water = pl.pallas_call(
            deliver,
            out_shape=(
                pltpu.HBM(head.shape, F32),
                pltpu.HBM(water.shape, F32),
            ),
            in_specs=[pl.BlockSpec(memory_space=vmem)] * 2,
            out_specs=(hbm, hbm),
            scratch_shapes=[pltpu.SemaphoreType.DMA((2,))],
            compiler_params=pltpu.CompilerParams(vmem_limit_bytes=2 * 1024 * 1024),
        )(head, water)
        return head, water.T

    tile = P(None, ("grp", "gy"), "gx")
    flat = P("grp", ("gx", "gy"))
    return jax.shard_map(
        local,
        mesh=mesh,
        in_specs=(tile, tile, P(), P(), P(), P()) + (flat,) * 6,
        out_specs=(tile, flat),
        check_vma=False,
    )
```
